32 devices in a mesh: section: 2 (over x), dp: 16 (over z, y, core).
Axes of the slice: x: 2, y: 2, z: 4, core: 2. Of those that a mesh axis runs over, the one named last changes fastest.
Arguments:
- content_in: bfloat16 [2, 4096, 768], P(None, 'dp'), may hold values from -6 to 6
- query_in: bfloat16 [2, 4096, 768], P(None, 'dp'), may hold values from -6 to 6
- content_cot: bfloat16 [2, 4096, 768], P(None, 'dp'), may hold values from -6 to 6
- query_cot: bfloat16 [2, 4096, 768], P(None, 'dp'), may hold values from -6 to 6
- lengths: int32 [2, 16, 16], P(None, 'dp'), may hold values from 0 to 256, as said below
- order: int32 [2, 4096], P(None, 'dp'), may hold values from 0 to 4095, each once within a row
- predicted: int32 [2, 4096], P(None, 'dp'), may hold values 0 or 1
- proj_weight: bfloat16 [2, 3, 768, 768], P('section'), may hold values from -0.21875 to 0.21875
- out_weight: bfloat16 [2, 768, 768], P('section'), may hold values from -0.875 to 0.875
- up_weight: bfloat16 [2, 768, 3072], P('section'), may hold values from -0.21875 to 0.21875
- down_weight: bfloat16 [2, 3072, 768], P('section'), may hold values from -0.109375 to 0.109375
- up_bias: float32 [2, 3072], P('section'), may hold values from -3 to 3
- biases: float32 [2, 6, 768], P('section'), may hold values from -3 to 3
- gains: float32 [2, 2, 768], P('section'), may hold values from 0.5 to 1.5
- rel_table: float32 [2, 384], P('section'), may hold values from -5 to 5
Outputs:
- content_out: bfloat16 [2, 2, 4096, 768], P('section', None, 'dp')
- query_out: bfloat16 [2, 2, 4096, 768], P('section', None, 'dp')
- content_grad: bfloat16 [2, 2, 4096, 768], P('section', None, 'dp')
- query_grad: bfloat16 [2, 2, 4096, 768], P('section', None, 'dp')
- proj_grad: float32 [2, 3, 768, 768], P('section', None, 'dp')
- out_grad: float32 [2, 768, 768], P('section', 'dp')
- up_grad: float32 [2, 768, 3072], P('section', 'dp')
- down_grad: float32 [2, 3072, 768], P('section', 'dp')
- up_bias_grad: float32 [2, 3072], P('section', 'dp')
- biases_grad: float32 [2, 6, 768], P('section', None, 'dp')
- gains_grad: float32 [2, 2, 768], P('section', None, 'dp')
- table_grad: float32 [2, 384], P('section', 'dp')
The draws below stay inside these ranges and needn't reach their ends.
Inputs may be any that keep to these rules, and one draw needn't show every extreme that they name: Each row of 16 lengths (one micro-batch, one index of dp) lists sequences of one token or more first and zeros after them; a row sums to 224 or more and to 256 at most; in every draw some row is one sequence of 256 tokens. `order`: within a micro-batch every token has a rank of its own.
All inputs are finite; a program needn't handle non-finite values. No bound on the sum of `predicted` on one device may be relied on, other than what follows from the above.
Results may differ from the reference program's by a relative error of at most 0.03.
Values may be sent and summed in bfloat16 or wider, within the bound.
No kernel may reach another device: no remote copies, remote signals or barrier semaphores. Data moves between devices by JAX's collectives and lax.ppermute only.
A program may use at most 320 MiB of HBM per device.

```python
import jax
import jax.numpy as jnp
from jax import lax

HEADS = 12
D = 768
FF = 3072
ROWS = 256
SEQS = 16
MICRO = 2
LAYERS = 2
TOKENS = 4096
BH = 384
N_DP = 16


def draw_lengths(key, part):
    key = jax.random.fold_in(key, 7)
    key_div, key_pad, key_pick = jax.random.split(key, 3)
    device_rows = TOKENS // ROWS
    divisor = jax.random.randint(key_div, (MICRO, device_rows, SEQS), 1, 17)
    natural_len = ROWS // divisor
    pad_count = jax.random.randint(key_pad, (MICRO, device_rows, 1), 0, ROWS // 8 + 1)
    chosen = jax.random.randint(key_pick, (), 0, MICRO * device_rows)
    row_number = jnp.arange(MICRO * device_rows).reshape(MICRO, device_rows, 1)
    slot_number = jnp.arange(SEQS).reshape(1, 1, SEQS)
    forced = row_number == chosen
    natural_len = jnp.where(forced & (slot_number == 0), ROWS, natural_len)
    target = jnp.where(forced, ROWS, ROWS - pad_count)
    before = jnp.cumsum(natural_len, axis=-1) - natural_len
    return jnp.clip(target - before, 0, natural_len).astype(jnp.int32)


def with_ends(result, rng, low, top_value):
    shape = result.shape
    spot = [jax.random.randint(jax.random.fold_in(rng, axis), (), 0, shape[axis]) for axis in range(len(shape))]
    result = result.at[tuple(spot)].set(low)
    longest = shape.index(max(shape))
    spot[longest] = (spot[longest] + 1) % shape[longest]
    return result.at[tuple(spot)].set(top_value)


def level_of(own_key, dims, cuts, smallest, top_value):
    factor_of, own = 1.0, jax.random.fold_in(own_key, 6)
    for axis_at, blocks in cuts:
        steps = jnp.exp(jax.random.uniform(jax.random.fold_in(own, axis_at), (blocks,), jnp.float32, smallest / len(cuts), top_value / len(cuts)))
        factor_of = factor_of * jnp.repeat(steps, dims[axis_at] // blocks).reshape([-1 if axis == axis_at else 1 for axis in range(len(dims))])
    return factor_of


def normal_values(key, extent, width, most, shards=(), kind=jnp.bfloat16):
    result = jax.random.normal(key, extent, jnp.float32) * width
    if len(shards) > 0:
        result = level_of(key, extent, shards, -0.22, 0.18) * result
    return jnp.clip(result, min=-most, max=most).astype(kind)


def setup_inputs(seed: int = 0) -> dict:
    arg_keys = jax.random.split(jax.random.key(seed), 16)
    return {
        "content_in": normal_values(arg_keys[0], (MICRO, TOKENS, D), 1.0, 6.0, ((1, 16),)),
        "query_in": normal_values(arg_keys[1], (MICRO, TOKENS, D), 1.0, 6.0, ((1, 16),)),
        "content_cot": normal_values(arg_keys[2], (MICRO, TOKENS, D), 1.0, 6.0, ((1, 16),)),
        "query_cot": normal_values(arg_keys[3], (MICRO, TOKENS, D), 1.0, 6.0, ((1, 16),)),
        "lengths": draw_lengths(jax.random.fold_in(arg_keys[15], 71), 0),
        "order": jax.vmap(lambda own: jax.random.permutation(own, TOKENS))(jax.random.split(arg_keys[5], MICRO)).reshape((MICRO, TOKENS)).astype(jnp.int32),
        "predicted": with_ends((jax.random.randint(arg_keys[6], (MICRO, TOKENS), 0, 100) < 15).astype(jnp.int32), jax.random.fold_in(arg_keys[6], 1), 0, 1),
        "proj_weight": normal_values(arg_keys[7], (LAYERS, 3, D, D), D ** -0.5, 0.21875, ((0, 2),)),
        "out_weight": normal_values(arg_keys[8], (LAYERS, D, D), (D // 16) ** -0.5, 0.875, ((0, 2),)),
        "up_weight": normal_values(arg_keys[9], (LAYERS, D, FF), D ** -0.5, 0.21875, ((0, 2),)),
        "down_weight": normal_values(arg_keys[10], (LAYERS, FF, D), FF ** -0.5, 0.109375, ((0, 2),)),
        "up_bias": normal_values(arg_keys[11], (LAYERS, FF), 0.5, 3.0, ((0, 2),), jnp.float32),
        "biases": normal_values(arg_keys[12], (LAYERS, 6, D), 0.5, 3.0, ((0, 2),), jnp.float32),
        "gains": jnp.clip(1.0 + 0.1 * jax.random.normal(arg_keys[13], (LAYERS, 2, D), jnp.float32), 0.5, 1.5),
        "rel_table": normal_values(arg_keys[14], (LAYERS, BH), 1.0, 5.0, ((0, 2),), jnp.float32),
    }


@jax.custom_vjp
def low(v):
    return lax.optimization_barrier(v.astype(jnp.bfloat16)).astype(jnp.float32)

@jax.custom_vjp
def low_back(v):
    return v

def low_keep(v):
    return (low(v), None)

def low_pass(kept, grad):
    return (grad,)

def back_keep(v):
    return (v, None)

def back_low(kept, grad):
    return (low(grad),)
low.defvjp(low_keep, low_pass)
low_back.defvjp(back_keep, back_low)
PRECISE = lax.Precision.HIGHEST
NEG_FILL = -1e+30
LN_EPS = 1e-05
BUCKET_EDGES = (12, 16, 23, 32, 46, 64, 91)

def round_both(value):
    return low(low_back(value))

def layer_norm(values, gain_vec, shift_vec):
    center = values - lax.optimization_barrier(jnp.mean(values, axis=-1, keepdims=True))
    spread = lax.optimization_barrier(jnp.mean(center * center, axis=-1, keepdims=True))
    return center * lax.rsqrt(spread + LN_EPS) * gain_vec + shift_vec

def bucket_index(relative):
    magnitude = jnp.abs(relative)
    far_part = jnp.full_like(magnitude, 8)
    for edge_at in BUCKET_EDGES:
        far_part = far_part + (magnitude >= edge_at).astype(jnp.int32)
    near_far = jnp.where(magnitude < 8, magnitude, far_part)
    return (near_far + 16 * (relative > 0).astype(jnp.int32)).astype(jnp.int32)

def layout(length_row, order_row, predicted_row):
    row_count = order_row.shape[0]
    tokens_idx = jnp.arange(row_count, dtype=jnp.int32)
    seq_ends = jnp.cumsum(length_row).astype(jnp.int32)
    passed = tokens_idx[:, None] >= seq_ends[None, :]
    segment = lax.optimization_barrier(jnp.sum(passed.astype(jnp.int32), axis=1)).astype(jnp.int32)
    starts = lax.optimization_barrier(jnp.sum(jnp.where(passed, length_row[None, :], 0), axis=1)).astype(jnp.int32)
    inside = tokens_idx < seq_ends[-1]
    position = jnp.where(inside, tokens_idx - starts, 0).astype(jnp.int32)
    segment = jnp.where(inside, segment, -1 - tokens_idx).astype(jnp.int32)
    masked_tok = (predicted_row > 0) & inside & (position > 0)
    same_seq = segment[:, None] == segment[None, :]
    shown_key = jnp.logical_not(masked_tok)[None, :]
    earlier_eq = order_row[None, :] <= order_row[:, None]
    earlier = order_row[None, :] < order_row[:, None]
    see_content = same_seq & (shown_key | earlier_eq)
    see_query = same_seq & (shown_key | earlier)
    buckets = bucket_index(position[None, :] - position[:, None])
    return (see_content, see_query, buckets)

def attention(queries, key_heads, value_heads, rel_bias, visible):
    row_count = queries.shape[0]
    head_count = rel_bias.shape[0]
    query_split = queries.reshape(row_count, head_count, -1)
    key_split = key_heads.reshape(row_count, head_count, -1)
    value_split = value_heads.reshape(row_count, head_count, -1)
    raw_scores = jnp.einsum('qhe,khe->hqk', query_split, key_split, precision=PRECISE) * 0.125 + rel_bias
    scores = low_back(raw_scores)
    logits = jnp.where(visible[None], scores, NEG_FILL)
    softmaxed = jax.nn.softmax(logits, axis=-1)
    mixed_out = jnp.einsum('hqk,khe->qhe', low(softmaxed), value_split, precision=PRECISE)
    return round_both(mixed_out.reshape(row_count, -1))

def run_layer(content, query, probe, params, see_content, see_query, buckets):
    projections, out_proj, up_proj, down_proj, up_shift, bias_rows, gain_rows, table_flat = params
    rel_bias = jnp.transpose(table_flat.reshape(32, HEADS)[buckets], (2, 0, 1))
    key_heads = round_both(jnp.dot(content, projections[1], precision=PRECISE))
    value_heads = round_both(jnp.dot(content, projections[2], precision=PRECISE) + bias_rows[1])

    def run_stream(inputs, visible):
        queries = round_both(jnp.dot(inputs, projections[0], precision=PRECISE) + bias_rows[0])
        mixed_out = attention(queries, key_heads, value_heads, rel_bias, visible)
        branch = low_back(jnp.dot(mixed_out, out_proj, precision=PRECISE) + bias_rows[2])
        normed = layer_norm(inputs + branch, gain_rows[0], bias_rows[4])
        inner_pre = low_back(jnp.dot(low(normed), up_proj, precision=PRECISE) + up_shift)
        act_low = low(jax.nn.gelu(inner_pre, approximate=False))
        ffn_out = low_back(jnp.dot(act_low, down_proj, precision=PRECISE) + bias_rows[3])
        return layer_norm(normed + ffn_out, gain_rows[1], bias_rows[5])
    content_next = round_both(run_stream(content, see_content) + probe[0])
    query_next = round_both(run_stream(query, see_query) + probe[1])
    return (content_next, query_next)

def reference(content_in, query_in, content_cot, query_cot, lengths, order, predicted, proj_weight, out_weight, up_weight, down_weight, up_bias, biases, gains, rel_table):
    params_f32 = tuple((member.astype(jnp.float32) for member in (proj_weight, out_weight, up_weight, down_weight, up_bias, biases, gains, rel_table)))
    block_count = MICRO * N_DP

    def split_blocks(array):
        return array.reshape((block_count, ROWS) + array.shape[2:])
    inputs = (split_blocks(content_in), split_blocks(query_in), split_blocks(content_cot), split_blocks(query_cot), lengths.reshape(block_count, SEQS), split_blocks(order), split_blocks(predicted))

    def block_step(carry_sum, block):
        content_blk, query_blk, content_up, query_up, length_row, order_row, predicted_row = block
        visibility = layout(length_row, order_row, predicted_row)

        def forward(params, content, query, probe):
            layer_one = jax.tree.map(lambda member: member[0], params)
            layer_two = jax.tree.map(lambda member: member[1], params)
            content_mid, query_mid = run_layer(content, query, probe, layer_one, *visibility)
            content_end, query_end = run_layer(content_mid, query_mid, jnp.zeros_like(probe), layer_two, *visibility)
            return (content_mid, query_mid, content_end, query_end)
        zero_probe = jnp.zeros((2, ROWS, D), jnp.float32)
        outputs, pullback = jax.vjp(forward, params_f32, content_blk.astype(jnp.float32), query_blk.astype(jnp.float32), zero_probe)
        zero_rows = jnp.zeros((ROWS, D), jnp.float32)
        grad_params, grad_content, grad_query, grad_probe = pullback((zero_rows, zero_rows, content_up.astype(jnp.float32), query_up.astype(jnp.float32)))
        carry_sum = jax.tree.map(jnp.add, carry_sum, grad_params)
        return (carry_sum, (outputs[0], outputs[2], outputs[1], outputs[3], grad_content, grad_probe[0], grad_query, grad_probe[1]))
    start_sums = tuple((jnp.zeros_like(member) for member in params_f32))
    grad_sums, stacked = lax.scan(block_step, start_sums, inputs)

    def join(layer_one, layer_two):
        return jnp.stack([layer_one.reshape(MICRO, TOKENS, D), layer_two.reshape(MICRO, TOKENS, D)]).astype(jnp.bfloat16)
    content_out = join(stacked[0], stacked[1])
    query_out = join(stacked[2], stacked[3])
    content_grad = join(stacked[4], stacked[5])
    query_grad = join(stacked[6], stacked[7])
    return (content_out, query_out, content_grad, query_grad, grad_sums[0], grad_sums[1], grad_sums[2], grad_sums[3], grad_sums[4], grad_sums[5], grad_sums[6], grad_sums[7])
```

```python
from functools import partial

import jax
import jax.numpy as jnp
from jax import lax
from jax.experimental import pallas as pl
from jax.experimental.pallas import tpu as pltpu
from jax.sharding import PartitionSpec as P

LN_EPS = 1e-05
NEG_FILL = -1e30
BUCKET_EDGES = (12, 16, 23, 32, 46, 64, 91)
BUCKETS = 32
F32, BF16 = jnp.float32, jnp.bfloat16
VMEM_LIMIT = 60 * 1024 * 1024
TAIL = (0.127414796, -0.142248368, 0.7107068705, -0.7265760135, 0.5307027145)
TAIL_SLOPE = 0.3275911 / 2**0.5
DENSITY = 0.3989422804014327


def nn(left, right):
    return jnp.dot(left, right, preferred_element_type=F32)


def nt(left, right):
    return lax.dot_general(left, right, (((1,), (1,)), ((), ())), preferred_element_type=F32)


def iota(shape, dim):
    return lax.broadcasted_iota(jnp.int32, shape, dim)


def bucket_index(relative):
    magnitude = jnp.abs(relative)
    far_part = jnp.full_like(magnitude, 8)
    for edge_at in BUCKET_EDGES:
        far_part = far_part + jnp.where(magnitude >= edge_at, 1, 0)
    near_far = jnp.where(magnitude < 8, magnitude, far_part)
    return near_far + jnp.where(relative > 0, 16, 0)


def gelu_and_slope(v):
    z = jnp.abs(v)
    t = 1.0 / (1.0 + TAIL_SLOPE * z)
    poly = TAIL[4]
    for coefficient in TAIL[3::-1]:
        poly = coefficient + t * poly
    bell = jnp.exp(-0.5 * (v * v))
    tail = t * poly * bell
    below = jnp.where(v >= 0, 1.0 - tail, tail)
    return v * below, below + DENSITY * (v * bell)


class Copies:
    def __init__(self, sems):
        self.sems, self.used, self.open = sems, 0, []

    def start(self, src, dst):
        copy = pltpu.make_async_copy(src, dst, self.sems.at[self.used])
        self.used += 1
        copy.start()
        return copy

    def out(self, src, dst):
        self.open.append(self.start(src, dst))

    def finish(self):
        for copy in self.open:
            copy.wait()


def head_map(entries, heads, span):
    entry = iota((16, entries), 1)
    own_head = (entry - heads * ((entry * 5462) >> 16)) == iota((16, entries), 0)
    bucket = bucket_index(span // 2 - iota((entries, span), 1))
    row = iota((entries, span), 0)
    own_bucket = (row >= heads * bucket) & (row < heads * bucket + heads)
    return own_head, own_bucket


def make_masks(lengths, order_ref, predicted_ref, m, rows):
    def place(shape, dim):
        token = iota(shape, dim)
        segment, start, end = jnp.zeros(shape, jnp.int32), jnp.zeros(shape, jnp.int32), 0
        for slot in range(lengths.shape[2]):
            size = lengths[m, 0, slot]
            end = end + size
            passed = token >= end
            segment = segment + jnp.where(passed, 1, 0)
            start = start + jnp.where(passed, size, 0)
        inside = token < end
        return jnp.where(inside, segment, -1 - token), inside & (token - start > 0)

    segment, later = place((1, rows), 1)
    order = order_ref[pl.ds(m, 1), :]
    flag = (predicted_ref[pl.ds(m, 1), :] > 0) & later
    gate = jnp.where(flag, order, -1).astype(F32)
    gate_column = jnp.transpose(jnp.broadcast_to(gate, (128, rows)))
    segment_column = jnp.transpose(jnp.broadcast_to(segment.astype(F32), (128, rows)))
    gate_column = jnp.concatenate([gate_column] * (rows // 128), axis=1)
    segment_column = jnp.concatenate([segment_column] * (rows // 128), axis=1)
    same = segment_column == segment.astype(F32)
    order = order.astype(F32)
    return [
        jnp.where(same & (gate_column <= order), 0.0, NEG_FILL),
        jnp.where(same & (gate_column < order), 0.0, NEG_FILL),
    ]


def fwd_kernel(m, names_in, names_out, *refs):
    r = dict(zip(names_in, refs))
    refs = refs[len(names_in):]
    r.update(zip(names_out, refs))
    (x_s, wp_s, wo_s, wu_s, wd_s, q_t, k_s, k_t, v_s, v_t, mask_s, toep_s, e_s, inv_s, mix_t, mix_s,
     sum_s, nl_s, act_s, gp_s, xh_s, rs_s, out_s, sems) = refs[len(names_out):]
    rows = x_s.shape[0] // 2
    width = x_s.shape[1]
    heads = r["rel_table"].shape[1] // BUCKETS
    depth = width // heads
    hidden = wu_s.shape[1]
    span = 2 * rows

    @pl.when(r["active"][0] == 1)
    def _():
        cp = Copies(sems)
        if r["xc"].shape[0] == rows:
            xc, xq = r["xc"], r["xq"]
        else:
            xc, xq = r["xc"].at[pl.ds(m * rows, rows)], r["xq"].at[pl.ds(m * rows, rows)]
        get_x = [cp.start(xc, x_s.at[pl.ds(0, rows)]), cp.start(xq, x_s.at[pl.ds(rows, rows)])]
        get_p = [cp.start(r["proj_weight"].at[0, i], wp_s.at[i]) for i in range(3)]
        get_o = cp.start(r["out_weight"].at[0], wo_s)
        get_u = cp.start(r["up_weight"].at[0], wu_s)
        get_d = cp.start(r["down_weight"].at[0], wd_s)

        masks = make_masks(r["lengths"], r["order"], r["predicted"], m, rows)
        mask_s[0], mask_s[1] = masks
        own_head, own_bucket = head_map(heads * BUCKETS, heads, span)
        picked = jnp.where(own_head, r["rel_table"][...], 0.0)
        toep_s[...] = jnp.dot(
            picked, jnp.where(own_bucket, 1.0, 0.0), precision=lax.Precision.HIGHEST, preferred_element_type=F32
        )
        biases = r["biases"]
        gains = r["gains"]

        for copy in get_x:
            copy.wait()
        wrows = [pl.ds(s * 2 * rows + m * rows, rows) for s in range(2)]
        for s in range(2):
            cp.out(x_s.at[pl.ds(s * rows, rows)], r["w_x"].at[wrows[s]])
        step = 256
        get_p[0].wait()
        for n in range(0, width, step):
            q = nn(x_s[...], wp_s[0, :, n:n + step]) + biases[0, 0:1, n:n + step]
            q_t[n:n + step, :] = jnp.transpose(q.astype(BF16) * 0.125)
        get_p[1].wait()
        get_p[2].wait()
        for n in range(0, width, step):
            k = nn(x_s[0:rows, :], wp_s[1, :, n:n + step]).astype(BF16)
            k_s[:, n:n + step] = k
            k_t[n:n + step, :] = jnp.transpose(k)
            v = (nn(x_s[0:rows, :], wp_s[2, :, n:n + step]) + biases[0, 1:2, n:n + step]).astype(BF16)
            v_s[:, n:n + step] = v
            v_t[n:n + step, :] = jnp.transpose(v)
        cp.out(q_t, r["q_t"])
        cp.out(k_s, r["k"])
        cp.out(k_t, r["k_t"])
        cp.out(v_s, r["v"])

        blank = jnp.zeros((depth, 2 * rows), BF16)

        def pair_step(pair, carry):
            base = pl.multiple_of(pair * 2 * depth, 2 * depth)
            k_pair = k_s[:, pl.ds(base, 2 * depth)]
            for half in range(2):
                head = 2 * pair + half
                at = pl.multiple_of(base + half * depth, depth)
                q_head = q_t[pl.ds(at, depth), :]
                stacked = jnp.concatenate([q_head, blank] if half == 0 else [blank, q_head], axis=0)
                scores = nn(k_pair, stacked)
                line = jnp.broadcast_to(toep_s[pl.ds(head, 1), :], (rows, span))
                rel = pltpu.roll(line, rows, 1, stride=1, stride_axis=0)[:, :rows]
                for s in range(2):
                    logits = scores[:, s * rows:(s + 1) * rows] + rel + mask_s[s]
                    top = jnp.max(logits, axis=0, keepdims=True)
                    e = jnp.exp(logits - top)
                    inv = 1.0 / jnp.sum(e, axis=0, keepdims=True)
                    e = e.astype(BF16)
                    e_s[s, head] = e
                    inv_s[s, pl.ds(head, 1), :] = inv
                    mixed = nn(v_t[pl.ds(at, depth), :], e) * inv
                    mix_t[pl.ds(at, depth), s * rows:(s + 1) * rows] = mixed.astype(BF16)
            return carry

        lax.fori_loop(0, heads // 2, pair_step, 0)
        cp.out(e_s, r["e"])
        cp.out(inv_s, r["inv"])
        for s in range(2):
            cp.out(mix_t.at[:, pl.ds(s * rows, rows)], r["w_mix_t"].at[:, wrows[s]])
        for n in range(0, width, step):
            mix_s[:, n:n + step] = jnp.transpose(mix_t[n:n + step, :])
        get_o.wait()
        for n in range(0, width, step):
            sum_s[:, n:n + step] = nn(mix_s[...], wo_s[:, n:n + step])

        block = 64

        def norm_one(i, carry):
            at = pl.ds(pl.multiple_of(i * block, block), block)
            summed = x_s[at, :].astype(F32) + sum_s[at, :] + biases[0, 2:3, :]
            center = summed - jnp.mean(summed, axis=1, keepdims=True)
            scale = lax.rsqrt(jnp.mean(center * center, axis=1, keepdims=True) + LN_EPS)
            xhat = center * scale
            normed = xhat * gains[0, 0:1, :] + biases[0, 4:5, :]
            xh_s[0, at, :] = xhat.astype(BF16)
            rs_s[0, at, :] = jnp.broadcast_to(scale, (block, 128))
            nl_s[at, :] = normed.astype(BF16)
            sum_s[at, :] = normed + biases[0, 3:4, :]
            return carry

        lax.fori_loop(0, 2 * rows // block, norm_one, 0)
        for s in range(2):
            cp.out(nl_s.at[pl.ds(s * rows, rows)], r["w_nl"].at[wrows[s]])
        get_u.wait()
        chunk = 512

        def up_step(j, carry):
            at = pl.ds(pl.multiple_of(j * chunk, chunk), chunk)
            pre = nn(nl_s[...], wu_s[:, at]) + r["up_bias"][0:1, at]
            act, slope = gelu_and_slope(pre)
            act_s[:, at] = act.astype(BF16)
            gp_s[:, at] = slope.astype(BF16)
            return carry

        lax.fori_loop(0, hidden // chunk, up_step, 0)
        cp.out(gp_s, r["gp"])
        for s in range(2):
            cp.out(act_s.at[pl.ds(s * rows, rows)], r["w_act"].at[wrows[s]])
        get_d.wait()
        for n in range(0, width, step):
            sum_s[:, n:n + step] += nn(act_s[...], wd_s[:, n:n + step])

        def norm_two(i, carry):
            at = pl.ds(pl.multiple_of(i * block, block), block)
            total = sum_s[at, :]
            center = total - jnp.mean(total, axis=1, keepdims=True)
            scale = lax.rsqrt(jnp.mean(center * center, axis=1, keepdims=True) + LN_EPS)
            xhat = center * scale
            xh_s[1, at, :] = xhat.astype(BF16)
            rs_s[1, at, :] = jnp.broadcast_to(scale, (block, 128))
            out_s[at, :] = (xhat * gains[0, 1:2, :] + biases[0, 5:6, :]).astype(BF16)
            return carry

        lax.fori_loop(0, 2 * rows // block, norm_two, 0)
        for s in range(2):
            cp.out(out_s.at[pl.ds(s * rows, rows)], r["out"].at[s])
        cp.out(xh_s, r["xhat"])
        cp.out(rs_s, r["scale"])
        cp.finish()


def bwd_kernel(m, names_in, names_out, *refs):
    r = dict(zip(names_in, refs))
    refs = refs[len(names_in):]
    r.update(zip(names_out, refs))
    (g_s, wp_s, wo_s, wu_s, wd_s, q_t, k_s, k_t, v_s, e_s, inv_s, gp_s, xh_s, rs_s,
     grad_s, dz_s, dpre_s, acc_s, da_s, dm_t, dq_t, dk_t, dv_t, dq_s, dk_s, dv_s, diag_s, small_s, upb_s, tab_s,
     out_s, sems) = refs[len(names_out):]
    rows = g_s.shape[0] // 2
    width = g_s.shape[1]
    heads = r["rel_table"].shape[1] // BUCKETS
    depth = width // heads
    hidden = wu_s.shape[1]
    span = 2 * rows

    @pl.when(r["active"][0] == 1)
    def _():
        cp = Copies(sems)
        if r["gc"].shape[0] == rows:
            gc, gq = r["gc"], r["gq"]
        else:
            gc, gq = r["gc"].at[pl.ds(m * rows, rows)], r["gq"].at[pl.ds(m * rows, rows)]
        wrows = [pl.ds(s * 2 * rows + m * rows, rows) for s in range(2)]
        get_g = [cp.start(gc, g_s.at[pl.ds(0, rows)]), cp.start(gq, g_s.at[pl.ds(rows, rows)])]
        get_g += [cp.start(r["xhat"], xh_s), cp.start(r["scale"], rs_s)]
        get_d = cp.start(r["down_weight"].at[0], wd_s)
        get_gp = cp.start(r["gp"], gp_s)
        get_u = cp.start(r["up_weight"].at[0], wu_s)
        get_o = cp.start(r["out_weight"].at[0], wo_s)
        get_a = [cp.start(r["inv"], inv_s)]
        get_e = [cp.start(r["e"], e_s), cp.start(r["q_t"], q_t), cp.start(r["k"], k_s)]
        get_e += [cp.start(r["k_t"], k_t), cp.start(r["v"], v_s)]
        get_p = [cp.start(r["proj_weight"].at[0, i], wp_s.at[i]) for i in range(3)]
        gains = r["gains"]
        small_s[...] = jnp.zeros(small_s.shape, F32)
        step, block, chunk = 256, 64, 512

        def add_small(row, value):
            small_s[row:row + 1, :] += jnp.sum(value, axis=0, keepdims=True)

        for copy in get_g:
            copy.wait()

        def norm_two(i, carry):
            at = pl.ds(pl.multiple_of(i * block, block), block)
            grad = g_s[at, :].astype(F32)
            xhat = xh_s[1, at, :].astype(F32)
            both = grad * xhat
            add_small(7, both)
            add_small(5, grad)
            scaled = grad * gains[0, 1:2, :]
            mean_a = jnp.mean(scaled, axis=1, keepdims=True)
            mean_b = jnp.mean(scaled * xhat, axis=1, keepdims=True)
            back = (scaled - mean_a - xhat * mean_b) * rs_s[1, at, 0:1]
            grad_s[at, :] = back
            low = back.astype(BF16)
            dz_s[at, :] = low
            add_small(3, low.astype(F32))
            return carry

        lax.fori_loop(0, 2 * rows // block, norm_two, 0)
        for s in range(2):
            cp.out(dz_s.at[pl.ds(s * rows, rows)], r["w_dz"].at[wrows[s]])
        get_d.wait()
        get_gp.wait()

        def up_step(j, carry):
            at = pl.ds(pl.multiple_of(j * chunk, chunk), chunk)
            d_act = nt(dz_s[...], wd_s[at, :])
            d_pre = (d_act * gp_s[:, at].astype(F32)).astype(BF16)
            dpre_s[:, at] = d_pre
            upb_s[0:1, at] = jnp.sum(d_pre.astype(F32), axis=0, keepdims=True)
            return carry

        lax.fori_loop(0, hidden // chunk, up_step, 0)
        for s in range(2):
            cp.out(dpre_s.at[pl.ds(s * rows, rows)], r["w_dpre"].at[wrows[s]])
        get_u.wait()
        for n in range(0, width, step):
            acc_s[:, n:n + step] = nt(dpre_s[...], wu_s[n:n + step, :])

        def norm_one(i, carry):
            at = pl.ds(pl.multiple_of(i * block, block), block)
            grad = grad_s[at, :] + acc_s[at, :]
            xhat = xh_s[0, at, :].astype(F32)
            add_small(6, grad * xhat)
            add_small(4, grad)
            scaled = grad * gains[0, 0:1, :]
            mean_a = jnp.mean(scaled, axis=1, keepdims=True)
            mean_b = jnp.mean(scaled * xhat, axis=1, keepdims=True)
            back = (scaled - mean_a - xhat * mean_b) * rs_s[0, at, 0:1]
            grad_s[at, :] = back
            low = back.astype(BF16)
            da_s[at, :] = low
            add_small(2, low.astype(F32))
            return carry

        lax.fori_loop(0, 2 * rows // block, norm_one, 0)
        for s in range(2):
            cp.out(da_s.at[pl.ds(s * rows, rows)], r["w_da"].at[wrows[s]])
        get_o.wait()
        for copy in get_a:
            copy.wait()
        for n in range(0, width, step):
            d_mix = nt(wo_s[n:n + step, :], da_s[...])
            for h in range(n // depth, (n + step) // depth):
                part = d_mix[h * depth - n:(h + 1) * depth - n, :]
                inv = jnp.concatenate([inv_s[s, h:h + 1, :] for s in range(2)], axis=1)
                dm_t[h * depth:(h + 1) * depth, :] = (part * inv).astype(BF16)
        for copy in get_e:
            copy.wait()
        blank = jnp.zeros((depth, 2 * rows), BF16)
        diag_s[...] = jnp.zeros(diag_s.shape, F32)

        def pair_step(pair, carry):
            base = pl.multiple_of(pair * 2 * depth, 2 * depth)
            v_pair = v_s[:, pl.ds(base, 2 * depth)]
            for half in range(2):
                head = 2 * pair + half
                at = pl.ds(pl.multiple_of(base + half * depth, depth), depth)
                dm_head = dm_t[at, :]
                stacked = jnp.concatenate([dm_head, blank] if half == 0 else [blank, dm_head], axis=0)
                d_prob = nn(v_pair, stacked)
                parts, whole = [], 0.0
                for s in range(2):
                    e = e_s[s, head].astype(F32)
                    part = d_prob[:, s * rows:(s + 1) * rows]
                    mean = jnp.sum(e * part, axis=0, keepdims=True) * inv_s[s, pl.ds(head, 1), :]
                    d_score = (e * (part - mean)).astype(BF16)
                    parts.append(d_score)
                    whole = whole + d_score.astype(F32)
                both = jnp.concatenate(parts, axis=1)
                e_both = jnp.concatenate([e_s[0, head], e_s[1, head]], axis=1)
                dq_t[at, :] = (nn(k_t[at, :], both) * 0.125).astype(BF16)
                dv_t[at, :] = nt(dm_head, e_both).astype(BF16)
                dk_t[at, :] = nt(q_t[at, :], both).astype(BF16)
                wide = jnp.concatenate([jnp.zeros_like(whole), whole], axis=1)
                count = rows
                while count > 8:
                    count //= 2
                    wide = wide[:count, :] + pltpu.roll(wide[count:, :], span - count, 1)
                line = wide[0:1, :]
                for k in range(1, 8):
                    line = line + pltpu.roll(wide, span - k, 1)[k:k + 1, :]
                diag_s[pl.ds(head, 1), :] = line
            return carry

        lax.fori_loop(0, heads // 2, pair_step, 0)
        for n in range(0, width, step):
            part = jnp.transpose(dq_t[n:n + step, :])
            dq_s[:, n:n + step] = part
            small_s[0:1, n:n + step] = jnp.sum(part.astype(F32), axis=0, keepdims=True)
            dk_s[:, n:n + step] = jnp.transpose(dk_t[n:n + step, :])
            part = jnp.transpose(dv_t[n:n + step, :])
            dv_s[:, n:n + step] = part
            small_s[1:2, n:n + step] = jnp.sum(part.astype(F32), axis=0, keepdims=True)
        for s in range(2):
            cp.out(dq_s.at[pl.ds(s * rows, rows)], r["w_dq"].at[wrows[s]])
        cp.out(dk_s, r["w_dk"].at[pl.ds(m * rows, rows)])
        cp.out(dv_s, r["w_dv"].at[pl.ds(m * rows, rows)])
        for copy in get_p:
            copy.wait()
        for n in range(0, width, step):
            back = grad_s[:, n:n + step] + nt(dq_s[...], wp_s[0, n:n + step, :])
            more = nt(dk_s[...], wp_s[1, n:n + step, :]) + nt(dv_s[...], wp_s[2, n:n + step, :])
            out_s[0:rows, n:n + step] = (back[0:rows, :] + more).astype(BF16)
            out_s[rows:, n:n + step] = back[rows:, :].astype(BF16)
        for s in range(2):
            cp.out(out_s.at[pl.ds(s * rows, rows)], r["grad"].at[s])

        own_head, own_bucket = head_map(heads * BUCKETS, heads, span)
        folded = lax.dot_general(
            diag_s[...],
            jnp.where(own_bucket, 1.0, 0.0),
            (((1,), (1,)), ((), ())),
            precision=lax.Precision.HIGHEST,
            preferred_element_type=F32,
        )
        tab_s[...] = jnp.broadcast_to(
            jnp.sum(jnp.where(own_head, folded, 0.0), axis=0, keepdims=True), tab_s.shape
        )
        cp.out(small_s, r["small"])
        cp.out(upb_s, r["up_small"])
        cp.out(tab_s, r["tab_small"])
        cp.finish()


SMEM = pl.BlockSpec(memory_space=pltpu.SMEM)
VMEM = pl.BlockSpec(memory_space=pltpu.VMEM)
ANY = pl.BlockSpec(memory_space=pl.ANY)


def call(kernel, m, operands, buffers, made, scratch, flops, copies):
    names_in = list(operands) + ["old_" + name for name in buffers]
    names_out = list(buffers) + list(made)
    shapes = [jax.ShapeDtypeStruct(a.shape, a.dtype) for a in buffers.values()] + list(made.values())
    outs = pl.pallas_call(
        partial(kernel, m, names_in, names_out),
        in_specs=[spec for _, spec in operands.values()] + [ANY] * len(buffers),
        out_specs=[ANY] * len(names_out),
        out_shape=shapes,
        scratch_shapes=scratch + [pltpu.SemaphoreType.DMA((copies,))],
        input_output_aliases={len(operands) + i: i for i in range(len(buffers))},
        compiler_params=pltpu.CompilerParams(vmem_limit_bytes=VMEM_LIMIT),
        cost_estimate=pl.CostEstimate(flops=flops, bytes_accessed=30_000_000, transcendentals=0),
    )(*[a for a, _ in operands.values()], *buffers.values())
    return dict(zip(names_out, outs))


def shape(*dims, dtype=BF16):
    return jax.ShapeDtypeStruct(dims, dtype)


def forward_shapes(rows, width, hidden, heads):
    return {
        "q_t": shape(width, 2 * rows),
        "k": shape(rows, width),
        "k_t": shape(width, rows),
        "v": shape(rows, width),
        "e": shape(2, heads, rows, rows),
        "inv": shape(2, 16, rows, dtype=F32),
        "gp": shape(2 * rows, hidden),
        "xhat": shape(2, 2 * rows, width),
        "scale": shape(2, 2 * rows, 128, dtype=F32),
        "out": shape(2, rows, width),
    }


def forward(m, active, xc, xq, fixed, weights, kept, store):
    rows, width, hidden, heads, micro = fixed["dims"]
    operands = {
        "active": (active, SMEM),
        "lengths": (fixed["lengths"], SMEM),
        "order": (fixed["order"], VMEM),
        "predicted": (fixed["predicted"], VMEM),
        "rel_table": (weights["rel_table"], VMEM),
        "up_bias": (weights["up_bias"], VMEM),
        "biases": (weights["biases"], VMEM),
        "gains": (weights["gains"], VMEM),
        "proj_weight": (weights["proj_weight"], ANY),
        "out_weight": (weights["out_weight"], ANY),
        "up_weight": (weights["up_weight"], ANY),
        "down_weight": (weights["down_weight"], ANY),
        "xc": (xc, ANY),
        "xq": (xq, ANY),
    }
    wide = 2 * rows * micro
    made = {}
    if kept is None:
        made.update(forward_shapes(rows, width, hidden, heads))
    if store is None:
        made.update(
            w_x=shape(wide, width), w_mix_t=shape(width, wide), w_nl=shape(wide, width), w_act=shape(wide, hidden)
        )
    both = 2 * rows
    scratch = [
        pltpu.VMEM((both, width), BF16),
        pltpu.VMEM((3, width, width), BF16),
        pltpu.VMEM((width, width), BF16),
        pltpu.VMEM((width, hidden), BF16),
        pltpu.VMEM((hidden, width), BF16),
        pltpu.VMEM((width, both), BF16),
        pltpu.VMEM((rows, width), BF16),
        pltpu.VMEM((width, rows), BF16),
        pltpu.VMEM((rows, width), BF16),
        pltpu.VMEM((width, rows), BF16),
        pltpu.VMEM((2, rows, rows), F32),
        pltpu.VMEM((16, 2 * rows), F32),
        pltpu.VMEM((2, heads, rows, rows), BF16),
        pltpu.VMEM((2, 16, rows), F32),
        pltpu.VMEM((width, both), BF16),
        pltpu.VMEM((both, width), BF16),
        pltpu.VMEM((both, width), F32),
        pltpu.VMEM((both, width), BF16),
        pltpu.VMEM((both, hidden), BF16),
        pltpu.VMEM((both, hidden), BF16),
        pltpu.VMEM((2, both, width), BF16),
        pltpu.VMEM((2, both, 128), F32),
        pltpu.VMEM((both, width), BF16),
    ]
    buffers = {**(kept or {}), **(store or {})}
    outs = call(fwd_kernel, m, operands, buffers, made, scratch, 8_000_000_000, 32)
    return (
        {n: v for n, v in outs.items() if not n.startswith("w_")},
        {n: v for n, v in outs.items() if n.startswith("w_")},
    )


def backward(m, active, gc, gq, fixed, weights, kept, store, back, made_back):
    rows, width, hidden, heads, micro = fixed["dims"]
    operands = {
        "active": (active, SMEM),
        "rel_table": (weights["rel_table"], VMEM),
        "gains": (weights["gains"], VMEM),
        "proj_weight": (weights["proj_weight"], ANY),
        "out_weight": (weights["out_weight"], ANY),
        "up_weight": (weights["up_weight"], ANY),
        "down_weight": (weights["down_weight"], ANY),
        "gc": (gc, ANY),
        "gq": (gq, ANY),
    }
    for name in ("q_t", "k", "k_t", "v", "e", "inv", "gp", "xhat", "scale"):
        operands[name] = (kept[name], ANY)
    wide = 2 * rows * micro
    both = 2 * rows
    made = {}
    if back is None:
        made.update(
            w_dz=shape(wide, width),
            w_dpre=shape(wide, hidden),
            w_da=shape(wide, width),
            w_dq=shape(wide, width),
            w_dk=shape(wide // 2, width),
            w_dv=shape(wide // 2, width),
        )
    if made_back is None:
        made.update(
            grad=shape(2, rows, width),
            small=shape(8, width, dtype=F32),
            up_small=shape(8, hidden, dtype=F32),
            tab_small=shape(8, heads * BUCKETS, dtype=F32),
        )
    scratch = [
        pltpu.VMEM((both, width), BF16),
        pltpu.VMEM((3, width, width), BF16),
        pltpu.VMEM((width, width), BF16),
        pltpu.VMEM((width, hidden), BF16),
        pltpu.VMEM((hidden, width), BF16),
        pltpu.VMEM((width, both), BF16),
        pltpu.VMEM((rows, width), BF16),
        pltpu.VMEM((width, rows), BF16),
        pltpu.VMEM((rows, width), BF16),
        pltpu.VMEM((2, heads, rows, rows), BF16),
        pltpu.VMEM((2, 16, rows), F32),
        pltpu.VMEM((both, hidden), BF16),
        pltpu.VMEM((2, both, width), BF16),
        pltpu.VMEM((2, both, 128), F32),
        pltpu.VMEM((both, width), F32),
        pltpu.VMEM((both, width), BF16),
        pltpu.VMEM((both, hidden), BF16),
        pltpu.VMEM((both, width), F32),
        pltpu.VMEM((both, width), BF16),
        pltpu.VMEM((width, both), BF16),
        pltpu.VMEM((width, both), BF16),
        pltpu.VMEM((width, rows), BF16),
        pltpu.VMEM((width, rows), BF16),
        pltpu.VMEM((both, width), BF16),
        pltpu.VMEM((rows, width), BF16),
        pltpu.VMEM((rows, width), BF16),
        pltpu.VMEM((16, both), F32),
        pltpu.VMEM((8, width), F32),
        pltpu.VMEM((8, hidden), F32),
        pltpu.VMEM((8, heads * BUCKETS), F32),
        pltpu.VMEM((both, width), BF16),
    ]
    buffers = {**(back or {}), **(made_back or {})}
    outs = call(bwd_kernel, m, operands, buffers, made, scratch, 8_000_000_000, 36)
    return (
        {n: v for n, v in outs.items() if n.startswith("w_")},
        {n: v for n, v in outs.items() if not n.startswith("w_")},
    )


def contract_rows(left, right):
    return jnp.einsum("ra,rb->ab", left, right, preferred_element_type=F32)


def body(
    content_in,
    query_in,
    content_cot,
    query_cot,
    lengths,
    order,
    predicted,
    proj_weight,
    out_weight,
    up_weight,
    down_weight,
    up_bias,
    biases,
    gains,
    rel_table,
):
    micro, rows, width = content_in.shape
    hidden = up_bias.shape[1]
    heads = rel_table.shape[1] // BUCKETS
    first = (lax.axis_index("section") == 0).astype(jnp.int32).reshape(1)
    second = 1 - first
    weights = dict(
        proj_weight=proj_weight,
        out_weight=out_weight,
        up_weight=up_weight,
        down_weight=down_weight,
        up_bias=up_bias,
        biases=biases,
        gains=gains,
        rel_table=rel_table,
    )
    fixed = dict(lengths=lengths, order=order, predicted=predicted, dims=(rows, width, hidden, heads, micro))
    flat = lambda a: a.reshape(micro * rows, width)
    ahead, behind = [(0, 1)], [(1, 0)]
    kept, store, arrived = [None] * micro, None, [None] * micro
    for m in range(micro):
        kept[m], store = forward(m, first, flat(content_in), flat(query_in), fixed, weights, None, store)
        arrived[m] = lax.ppermute(kept[m]["out"], "section", ahead)
    back, made, returned = None, [None] * micro, [None] * micro
    for m in range(micro):
        kept[m], store = forward(m, second, arrived[m][0], arrived[m][1], fixed, weights, kept[m], store)
        back, made[m] = backward(
            m, second, flat(content_cot), flat(query_cot), fixed, weights, kept[m], store, back, None
        )
        returned[m] = lax.ppermute(made[m]["grad"], "section", behind)
    for m in range(micro):
        back, made[m] = backward(
            m, first, returned[m][0], returned[m][1], fixed, weights, kept[m], store, back, made[m]
        )
    half = micro * rows
    down_grad = contract_rows(store["w_act"], back["w_dz"])
    up_grad = contract_rows(store["w_nl"], back["w_dpre"])
    out_grad = jnp.dot(store["w_mix_t"], back["w_da"], preferred_element_type=F32)
    proj_grad = jnp.stack(
        [
            contract_rows(store["w_x"], back["w_dq"]),
            contract_rows(store["w_x"][:half], back["w_dk"]),
            contract_rows(store["w_x"][:half], back["w_dv"]),
        ]
    )
    small = sum(part["small"] for part in made)
    up_small = sum(part["up_small"] for part in made)[0]
    tab_small = sum(part["tab_small"] for part in made)[0]

    def scatter(array, dim):
        array = array.astype(BF16)
        return lax.psum_scatter(array, "dp", scatter_dimension=dim, tiled=True).astype(F32)[None]

    small = scatter(small, 1)
    stack = lambda name, parts, s: jnp.stack([part[name][s] for part in parts])[None]
    return (
        stack("out", kept, 0),
        stack("out", kept, 1),
        stack("grad", made, 0),
        stack("grad", made, 1),
        scatter(proj_grad, 1),
        scatter(out_grad, 0),
        scatter(up_grad, 0),
        scatter(down_grad, 0),
        scatter(up_small, 0),
        small[:, 0:6],
        small[:, 6:8],
        scatter(tab_small, 0),
    )


def solution(mesh):
    return jax.shard_map(
        body,
        mesh=mesh,
        in_specs=(
            P(None, "dp", None),
            P(None, "dp", None),
            P(None, "dp", None),
            P(None, "dp", None),
            P(None, "dp", None),
            P(None, "dp"),
            P(None, "dp"),
            P("section", None, None, None),
            P("section", None, None),
            P("section", None, None),
            P("section", None, None),
            P("section", None),
            P("section", None, None),
            P("section", None, None),
            P("section", None),
        ),
        out_specs=(
            P("section", None, "dp", None),
            P("section", None, "dp", None),
            P("section", None, "dp", None),
            P("section", None, "dp", None),
            P("section", None, "dp", None),
            P("section", "dp", None),
            P("section", "dp", None),
            P("section", "dp", None),
            P("section", "dp"),
            P("section", None, "dp"),
            P("section", None, "dp"),
            P("section", "dp"),
        ),
        check_vma=False,
    )
```

```python
from functools import partial

import jax
import jax.numpy as jnp
from jax import lax
from jax.experimental import pallas as pl
from jax.experimental.pallas import tpu as pltpu
from jax.sharding import PartitionSpec as P

LN_EPS = 1e-05
NEG_FILL = -1e30
BUCKET_EDGES = (12, 16, 23, 32, 46, 64, 91)
BUCKETS = 32
F32, BF16 = jnp.float32, jnp.bfloat16
VMEM_LIMIT = 60 * 1024 * 1024
TAIL = (0.127414796, -0.142248368, 0.7107068705, -0.7265760135, 0.5307027145)
TAIL_SLOPE = 0.3275911 / 2**0.5
DENSITY = 0.3989422804014327


def nn(left, right):
    return jnp.dot(left, right, preferred_element_type=F32)


def nt(left, right):
    return lax.dot_general(left, right, (((1,), (1,)), ((), ())), preferred_element_type=F32)


def iota(shape, dim):
    return lax.broadcasted_iota(jnp.int32, shape, dim)


def bucket_index(relative):
    magnitude = jnp.abs(relative)
    far_part = jnp.full_like(magnitude, 8)
    for edge_at in BUCKET_EDGES:
        far_part = far_part + jnp.where(magnitude >= edge_at, 1, 0)
    near_far = jnp.where(magnitude < 8, magnitude, far_part)
    return near_far + jnp.where(relative > 0, 16, 0)


def gelu_and_slope(v):
    z = jnp.abs(v)
    t = 1.0 / (1.0 + TAIL_SLOPE * z)
    poly = TAIL[4]
    for coefficient in TAIL[3::-1]:
        poly = coefficient + t * poly
    bell = jnp.exp(-0.5 * (v * v))
    tail = t * poly * bell
    below = jnp.where(v >= 0, 1.0 - tail, tail)
    return v * below, below + DENSITY * (v * bell)


class Copies:
    def __init__(self, sems):
        self.sems, self.used, self.open = sems, 0, []

    def start(self, src, dst):
        copy = pltpu.make_async_copy(src, dst, self.sems.at[self.used])
        self.used += 1
        copy.start()
        return copy

    def out(self, src, dst):
        self.open.append(self.start(src, dst))

    def finish(self):
        for copy in self.open:
            copy.wait()


def head_map(entries, heads, span):
    entry = iota((16, entries), 1)
    own_head = (entry - heads * ((entry * 5462) >> 16)) == iota((16, entries), 0)
    bucket = bucket_index(span // 2 - iota((entries, span), 1))
    row = iota((entries, span), 0)
    own_bucket = (row >= heads * bucket) & (row < heads * bucket + heads)
    return own_head, own_bucket


def make_masks(lengths, order_ref, predicted_ref, m, rows):
    def place(shape, dim):
        token = iota(shape, dim)
        segment, start, end = jnp.zeros(shape, jnp.int32), jnp.zeros(shape, jnp.int32), 0
        for slot in range(lengths.shape[2]):
            size = lengths[m, 0, slot]
            end = end + size
            passed = token >= end
            segment = segment + jnp.where(passed, 1, 0)
            start = start + jnp.where(passed, size, 0)
        inside = token < end
        return jnp.where(inside, segment, -1 - token), inside & (token - start > 0)

    segment, later = place((1, rows), 1)
    order = order_ref[pl.ds(m, 1), :]
    flag = (predicted_ref[pl.ds(m, 1), :] > 0) & later
    gate = jnp.where(flag, order, -1).astype(F32)
    gate_column = jnp.transpose(jnp.broadcast_to(gate, (128, rows)))
    segment_column = jnp.transpose(jnp.broadcast_to(segment.astype(F32), (128, rows)))
    gate_column = jnp.concatenate([gate_column] * (rows // 128), axis=1)
    segment_column = jnp.concatenate([segment_column] * (rows // 128), axis=1)
    same = segment_column == segment.astype(F32)
    order = order.astype(F32)
    return [
        jnp.where(same & (gate_column <= order), 0.0, NEG_FILL),
        jnp.where(same & (gate_column < order), 0.0, NEG_FILL),
    ]


def fwd_kernel(m, names_in, names_out, *refs):
    r = dict(zip(names_in, refs))
    refs = refs[len(names_in):]
    r.update(zip(names_out, refs))
    (x_s, wp_s, wo_s, wu_s, wd_s, q_t, k_s, k_t, v_s, v_t, mask_s, toep_s, e_s, inv_s, mix_t, mix_s,
     sum_s, nl_s, act_s, gp_s, xh_s, rs_s, out_s, sems) = refs[len(names_out):]
    rows = x_s.shape[0] // 2
    width = x_s.shape[1]
    heads = r["rel_table"].shape[1] // BUCKETS
    depth = width // heads
    hidden = wu_s.shape[1]
    span = 2 * rows

    @pl.when(r["active"][0] == 1)
    def _():
        cp = Copies(sems)
        if r["xc"].shape[0] == rows:
            xc, xq = r["xc"], r["xq"]
        else:
            xc, xq = r["xc"].at[pl.ds(m * rows, rows)], r["xq"].at[pl.ds(m * rows, rows)]
        get_x = [cp.start(xc, x_s.at[pl.ds(0, rows)]), cp.start(xq, x_s.at[pl.ds(rows, rows)])]
        get_p = [cp.start(r["proj_weight"].at[0, i], wp_s.at[i]) for i in range(3)]
        get_o = cp.start(r["out_weight"].at[0], wo_s)
        get_u = cp.start(r["up_weight"].at[0], wu_s)
        get_d = cp.start(r["down_weight"].at[0], wd_s)

        masks = make_masks(r["lengths"], r["order"], r["predicted"], m, rows)
        mask_s[0], mask_s[1] = masks
        own_head, own_bucket = head_map(heads * BUCKETS, heads, span)
        picked = jnp.where(own_head, r["rel_table"][...], 0.0)
        toep_s[...] = jnp.dot(
            picked, jnp.where(own_bucket, 1.0, 0.0), precision=lax.Precision.HIGHEST, preferred_element_type=F32
        )
        biases = r["biases"]
        gains = r["gains"]

        for copy in get_x:
            copy.wait()
        wrows = [pl.ds(s * 2 * rows + m * rows, rows) for s in range(2)]
        for s in range(2):
            cp.out(x_s.at[pl.ds(s * rows, rows)], r["w_x"].at[wrows[s]])
        step = 256
        get_p[0].wait()
        for n in range(0, width, step):
            q = nn(x_s[...], wp_s[0, :, n:n + step]) + biases[0, 0:1, n:n + step]
            q_t[n:n + step, :] = jnp.transpose(q.astype(BF16) * 0.125)
        get_p[1].wait()
        get_p[2].wait()
        for n in range(0, width, step):
            k = nn(x_s[0:rows, :], wp_s[1, :, n:n + step]).astype(BF16)
            k_s[:, n:n + step] = k
            k_t[n:n + step, :] = jnp.transpose(k)
            v = (nn(x_s[0:rows, :], wp_s[2, :, n:n + step]) + biases[0, 1:2, n:n + step]).astype(BF16)
            v_s[:, n:n + step] = v
            v_t[n:n + step, :] = jnp.transpose(v)
        cp.out(q_t, r["q_t"])
        cp.out(k_s, r["k"])
        cp.out(k_t, r["k_t"])
        cp.out(v_s, r["v"])

        blank = jnp.zeros((depth, 2 * rows), BF16)

        for pair in range(heads // 2):
            base = pair * 2 * depth
            k_pair = k_s[:, pl.ds(base, 2 * depth)]
            for half in range(2):
                head = 2 * pair + half
                at = base + half * depth
                q_head = q_t[pl.ds(at, depth), :]
                stacked = jnp.concatenate([q_head, blank] if half == 0 else [blank, q_head], axis=0)
                scores = nn(k_pair, stacked)
                line = jnp.broadcast_to(toep_s[pl.ds(head, 1), :], (rows, span))
                rel = pltpu.roll(line, rows, 1, stride=1, stride_axis=0)[:, :rows]
                for s in range(2):
                    logits = scores[:, s * rows:(s + 1) * rows] + rel + mask_s[s]
                    top = jnp.max(logits, axis=0, keepdims=True)
                    e = jnp.exp(logits - top)
                    inv = 1.0 / jnp.sum(e, axis=0, keepdims=True)
                    e = e.astype(BF16)
                    e_s[s, head] = e
                    inv_s[s, pl.ds(head, 1), :] = inv
                    mixed = nn(v_t[pl.ds(at, depth), :], e) * inv
                    mix_t[pl.ds(at, depth), s * rows:(s + 1) * rows] = mixed.astype(BF16)
        cp.out(e_s, r["e"])
        cp.out(inv_s, r["inv"])
        for s in range(2):
            cp.out(mix_t.at[:, pl.ds(s * rows, rows)], r["w_mix_t"].at[:, wrows[s]])
        for n in range(0, width, step):
            mix_s[:, n:n + step] = jnp.transpose(mix_t[n:n + step, :])
        get_o.wait()
        for n in range(0, width, step):
            sum_s[:, n:n + step] = nn(mix_s[...], wo_s[:, n:n + step])

        block = 64

        for i in range(2 * rows // block):
            at = pl.ds(i * block, block)
            summed = x_s[at, :].astype(F32) + sum_s[at, :] + biases[0, 2:3, :]
            center = summed - jnp.mean(summed, axis=1, keepdims=True)
            scale = lax.rsqrt(jnp.mean(center * center, axis=1, keepdims=True) + LN_EPS)
            xhat = center * scale
            normed = xhat * gains[0, 0:1, :] + biases[0, 4:5, :]
            xh_s[0, at, :] = xhat.astype(BF16)
            rs_s[0, at, :] = jnp.broadcast_to(scale, (block, 128))
            nl_s[at, :] = normed.astype(BF16)
            sum_s[at, :] = normed + biases[0, 3:4, :]
        cp.out(xh_s.at[0], r["xhat"].at[0])
        cp.out(rs_s.at[0], r["scale"].at[0])
        for s in range(2):
            cp.out(nl_s.at[pl.ds(s * rows, rows)], r["w_nl"].at[wrows[s]])
        get_u.wait()
        chunk = 512

        for j in range(hidden // chunk):
            at = pl.ds(j * chunk, chunk)
            pre = nn(nl_s[...], wu_s[:, at]) + r["up_bias"][0:1, at]
            act, slope = gelu_and_slope(pre)
            act_s[:, at] = act.astype(BF16)
            gp_s[:, at] = slope.astype(BF16)
            cp.out(gp_s.at[:, at], r["gp"].at[:, at])
            for s in range(2):
                cp.out(act_s.at[pl.ds(s * rows, rows), at], r["w_act"].at[wrows[s], at])
        get_d.wait()
        for n in range(0, width, step):
            sum_s[:, n:n + step] += nn(act_s[...], wd_s[:, n:n + step])

        for i in range(2 * rows // block):
            at = pl.ds(i * block, block)
            total = sum_s[at, :]
            center = total - jnp.mean(total, axis=1, keepdims=True)
            scale = lax.rsqrt(jnp.mean(center * center, axis=1, keepdims=True) + LN_EPS)
            xhat = center * scale
            xh_s[1, at, :] = xhat.astype(BF16)
            rs_s[1, at, :] = jnp.broadcast_to(scale, (block, 128))
            out_s[at, :] = (xhat * gains[0, 1:2, :] + biases[0, 5:6, :]).astype(BF16)
        for s in range(2):
            cp.out(out_s.at[pl.ds(s * rows, rows)], r["out"].at[s])
        cp.out(xh_s.at[1], r["xhat"].at[1])
        cp.out(rs_s.at[1], r["scale"].at[1])
        cp.finish()


def bwd_kernel(m, names_in, names_out, *refs):
    r = dict(zip(names_in, refs))
    refs = refs[len(names_in):]
    r.update(zip(names_out, refs))
    (g_s, wp_s, wo_s, wu_s, wd_s, q_t, k_s, k_t, v_s, e_s, inv_s, gp_s, xh_s, rs_s,
     grad_s, dz_s, dpre_s, acc_s, da_s, dm_t, dq_t, dk_t, dv_t, dq_s, dk_s, dv_s, diag_s, small_s, upb_s, tab_s,
     out_s, sems) = refs[len(names_out):]
    rows = g_s.shape[0] // 2
    width = g_s.shape[1]
    heads = r["rel_table"].shape[1] // BUCKETS
    depth = width // heads
    hidden = wu_s.shape[1]
    span = 2 * rows

    @pl.when(r["active"][0] == 1)
    def _():
        cp = Copies(sems)
        if r["gc"].shape[0] == rows:
            gc, gq = r["gc"], r["gq"]
        else:
            gc, gq = r["gc"].at[pl.ds(m * rows, rows)], r["gq"].at[pl.ds(m * rows, rows)]
        wrows = [pl.ds(s * 2 * rows + m * rows, rows) for s in range(2)]
        get_g = [cp.start(gc, g_s.at[pl.ds(0, rows)]), cp.start(gq, g_s.at[pl.ds(rows, rows)])]
        get_g += [cp.start(r["xhat"], xh_s), cp.start(r["scale"], rs_s)]
        get_d = cp.start(r["down_weight"].at[0], wd_s)
        get_gp = cp.start(r["gp"], gp_s)
        get_u = cp.start(r["up_weight"].at[0], wu_s)
        get_o = cp.start(r["out_weight"].at[0], wo_s)
        get_a = [cp.start(r["inv"], inv_s)]
        get_e = [cp.start(r["e"], e_s), cp.start(r["q_t"], q_t), cp.start(r["k"], k_s)]
        get_e += [cp.start(r["k_t"], k_t), cp.start(r["v"], v_s)]
        get_p = [cp.start(r["proj_weight"].at[0, i], wp_s.at[i]) for i in range(3)]
        gains = r["gains"]
        small_s[...] = jnp.zeros(small_s.shape, F32)
        step, block, chunk = 256, 64, 512

        def add_small(row, value):
            small_s[row:row + 1, :] += jnp.sum(value, axis=0, keepdims=True)

        for copy in get_g:
            copy.wait()

        for i in range(2 * rows // block):
            at = pl.ds(i * block, block)
            grad = g_s[at, :].astype(F32)
            xhat = xh_s[1, at, :].astype(F32)
            both = grad * xhat
            add_small(7, both)
            add_small(5, grad)
            scaled = grad * gains[0, 1:2, :]
            mean_a = jnp.mean(scaled, axis=1, keepdims=True)
            mean_b = jnp.mean(scaled * xhat, axis=1, keepdims=True)
            back = (scaled - mean_a - xhat * mean_b) * rs_s[1, at, 0:1]
            grad_s[at, :] = back
            low = back.astype(BF16)
            dz_s[at, :] = low
            add_small(3, low.astype(F32))
        for s in range(2):
            cp.out(dz_s.at[pl.ds(s * rows, rows)], r["w_dz"].at[wrows[s]])
        get_d.wait()
        get_gp.wait()

        for j in range(hidden // chunk):
            at = pl.ds(j * chunk, chunk)
            d_act = nt(dz_s[...], wd_s[at, :])
            d_pre = (d_act * gp_s[:, at].astype(F32)).astype(BF16)
            dpre_s[:, at] = d_pre
            for s in range(2):
                cp.out(dpre_s.at[pl.ds(s * rows, rows), at], r["w_dpre"].at[wrows[s], at])
            upb_s[0:1, at] = jnp.sum(d_pre.astype(F32), axis=0, keepdims=True)
        get_u.wait()
        for n in range(0, width, step):
            acc_s[:, n:n + step] = nt(dpre_s[...], wu_s[n:n + step, :])

        for i in range(2 * rows // block):
            at = pl.ds(i * block, block)
            grad = grad_s[at, :] + acc_s[at, :]
            xhat = xh_s[0, at, :].astype(F32)
            add_small(6, grad * xhat)
            add_small(4, grad)
            scaled = grad * gains[0, 0:1, :]
            mean_a = jnp.mean(scaled, axis=1, keepdims=True)
            mean_b = jnp.mean(scaled * xhat, axis=1, keepdims=True)
            back = (scaled - mean_a - xhat * mean_b) * rs_s[0, at, 0:1]
            grad_s[at, :] = back
            low = back.astype(BF16)
            da_s[at, :] = low
            add_small(2, low.astype(F32))
        for s in range(2):
            cp.out(da_s.at[pl.ds(s * rows, rows)], r["w_da"].at[wrows[s]])
        get_o.wait()
        for copy in get_a:
            copy.wait()
        for n in range(0, width, step):
            d_mix = nt(wo_s[n:n + step, :], da_s[...])
            for h in range(n // depth, (n + step) // depth):
                part = d_mix[h * depth - n:(h + 1) * depth - n, :]
                inv = jnp.concatenate([inv_s[s, h:h + 1, :] for s in range(2)], axis=1)
                dm_t[h * depth:(h + 1) * depth, :] = (part * inv).astype(BF16)
        for copy in get_e:
            copy.wait()
        blank = jnp.zeros((depth, 2 * rows), BF16)
        diag_s[...] = jnp.zeros(diag_s.shape, F32)

        for pair in range(heads // 2):
            base = pair * 2 * depth
            v_pair = v_s[:, pl.ds(base, 2 * depth)]
            for half in range(2):
                head = 2 * pair + half
                at = pl.ds(base + half * depth, depth)
                dm_head = dm_t[at, :]
                stacked = jnp.concatenate([dm_head, blank] if half == 0 else [blank, dm_head], axis=0)
                d_prob = nn(v_pair, stacked)
                parts, whole = [], 0.0
                for s in range(2):
                    e = e_s[s, head].astype(F32)
                    part = d_prob[:, s * rows:(s + 1) * rows]
                    mean = jnp.sum(e * part, axis=0, keepdims=True) * inv_s[s, pl.ds(head, 1), :]
                    d_score = (e * (part - mean)).astype(BF16)
                    parts.append(d_score)
                    whole = whole + d_score.astype(F32)
                both = jnp.concatenate(parts, axis=1)
                e_both = jnp.concatenate([e_s[0, head], e_s[1, head]], axis=1)
                dq_t[at, :] = (nn(k_t[at, :], both) * 0.125).astype(BF16)
                dv_t[at, :] = nt(dm_head, e_both).astype(BF16)
                dk_t[at, :] = nt(q_t[at, :], both).astype(BF16)
                wide = jnp.concatenate([jnp.zeros_like(whole), whole], axis=1)
                count = rows
                while count > 8:
                    count //= 2
                    wide = wide[:count, :] + pltpu.roll(wide[count:, :], span - count, 1)
                line = wide[0:1, :]
                for k in range(1, 8):
                    line = line + pltpu.roll(wide, span - k, 1)[k:k + 1, :]
                diag_s[pl.ds(head, 1), :] = line
        for n in range(0, width, step):
            part = jnp.transpose(dq_t[n:n + step, :])
            dq_s[:, n:n + step] = part
            small_s[0:1, n:n + step] = jnp.sum(part.astype(F32), axis=0, keepdims=True)
            dk_s[:, n:n + step] = jnp.transpose(dk_t[n:n + step, :])
            part = jnp.transpose(dv_t[n:n + step, :])
            dv_s[:, n:n + step] = part
            small_s[1:2, n:n + step] = jnp.sum(part.astype(F32), axis=0, keepdims=True)
        for s in range(2):
            cp.out(dq_s.at[pl.ds(s * rows, rows)], r["w_dq"].at[wrows[s]])
        cp.out(dk_s, r["w_dk"].at[pl.ds(m * rows, rows)])
        cp.out(dv_s, r["w_dv"].at[pl.ds(m * rows, rows)])
        for copy in get_p:
            copy.wait()
        for n in range(0, width, step):
            back = grad_s[:, n:n + step] + nt(dq_s[...], wp_s[0, n:n + step, :])
            more = nt(dk_s[...], wp_s[1, n:n + step, :]) + nt(dv_s[...], wp_s[2, n:n + step, :])
            out_s[0:rows, n:n + step] = (back[0:rows, :] + more).astype(BF16)
            out_s[rows:, n:n + step] = back[rows:, :].astype(BF16)
        for s in range(2):
            cp.out(out_s.at[pl.ds(s * rows, rows)], r["grad"].at[s])

        own_head, own_bucket = head_map(heads * BUCKETS, heads, span)
        folded = lax.dot_general(
            diag_s[...],
            jnp.where(own_bucket, 1.0, 0.0),
            (((1,), (1,)), ((), ())),
            precision=lax.Precision.HIGHEST,
            preferred_element_type=F32,
        )
        tab_s[...] = jnp.broadcast_to(
            jnp.sum(jnp.where(own_head, folded, 0.0), axis=0, keepdims=True), tab_s.shape
        )
        cp.out(small_s, r["small"])
        cp.out(upb_s, r["up_small"])
        cp.out(tab_s, r["tab_small"])
        cp.finish()


SMEM = pl.BlockSpec(memory_space=pltpu.SMEM)
VMEM = pl.BlockSpec(memory_space=pltpu.VMEM)
ANY = pl.BlockSpec(memory_space=pl.ANY)


def call(kernel, m, operands, buffers, made, scratch, flops, copies):
    names_in = list(operands) + ["old_" + name for name in buffers]
    names_out = list(buffers) + list(made)
    shapes = [jax.ShapeDtypeStruct(a.shape, a.dtype) for a in buffers.values()] + list(made.values())
    outs = pl.pallas_call(
        partial(kernel, m, names_in, names_out),
        in_specs=[spec for _, spec in operands.values()] + [ANY] * len(buffers),
        out_specs=[ANY] * len(names_out),
        out_shape=shapes,
        scratch_shapes=scratch + [pltpu.SemaphoreType.DMA((copies,))],
        input_output_aliases={len(operands) + i: i for i in range(len(buffers))},
        compiler_params=pltpu.CompilerParams(vmem_limit_bytes=VMEM_LIMIT),
        cost_estimate=pl.CostEstimate(flops=flops, bytes_accessed=30_000_000, transcendentals=0),
    )(*[a for a, _ in operands.values()], *buffers.values())
    return dict(zip(names_out, outs))


def shape(*dims, dtype=BF16):
    return jax.ShapeDtypeStruct(dims, dtype)


def forward_shapes(rows, width, hidden, heads):
    return {
        "q_t": shape(width, 2 * rows),
        "k": shape(rows, width),
        "k_t": shape(width, rows),
        "v": shape(rows, width),
        "e": shape(2, heads, rows, rows),
        "inv": shape(2, 16, rows, dtype=F32),
        "gp": shape(2 * rows, hidden),
        "xhat": shape(2, 2 * rows, width),
        "scale": shape(2, 2 * rows, 128, dtype=F32),
        "out": shape(2, rows, width),
    }


def forward(m, active, xc, xq, fixed, weights, kept, store):
    rows, width, hidden, heads, micro = fixed["dims"]
    operands = {
        "active": (active, SMEM),
        "lengths": (fixed["lengths"], SMEM),
        "order": (fixed["order"], VMEM),
        "predicted": (fixed["predicted"], VMEM),
        "rel_table": (weights["rel_table"], VMEM),
        "up_bias": (weights["up_bias"], VMEM),
        "biases": (weights["biases"], VMEM),
        "gains": (weights["gains"], VMEM),
        "proj_weight": (weights["proj_weight"], ANY),
        "out_weight": (weights["out_weight"], ANY),
        "up_weight": (weights["up_weight"], ANY),
        "down_weight": (weights["down_weight"], ANY),
        "xc": (xc, ANY),
        "xq": (xq, ANY),
    }
    wide = 2 * rows * micro
    made = {}
    if kept is None:
        made.update(forward_shapes(rows, width, hidden, heads))
    if store is None:
        made.update(
            w_x=shape(wide, width), w_mix_t=shape(width, wide), w_nl=shape(wide, width), w_act=shape(wide, hidden)
        )
    both = 2 * rows
    scratch = [
        pltpu.VMEM((both, width), BF16),
        pltpu.VMEM((3, width, width), BF16),
        pltpu.VMEM((width, width), BF16),
        pltpu.VMEM((width, hidden), BF16),
        pltpu.VMEM((hidden, width), BF16),
        pltpu.VMEM((width, both), BF16),
        pltpu.VMEM((rows, width), BF16),
        pltpu.VMEM((width, rows), BF16),
        pltpu.VMEM((rows, width), BF16),
        pltpu.VMEM((width, rows), BF16),
        pltpu.VMEM((2, rows, rows), F32),
        pltpu.VMEM((16, 2 * rows), F32),
        pltpu.VMEM((2, heads, rows, rows), BF16),
        pltpu.VMEM((2, 16, rows), F32),
        pltpu.VMEM((width, both), BF16),
        pltpu.VMEM((both, width), BF16),
        pltpu.VMEM((both, width), F32),
        pltpu.VMEM((both, width), BF16),
        pltpu.VMEM((both, hidden), BF16),
        pltpu.VMEM((both, hidden), BF16),
        pltpu.VMEM((2, both, width), BF16),
        pltpu.VMEM((2, both, 128), F32),
        pltpu.VMEM((both, width), BF16),
    ]
    buffers = {**(kept or {}), **(store or {})}
    outs = call(fwd_kernel, m, operands, buffers, made, scratch, 8_000_000_000, 60)
    return (
        {n: v for n, v in outs.items() if not n.startswith("w_")},
        {n: v for n, v in outs.items() if n.startswith("w_")},
    )


def backward(m, active, gc, gq, fixed, weights, kept, store, back, made_back):
    rows, width, hidden, heads, micro = fixed["dims"]
    operands = {
        "active": (active, SMEM),
        "rel_table": (weights["rel_table"], VMEM),
        "gains": (weights["gains"], VMEM),
        "proj_weight": (weights["proj_weight"], ANY),
        "out_weight": (weights["out_weight"], ANY),
        "up_weight": (weights["up_weight"], ANY),
        "down_weight": (weights["down_weight"], ANY),
        "gc": (gc, ANY),
        "gq": (gq, ANY),
    }
    for name in ("q_t", "k", "k_t", "v", "e", "inv", "gp", "xhat", "scale"):
        operands[name] = (kept[name], ANY)
    wide = 2 * rows * micro
    both = 2 * rows
    made = {}
    if back is None:
        made.update(
            w_dz=shape(wide, width),
            w_dpre=shape(wide, hidden),
            w_da=shape(wide, width),
            w_dq=shape(wide, width),
            w_dk=shape(wide // 2, width),
            w_dv=shape(wide // 2, width),
        )
    if made_back is None:
        made.update(
            grad=shape(2, rows, width),
            small=shape(8, width, dtype=F32),
            up_small=shape(8, hidden, dtype=F32),
            tab_small=shape(8, heads * BUCKETS, dtype=F32),
        )
    scratch = [
        pltpu.VMEM((both, width), BF16),
        pltpu.VMEM((3, width, width), BF16),
        pltpu.VMEM((width, width), BF16),
        pltpu.VMEM((width, hidden), BF16),
        pltpu.VMEM((hidden, width), BF16),
        pltpu.VMEM((width, both), BF16),
        pltpu.VMEM((rows, width), BF16),
        pltpu.VMEM((width, rows), BF16),
        pltpu.VMEM((rows, width), BF16),
        pltpu.VMEM((2, heads, rows, rows), BF16),
        pltpu.VMEM((2, 16, rows), F32),
        pltpu.VMEM((both, hidden), BF16),
        pltpu.VMEM((2, both, width), BF16),
        pltpu.VMEM((2, both, 128), F32),
        pltpu.VMEM((both, width), F32),
        pltpu.VMEM((both, width), BF16),
        pltpu.VMEM((both, hidden), BF16),
        pltpu.VMEM((both, width), F32),
        pltpu.VMEM((both, width), BF16),
        pltpu.VMEM((width, both), BF16),
        pltpu.VMEM((width, both), BF16),
        pltpu.VMEM((width, rows), BF16),
        pltpu.VMEM((width, rows), BF16),
        pltpu.VMEM((both, width), BF16),
        pltpu.VMEM((rows, width), BF16),
        pltpu.VMEM((rows, width), BF16),
        pltpu.VMEM((16, both), F32),
        pltpu.VMEM((8, width), F32),
        pltpu.VMEM((8, hidden), F32),
        pltpu.VMEM((8, heads * BUCKETS), F32),
        pltpu.VMEM((both, width), BF16),
    ]
    buffers = {**(back or {}), **(made_back or {})}
    outs = call(bwd_kernel, m, operands, buffers, made, scratch, 8_000_000_000, 60)
    return (
        {n: v for n, v in outs.items() if n.startswith("w_")},
        {n: v for n, v in outs.items() if not n.startswith("w_")},
    )


def contract_rows(left, right):
    return jnp.einsum("ra,rb->ab", left, right, preferred_element_type=F32)


def exchange_stages(count):
    sizes = []
    while count > 1:
        sizes.append(2 if count % 2 == 0 else count)
        count //= sizes[-1]
    return sizes


def sum_scattered(arrays, axis):
    count = lax.axis_size(axis)
    index = lax.axis_index(axis)
    sizes = exchange_stages(count)
    arrays = [array.reshape(tuple(sizes[::-1]) + array.shape[1:]) for array in arrays]
    stride = 1
    for level, size in enumerate(sizes):
        dim = len(sizes) - 1 - level
        place = (index // stride) % size
        results = []
        for array in arrays:
            take = lambda at: lax.dynamic_index_in_dim(array, at, dim, keepdims=False)
            total = take(place).astype(F32)
            for step in range(1, size):
                route = []
                for device in range(count):
                    old = (device // stride) % size
                    route.append((device, device + ((old + step) % size - old) * stride))
                total = total + lax.ppermute(take((place + step) % size), axis, route).astype(F32)
            results.append(total if level == len(sizes) - 1 else total.astype(BF16))
        arrays = results
        stride *= size
    return arrays


def body(
    content_in,
    query_in,
    content_cot,
    query_cot,
    lengths,
    order,
    predicted,
    proj_weight,
    out_weight,
    up_weight,
    down_weight,
    up_bias,
    biases,
    gains,
    rel_table,
):
    micro, rows, width = content_in.shape
    hidden = up_bias.shape[1]
    heads = rel_table.shape[1] // BUCKETS
    first = (lax.axis_index("section") == 0).astype(jnp.int32).reshape(1)
    second = 1 - first
    weights = dict(
        proj_weight=proj_weight,
        out_weight=out_weight,
        up_weight=up_weight,
        down_weight=down_weight,
        up_bias=up_bias,
        biases=biases,
        gains=gains,
        rel_table=rel_table,
    )
    fixed = dict(lengths=lengths, order=order, predicted=predicted, dims=(rows, width, hidden, heads, micro))
    flat = lambda a: a.reshape(micro * rows, width)
    ahead, behind = [(0, 1)], [(1, 0)]
    kept, store, arrived = [None] * micro, None, [None] * micro
    for m in range(micro):
        kept[m], store = forward(m, first, flat(content_in), flat(query_in), fixed, weights, None, store)
        arrived[m] = lax.ppermute(kept[m]["out"], "section", ahead)
    back, made, returned = None, [None] * micro, [None] * micro
    for m in range(micro):
        kept[m], store = forward(m, second, arrived[m][0], arrived[m][1], fixed, weights, kept[m], store)
        back, made[m] = backward(
            m, second, flat(content_cot), flat(query_cot), fixed, weights, kept[m], store, back, None
        )
        returned[m] = lax.ppermute(made[m]["grad"], "section", behind)
    for m in range(micro):
        back, made[m] = backward(
            m, first, returned[m][0], returned[m][1], fixed, weights, kept[m], store, back, made[m]
        )
    half = micro * rows
    small = sum(part["small"] for part in made)
    up_small = sum(part["up_small"] for part in made)[0]
    tab_small = sum(part["tab_small"] for part in made)[0]
    count = lax.axis_size("dp")
    strip = lambda array: array.astype(BF16).reshape(count, -1, array.shape[-1])
    down_grad = strip(contract_rows(store["w_act"], back["w_dz"]))
    up_grad = strip(contract_rows(store["w_nl"], back["w_dpre"]))
    own = width // count
    extras = jnp.concatenate(
        [
            small.reshape(8, count, own).transpose(1, 0, 2).reshape(count, 8 * own),
            up_small.reshape(count, hidden // count),
            tab_small.reshape(count, heads * BUCKETS // count),
        ],
        axis=1,
    ).astype(BF16)
    extra_count = extras.shape[1]
    extras = jnp.pad(extras, ((0, 0), (0, width - extra_count)))[:, None]
    attention_grad = jnp.concatenate(
        [
            strip(contract_rows(store["w_x"], back["w_dq"])),
            strip(contract_rows(store["w_x"][:half], back["w_dk"])),
            strip(contract_rows(store["w_x"][:half], back["w_dv"])),
            strip(jnp.dot(store["w_mix_t"], back["w_da"], preferred_element_type=F32)),
            jnp.pad(extras, ((0, 0), (0, 15), (0, 0))),
        ],
        axis=1,
    )
    down_grad, up_grad, attention_grad = sum_scattered([down_grad, up_grad, attention_grad], "dp")
    proj_grad = attention_grad[: 3 * own].reshape(1, 3, own, width)
    out_grad = attention_grad[3 * own : 4 * own][None]
    extras = attention_grad[4 * own]
    small = extras[: 8 * own].reshape(1, 8, own)
    up_small = extras[8 * own : 8 * own + hidden // count][None]
    tab_small = extras[8 * own + hidden // count : extra_count][None]
    stack = lambda name, parts, s: jnp.stack([part[name][s] for part in parts])[None]
    return (
        stack("out", kept, 0),
        stack("out", kept, 1),
        stack("grad", made, 0),
        stack("grad", made, 1),
        proj_grad,
        out_grad,
        up_grad[None],
        down_grad[None],
        up_small,
        small[:, 0:6],
        small[:, 6:8],
        tab_small,
    )


def solution(mesh):
    return jax.shard_map(
        body,
        mesh=mesh,
        in_specs=(
            P(None, "dp", None),
            P(None, "dp", None),
            P(None, "dp", None),
            P(None, "dp", None),
            P(None, "dp", None),
            P(None, "dp"),
            P(None, "dp"),
            P("section", None, None, None),
            P("section", None, None),
            P("section", None, None),
            P("section", None, None),
            P("section", None),
            P("section", None, None),
            P("section", None, None),
            P("section", None),
        ),
        out_specs=(
            P("section", None, "dp", None),
            P("section", None, "dp", None),
            P("section", None, "dp", None),
            P("section", None, "dp", None),
            P("section", None, "dp", None),
            P("section", "dp", None),
            P("section", "dp", None),
            P("section", "dp", None),
            P("section", "dp"),
            P("section", None, "dp"),
            P("section", None, "dp"),
            P("section", "dp"),
        ),
        check_vma=False,
    )
```

```python
from functools import partial

import jax
import jax.numpy as jnp
from jax import lax
from jax.experimental import pallas as pl
from jax.experimental.pallas import tpu as pltpu
from jax.sharding import PartitionSpec as P

LN_EPS = 1e-05
NEG_FILL = -1e30
BUCKET_EDGES = (12, 16, 23, 32, 46, 64, 91)
BUCKETS = 32
F32, BF16 = jnp.float32, jnp.bfloat16
VMEM_LIMIT = 60 * 1024 * 1024
TAIL = (0.127414796, -0.142248368, 0.7107068705, -0.7265760135, 0.5307027145)
TAIL_SLOPE = 0.3275911 / 2**0.5
DENSITY = 0.3989422804014327


def nn(left, right):
    return jnp.dot(left, right, preferred_element_type=F32)


def nt(left, right):
    return lax.dot_general(left, right, (((1,), (1,)), ((), ())), preferred_element_type=F32)


def iota(shape, dim):
    return lax.broadcasted_iota(jnp.int32, shape, dim)


def bucket_index(relative):
    magnitude = jnp.abs(relative)
    far_part = jnp.full_like(magnitude, 8)
    for edge_at in BUCKET_EDGES:
        far_part = far_part + jnp.where(magnitude >= edge_at, 1, 0)
    near_far = jnp.where(magnitude < 8, magnitude, far_part)
    return near_far + jnp.where(relative > 0, 16, 0)


def gelu_and_slope(v):
    z = jnp.abs(v)
    t = 1.0 / (1.0 + TAIL_SLOPE * z)
    poly = TAIL[4]
    for coefficient in TAIL[3::-1]:
        poly = coefficient + t * poly
    bell = jnp.exp(-0.5 * (v * v))
    tail = t * poly * bell
    below = jnp.where(v >= 0, 1.0 - tail, tail)
    return v * below, below + DENSITY * (v * bell)


class Copies:
    def __init__(self, sems):
        self.sems, self.used, self.open = sems, 0, []

    def copy(self, src, dst, at):
        return pltpu.make_async_copy(src, dst, self.sems.at[at])

    def start(self, src, dst):
        copy = self.copy(src, dst, self.used)
        self.used += 1
        copy.start()
        return copy

    def out(self, src, dst):
        self.open.append((src, dst, self.used))
        self.start(src, dst)

    def finish(self):
        for src, dst, at in self.open:
            self.copy(src, dst, at).wait()


def head_map(entries, heads, span):
    entry = iota((16, entries), 1)
    own_head = (entry - heads * ((entry * 5462) >> 16)) == iota((16, entries), 0)
    bucket = bucket_index(span // 2 - iota((entries, span), 1))
    row = iota((entries, span), 0)
    own_bucket = (row >= heads * bucket) & (row < heads * bucket + heads)
    return own_head, own_bucket


def make_masks(lengths, order_ref, predicted_ref, m, rows):
    def place(shape, dim):
        token = iota(shape, dim)
        segment, start, end = jnp.zeros(shape, jnp.int32), jnp.zeros(shape, jnp.int32), 0
        for slot in range(lengths.shape[2]):
            size = lengths[m, 0, slot]
            end = end + size
            passed = token >= end
            segment = segment + jnp.where(passed, 1, 0)
            start = start + jnp.where(passed, size, 0)
        inside = token < end
        return jnp.where(inside, segment, -1 - token), inside & (token - start > 0)

    segment, later = place((1, rows), 1)
    order = order_ref[pl.ds(m, 1), :]
    flag = (predicted_ref[pl.ds(m, 1), :] > 0) & later
    gate = jnp.where(flag, order, -1).astype(F32)
    gate_column = jnp.transpose(jnp.broadcast_to(gate, (128, rows)))
    segment_column = jnp.transpose(jnp.broadcast_to(segment.astype(F32), (128, rows)))
    gate_column = jnp.concatenate([gate_column] * (rows // 128), axis=1)
    segment_column = jnp.concatenate([segment_column] * (rows // 128), axis=1)
    same = segment_column == segment.astype(F32)
    order = order.astype(F32)
    return [
        jnp.where(same & (gate_column <= order), 0.0, NEG_FILL),
        jnp.where(same & (gate_column < order), 0.0, NEG_FILL),
    ]


def tn(left, right):
    return lax.dot_general(left, right, (((0,), (0,)), ((), ())), preferred_element_type=F32)


UNROLL_HEADS = 12
UNROLL_CHUNKS = 6
UNROLL_BLOCKS = 8
STEP = 256
CHUNK = 512
BLOCK = 64


MATRIX = dict(wp="proj_weight", wo="out_weight", wu="up_weight", wd="down_weight")


def loop(count, unroll, body):
    def turn(i, carry):
        for j in range(unroll):
            body(i * unroll + j)
        return carry

    if unroll == count:
        for i in range(count):
            body(i)
    else:
        lax.fori_loop(0, count // unroll, turn, 0)


def loop_heads(heads, body):
    def turn(i, carry):
        for j in range(UNROLL_HEADS):
            body(i * UNROLL_HEADS + j, j % 2)
        return carry

    if UNROLL_HEADS == heads:
        turn(0, 0)
    else:
        lax.fori_loop(0, heads // UNROLL_HEADS, turn, 0)


def span_of(i, size):
    return pl.ds(i * size if isinstance(i, int) else pl.multiple_of(i * size, size), size)


class Layer:
    def __init__(self, m, dims, r, s, cp, parts):
        self.m, self.r, self.s, self.cp, self.parts = m, r, s, cp, parts
        self.rows, self.width, self.hidden, self.heads, self.micro, self.count = dims
        self.depth = self.width // self.heads
        self.span = 2 * self.rows
        self.mine = pl.ds(m * 2 * self.rows, 2 * self.rows)
        self.mine_half = pl.ds(m * self.rows, self.rows)
        self.waits, self.later = {}, False

    def load(self, name, src, dst):
        self.waits[name] = (src, dst, self.cp.used)
        self.cp.used += 1
        if not self.later:
            self.begin(name)

    def begin(self, *names):
        for name in names or self.waits:
            self.cp.copy(*self.waits[name]).start()

    def need(self, *names):
        for name in names:
            if name in self.waits:
                self.cp.copy(*self.waits.pop(name)).wait()

    def load_weights(self, *names):
        r, s = self.r, self.s
        for name in names:
            self.load(name, r[MATRIX[name]].at[0], s[name])

    def load_streams(self, name, content, query):
        rows, dst = self.rows, self.s[name]
        if content.shape[0] != rows:
            content, query = content.at[self.mine_half], query.at[self.mine_half]
        self.load(name + "0", content, dst.at[pl.ds(0, rows)])
        self.load(name + "1", query, dst.at[pl.ds(rows, rows)])

    def forward(self):
        r, s, cp = self.r, self.s, self.cp
        rows, width, heads, depth, span = self.rows, self.width, self.heads, self.depth, self.span
        keep = "back" not in self.parts
        biases, gains = r["biases"], r["gains"]
        s["mask"][0], s["mask"][1] = make_masks(r["lengths"], r["order"], r["predicted"], self.m, rows)
        own_head, own_bucket = head_map(heads * BUCKETS, heads, span)
        picked = jnp.where(own_head, r["rel_table"][...], 0.0)
        s["toep"][...] = jnp.dot(
            picked, jnp.where(own_bucket, 1.0, 0.0), precision=lax.Precision.HIGHEST, preferred_element_type=F32
        )
        self.need("x0", "x1", "wp")
        cp.out(s["x"], r["w_x"].at[self.mine])
        for n in range(0, width, STEP):
            at = slice(n, n + STEP)
            q = nn(s["x"][...], s["wp"][0, :, at]) + biases[0, 0:1, at]
            s["q_t"][at, :] = jnp.transpose(q.astype(BF16) * 0.125)
        for n in range(0, width, STEP):
            at = slice(n, n + STEP)
            k = nn(s["x"][0:rows, :], s["wp"][1, :, at]).astype(BF16)
            s["k"][:, at] = k
            s["k_t"][at, :] = jnp.transpose(k)
            v = (nn(s["x"][0:rows, :], s["wp"][2, :, at]) + biases[0, 1:2, at]).astype(BF16)
            s["v"][:, at] = v
            s["v_t"][at, :] = jnp.transpose(v)
        blank = jnp.zeros((depth, 2 * rows), BF16)
        def head_step(head, odd):
            pair = span_of((head - odd) // 2, 2 * depth)
            at = span_of(head, depth)
            q_head = s["q_t"][at, :]
            stacked = jnp.concatenate([blank, q_head] if odd else [q_head, blank], axis=0)
            scores = nn(s["k"][:, pair], stacked)
            line = jnp.broadcast_to(s["toep"][pl.ds(head, 1), :], (rows, span))
            rel = pltpu.roll(line, rows, 1, stride=1, stride_axis=0)[:, :rows]
            for i in range(2):
                lanes = slice(i * rows, (i + 1) * rows)
                logits = scores[:, lanes] + rel + s["mask"][i]
                e = jnp.exp(logits - jnp.max(logits, axis=0, keepdims=True))
                inv = 1.0 / jnp.sum(e, axis=0, keepdims=True)
                e = e.astype(BF16)
                s["e"][i, head] = e
                s["inv"][i, pl.ds(head, 1), :] = inv
                s["mix_t"][at, lanes] = (nn(s["v_t"][at, :], e) * inv).astype(BF16)
        loop_heads(heads, head_step)
        if keep:
            for name in ("q_t", "k", "k_t", "v", "e", "inv"):
                cp.out(s[name], r[name])
        cp.out(s["mix_t"], r["w_mix_t"].at[:, self.mine])
        for n in range(0, width, STEP):
            s["mix"][:, n:n + STEP] = jnp.transpose(s["mix_t"][n:n + STEP, :])
        self.need("wo", "wu", "wd")
        for n in range(0, width, STEP):
            s["sum"][:, n:n + STEP] = nn(s["mix"][...], s["wo"][:, n:n + STEP])
        def block_step(n):
            at = span_of(n, BLOCK)
            summed = s["x"][at, :].astype(F32) + s["sum"][at, :] + biases[0, 2:3, :]
            center = summed - jnp.mean(summed, axis=1, keepdims=True)
            scale = lax.rsqrt(jnp.mean(center * center, axis=1, keepdims=True) + LN_EPS)
            xhat = center * scale
            normed = xhat * gains[0, 0:1, :] + biases[0, 4:5, :]
            s["xh"][0, at, :] = xhat.astype(BF16)
            s["rs"][0, at, :] = jnp.broadcast_to(scale, (BLOCK, 128))
            s["nl"][at, :] = normed.astype(BF16)
            s["sum"][at, :] = normed + biases[0, 3:4, :]
        loop(2 * self.rows // BLOCK, UNROLL_BLOCKS, block_step)
        if keep:
            cp.out(s["xh"].at[0], r["xhat"].at[0])
            cp.out(s["rs"].at[0], r["scale"].at[0])
        cp.out(s["nl"], r["w_nl"].at[self.mine])
        def chunk_step(j):
            at = span_of(j, CHUNK)
            act, slope = gelu_and_slope(nn(s["nl"][...], s["wu"][:, at]) + r["up_bias"][0:1, at])
            s["act"][:, at] = act.astype(BF16)
            s["gp"][:, at] = slope.astype(BF16)
        loop(self.hidden // CHUNK, UNROLL_CHUNKS, chunk_step)
        cp.out(s["act"], r["w_act"].at[self.mine])
        if keep:
            cp.out(s["gp"], r["gp"])
        for n in range(0, width, STEP):
            s["sum"][:, n:n + STEP] += nn(s["act"][...], s["wd"][:, n:n + STEP])
        def block_step(n):
            at = span_of(n, BLOCK)
            total = s["sum"][at, :]
            center = total - jnp.mean(total, axis=1, keepdims=True)
            scale = lax.rsqrt(jnp.mean(center * center, axis=1, keepdims=True) + LN_EPS)
            xhat = center * scale
            s["xh"][1, at, :] = xhat.astype(BF16)
            s["rs"][1, at, :] = jnp.broadcast_to(scale, (BLOCK, 128))
            s["out"][at, :] = (xhat * gains[0, 1:2, :] + biases[0, 5:6, :]).astype(BF16)
        loop(2 * self.rows // BLOCK, UNROLL_BLOCKS, block_step)
        cp.out(s["out"], r["out"])
        if keep:
            cp.out(s["xh"].at[1], r["xhat"].at[1])
            cp.out(s["rs"].at[1], r["scale"].at[1])

    def norm_back(self, which, grad, at, gain_sum, shift_sum):
        s = self.s
        xhat = s["xh"][which, at, :].astype(F32)
        ref, row = gain_sum
        s[ref][row:row + 1, :] += jnp.sum(grad * xhat, axis=0, keepdims=True)
        ref, row = shift_sum
        s[ref][row:row + 1, :] += jnp.sum(grad, axis=0, keepdims=True)
        scaled = grad * self.r["gains"][0, which:which + 1, :]
        mean_a = jnp.mean(scaled, axis=1, keepdims=True)
        mean_b = jnp.mean(scaled * xhat, axis=1, keepdims=True)
        return (scaled - mean_a - xhat * mean_b) * s["rs"][which, at, 0:1]

    def back_norm_two(self, dz):
        s = self.s
        s["sm_a"][...] = jnp.zeros(s["sm_a"].shape, F32)
        self.need("g0", "g1", "xh1", "rs1")
        def block_step(n):
            at = span_of(n, BLOCK)
            back = self.norm_back(1, s["g"][at, :].astype(F32), at, ("sm_a", 2), ("sm_a", 1))
            s["grad"][at, :] = back
            low = back.astype(BF16)
            dz[at, :] = low
            s["sm_a"][0:1, :] += jnp.sum(low.astype(F32), axis=0, keepdims=True)
        loop(2 * self.rows // BLOCK, UNROLL_BLOCKS, block_step)
        self.cp.out(dz, self.r["w_dz"].at[self.mine])
        self.cp.out(s["sm_a"], self.r["sm_a"])

    def back_up(self, dz, dpre):
        s = self.s
        self.need("wd")
        self.need("gp")
        def chunk_step(j):
            at = span_of(j, CHUNK)
            d_act = nt(dz[...], s["wd"][at, :])
            d_pre = (d_act * s["gp"][:, at].astype(F32)).astype(BF16)
            dpre[:, at] = d_pre
            s["upb"][0:1, at] = jnp.sum(d_pre.astype(F32), axis=0, keepdims=True)
        loop(self.hidden // CHUNK, UNROLL_CHUNKS, chunk_step)
        self.cp.out(dpre, self.r["w_dpre"].at[self.mine])
        self.cp.out(s["upb"], self.r["upb"])

    def back_norm_one(self, dpre, da):
        s = self.s
        s["sm_b"][...] = jnp.zeros(s["sm_b"].shape, F32)
        self.need("wu")
        for n in range(0, self.width, STEP):
            s["sum"][:, n:n + STEP] = nt(dpre[...], s["wu"][n:n + STEP, :])
        self.need("xh0", "rs0", "grad")
        def block_step(n):
            at = span_of(n, BLOCK)
            back = self.norm_back(0, s["grad"][at, :] + s["sum"][at, :], at, ("sm_b", 4), ("sm_b", 3))
            s["grad"][at, :] = back
            low = back.astype(BF16)
            da[at, :] = low
            s["sm_b"][2:3, :] += jnp.sum(low.astype(F32), axis=0, keepdims=True)
        loop(2 * self.rows // BLOCK, UNROLL_BLOCKS, block_step)
        self.cp.out(da, self.r["w_da"].at[self.mine])

    def back_attention(self, da, dq, dk, dv):
        s, cp, r = self.s, self.cp, self.r
        rows, width, heads, depth, span = self.rows, self.width, self.heads, self.depth, self.span
        self.need("wo", "inv")
        for n in range(0, width, STEP):
            d_mix = nt(s["wo"][n:n + STEP, :], da[...])
            for h in range(n // depth, (n + STEP) // depth):
                inv = jnp.concatenate([s["inv"][i, h:h + 1, :] for i in range(2)], axis=1)
                s["dm_t"][h * depth:(h + 1) * depth, :] = (d_mix[h * depth - n:(h + 1) * depth - n, :] * inv).astype(BF16)
        self.need("e", "q_t", "k", "k_t", "v")
        blank = jnp.zeros((depth, 2 * rows), BF16)
        s["diag"][...] = jnp.zeros(s["diag"].shape, F32)
        def head_step(head, odd):
            pair = span_of((head - odd) // 2, 2 * depth)
            at = span_of(head, depth)
            dm_head = s["dm_t"][at, :]
            stacked = jnp.concatenate([blank, dm_head] if odd else [dm_head, blank], axis=0)
            d_prob = nn(s["v"][:, pair], stacked)
            parts, whole = [], 0.0
            for i in range(2):
                e = s["e"][i, head].astype(F32)
                part = d_prob[:, i * rows:(i + 1) * rows]
                mean = jnp.sum(e * part, axis=0, keepdims=True) * s["inv"][i, pl.ds(head, 1), :]
                d_score = (e * (part - mean)).astype(BF16)
                parts.append(d_score)
                whole = whole + d_score.astype(F32)
            both = jnp.concatenate(parts, axis=1)
            e_both = jnp.concatenate([s["e"][0, head], s["e"][1, head]], axis=1)
            s["dq_t"][at, :] = (nn(s["k_t"][at, :], both) * 0.125).astype(BF16)
            s["dv_t"][at, :] = nt(dm_head, e_both).astype(BF16)
            s["dk_t"][at, :] = nt(s["q_t"][at, :], both).astype(BF16)
            wide = jnp.concatenate([jnp.zeros_like(whole), whole], axis=1)
            count = rows
            while count > 8:
                count //= 2
                wide = wide[:count, :] + pltpu.roll(wide[count:, :], span - count, 1)
            line = wide[0:1, :]
            for k in range(1, 8):
                line = line + pltpu.roll(wide, span - k, 1)[k:k + 1, :]
            s["diag"][pl.ds(head, 1), :] = line
        loop_heads(heads, head_step)
        for n in range(0, width, STEP):
            at = slice(n, n + STEP)
            part = jnp.transpose(s["dq_t"][at, :])
            dq[:, at] = part
            s["sm_b"][0:1, at] = jnp.sum(part.astype(F32), axis=0, keepdims=True)
            dk[:, at] = jnp.transpose(s["dk_t"][at, :])
            part = jnp.transpose(s["dv_t"][at, :])
            dv[:, at] = part
            s["sm_b"][1:2, at] = jnp.sum(part.astype(F32), axis=0, keepdims=True)
        cp.out(dq, r["w_dq"].at[self.mine])
        cp.out(dk, r["w_dk"].at[self.mine_half])
        cp.out(dv, r["w_dv"].at[self.mine_half])
        cp.out(s["sm_b"], r["sm_b"])
        cp.out(s["diag"], r["diag"])

    def back_input(self, dq, dk, dv):
        s, rows = self.s, self.rows
        self.need("wp")
        for n in range(0, self.width, STEP):
            at = slice(n, n + STEP)
            back = s["grad"][:, at] + nt(dq[...], s["wp"][0, at, :])
            more = nt(dk[...], s["wp"][1, at, :]) + nt(dv[...], s["wp"][2, at, :])
            s["gout"][0:rows, at] = (back[0:rows, :] + more).astype(BF16)
            s["gout"][rows:, at] = back[rows:, :].astype(BF16)
        self.cp.out(s["gout"], self.r["grad"])


def run_forward(layer):
    layer.load_streams("x", layer.r["xc"], layer.r["xq"])
    layer.load_weights("wp", "wo", "wu", "wd")
    layer.forward()
    layer.cp.finish()


def run_backward(layer):
    r, s = layer.r, layer.s
    layer.load_streams("g", r["gc"], r["gq"])
    for i in (1, 0):
        layer.load(f"xh{i}", r["xhat"].at[i], s["xh"].at[i])
        layer.load(f"rs{i}", r["scale"].at[i], s["rs"].at[i])
    layer.load_weights("wd")
    layer.load("gp", r["gp"], s["gp"])
    layer.load_weights("wu", "wo")
    for name in ("inv", "e", "q_t", "k", "k_t", "v"):
        layer.load(name, r[name], s[name])
    layer.load_weights("wp")
    all_back(layer)
    layer.cp.finish()


def all_back(layer):
    s = layer.s
    layer.back_norm_two(s["dz"])
    layer.back_up(s["dz"], s["dpre"])
    layer.back_norm_one(s["dpre"], s["da"])
    layer.back_attention(s["da"], s["dq"], s["dk"], s["dv"])
    layer.back_input(s["dq"], s["dk"], s["dv"])


def run_both(layer):
    layer.load_streams("x", layer.r["xc"], layer.r["xq"])
    layer.load_weights("wp", "wo", "wu", "wd")
    layer.load_streams("g", layer.r["gc"], layer.r["gq"])
    layer.forward()
    all_back(layer)
    layer.cp.finish()


def step_order(name, count):
    straight = list(range(1, count.bit_length() - 1))
    return straight[1:] + straight[:1] if name in TURNED else straight


def part_at(name, device, count):
    at = 0
    for bit in step_order(name, count):
        at = 2 * at + (device >> bit & 1)
    return at


def emit(layer, name, first, columns, value):
    parts = layer.s["G_" + name]
    size = value.shape[0] // layer.count
    for device in range(layer.count):
        rows = value[device * size:(device + 1) * size, :].astype(BF16)
        parts[part_at(name, device, layer.count), device % 2, first:first + size, columns] = rows


TURNED = ("second",)
PIECES = dict(down=1, up=4, first=2, second=2)


def sent(*names):
    return tuple(f"s_{name}{i}" for name in names for i in range(PIECES[name])) + tuple("k_" + name for name in names)


def send_parts(layer, *names):
    core = layer.r["core"][0]
    for name in names:
        for i in range(PIECES[name]):
            columns = layer.r[f"s_{name}{i}"].shape[2]
            layer.cp.out(
                layer.s["G_" + name].at[:, 1 - core, :, pl.ds(i * columns, columns)], layer.r[f"s_{name}{i}"]
            )
    for name in names:
        layer.cp.out(layer.s["G_" + name].at[:, core], layer.r["k_" + name])


def tail_down(layer):
    r, s, cp = layer.r, layer.s, layer.cp
    active = r["active"][0] == 1
    other = pl.ds((1 - layer.m) * 2 * layer.rows, 2 * layer.rows)
    mine = s["W_dz"].at[layer.mine]

    layer.later = True
    layer.load_streams("g", r["gc"], r["gq"])
    layer.load("xh1", r["xhat"].at[1], s["xh"].at[1])
    layer.load("rs1", r["scale"].at[1], s["rs"].at[1])
    layer.later = False

    @pl.when(active)
    def _():
        layer.begin()

    layer.load("act", r["w_act"], s["W_act"])
    layer.load("other", r["w_dz"].at[other], s["W_dz"].at[other])

    @pl.when(active)
    def _():
        layer.back_norm_two(mine)
        cp.out(s["grad"], r["d_total"])

    opened, cp.open = cp.open, []

    @pl.when(jnp.logical_not(active))
    def _():
        cp.start(r["w_dz"].at[layer.mine], mine).wait()

    layer.need("act", "other")
    size = layer.hidden // layer.count
    for n in range(0, layer.hidden, 2 * size):
        both = tn(s["W_act"][:, n:n + 2 * size], s["W_dz"][...]).astype(BF16)
        at = part_at("down", n // size, layer.count)
        s["G_down"][at, 0] = both[:size]
        s["G_down"][at, 1] = both[size:]
    send_parts(layer, "down")

    @pl.when(active)
    def _():
        for src, dst, at in opened:
            cp.copy(src, dst, at).wait()

    cp.finish()


def tail_up(layer):
    r, s, cp = layer.r, layer.s, layer.cp
    active = r["active"][0] == 1
    other = pl.ds((1 - layer.m) * 2 * layer.rows, 2 * layer.rows)
    mine = s["W_dpre"].at[layer.mine]

    layer.later = True
    layer.load("dz", r["w_dz"].at[layer.mine], s["dz"])
    layer.load_weights("wd")
    layer.load("gp", r["gp"], s["gp"])
    layer.later = False

    @pl.when(active)
    def _():
        layer.begin()

    layer.load("nl", r["w_nl"], s["W_nl"])
    layer.load("other", r["w_dpre"].at[other], s["W_dpre"].at[other])

    @pl.when(active)
    def _():
        layer.need("dz")
        layer.back_up(s["dz"], mine)

    opened, cp.open = cp.open, []

    @pl.when(jnp.logical_not(active))
    def _():
        cp.start(r["w_dpre"].at[layer.mine], mine).wait()

    layer.need("nl", "other")
    for n in range(0, layer.width, STEP):
        at = slice(n, n + STEP)
        s["T_nl"][at, :] = jnp.transpose(s["W_nl"][:, at])
    for n in range(0, layer.hidden, CHUNK):
        emit(layer, "up", 0, slice(n, n + CHUNK), nn(s["T_nl"][...], s["W_dpre"][:, n:n + CHUNK]))
    send_parts(layer, "up")

    @pl.when(active)
    def _():
        for src, dst, at in opened:
            cp.copy(src, dst, at).wait()

    cp.finish()


def tail_norm(layer):
    r, s = layer.r, layer.s
    layer.load("dpre", r["w_dpre"].at[layer.mine], s["dpre"])
    layer.load_weights("wu")
    layer.load("grad", r["d_total"], s["grad"])
    layer.load("xh0", r["xhat"].at[0], s["xh"].at[0])
    layer.load("rs0", r["scale"].at[0], s["rs"].at[0])
    layer.need("dpre")
    layer.back_norm_one(s["dpre"], s["da"])
    layer.cp.out(s["grad"], r["d_summed"])
    layer.cp.out(s["sm_b"], r["sm_c"])
    layer.cp.finish()


def tail_attention(layer):
    r, s, cp = layer.r, layer.s, layer.cp
    rows = layer.rows
    active = r["active"][0] == 1
    other = pl.ds((1 - layer.m) * 2 * rows, 2 * rows)
    other_half = pl.ds((1 - layer.m) * rows, rows)
    places = (
        ("dq", layer.mine, other), ("dk", layer.mine_half, other_half), ("dv", layer.mine_half, other_half),
    )
    mine = {name: s["W_" + name].at[own] for name, own, _ in places}

    layer.load("da", r["w_da"], s["W_da"])
    layer.later = True
    layer.load_weights("wo")
    for name in ("inv", "e", "q_t", "k", "k_t", "v"):
        layer.load(name, r[name], s[name])
    layer.later = False

    @pl.when(active)
    def _():
        layer.begin("wo", "inv", "e", "q_t", "k", "k_t", "v")

    layer.load("x", r["w_x"], s["W_x"])
    layer.load("mix", r["w_mix_t"], s["W_mix_t"])
    for name, _, far in places:
        layer.load("other" + name, r["w_" + name].at[far], s["W_" + name].at[far])
    layer.need("da")

    @pl.when(active)
    def _():
        s["sm_b"][...] = jnp.zeros(s["sm_b"].shape, F32)
        layer.back_attention(s["W_da"].at[layer.mine], mine["dq"], mine["dk"], mine["dv"])

    opened, cp.open = cp.open, []

    @pl.when(jnp.logical_not(active))
    def _():
        copies = [cp.start(r["w_" + name].at[own], mine[name]) for name, own, _ in places]
        for copy in copies:
            copy.wait()

    layer.need("x", "mix", *["other" + name for name, _, _ in places])
    for n in range(0, layer.width, STEP):
        at = slice(n, n + STEP)
        s["T_x"][at, :] = jnp.transpose(s["W_x"][:, at])
    content = jnp.concatenate([s["T_x"][:, m * 2 * rows:(m * 2 + 1) * rows] for m in range(layer.micro)], axis=1)
    size = layer.width // layer.count
    for n in range(0, layer.width, STEP):
        at = slice(n, n + STEP)
        emit(layer, "first", 0, at, nn(s["T_x"][...], s["W_dq"][:, at]))
        emit(layer, "first", size, at, nn(content, s["W_dk"][:, at]))
        emit(layer, "second", 0, at, nn(content, s["W_dv"][:, at]))
        emit(layer, "second", size, at, nn(s["W_mix_t"][...], s["W_da"][:, at]))
    send_parts(layer, "first", "second")

    @pl.when(active)
    def _():
        for src, dst, at in opened:
            cp.copy(src, dst, at).wait()

    cp.finish()


def tail_input(layer):
    r, s = layer.r, layer.s
    layer.load_weights("wp")
    layer.load("grad", r["d_summed"], s["grad"])
    layer.load("dq", r["w_dq"].at[layer.mine], s["dq"])
    layer.load("dk", r["w_dk"].at[layer.mine_half], s["dk"])
    layer.load("dv", r["w_dv"].at[layer.mine_half], s["dv"])
    layer.need("grad", "dq", "dk", "dv")
    layer.back_input(s["dq"], s["dk"], s["dv"])
    layer.cp.finish()


def scratch_shapes(dims):
    rows, width, hidden, heads, micro, count = dims
    both, all_rows = 2 * rows, 2 * rows * micro
    low = {
        "x": (both, width), "wp": (3, width, width), "wo": (width, width), "wu": (width, hidden),
        "wd": (hidden, width), "q_t": (width, both), "k": (rows, width), "k_t": (width, rows),
        "v": (rows, width), "v_t": (width, rows), "e": (2, heads, rows, rows), "mix_t": (width, both),
        "mix": (both, width), "nl": (both, width), "act": (both, hidden), "gp": (both, hidden),
        "xh": (2, both, width), "out": (both, width), "g": (both, width), "dz": (both, width),
        "dpre": (both, hidden), "da": (both, width), "dm_t": (width, both), "dq_t": (width, both),
        "dk_t": (width, rows), "dv_t": (width, rows), "dq": (both, width), "dk": (rows, width),
        "dv": (rows, width), "gout": (both, width),
    }
    high = {
        "mask": (2, rows, rows), "toep": (16, both), "inv": (2, 16, rows), "sum": (both, width),
        "rs": (2, both, 128), "grad": (both, width), "sm_a": (8, width), "sm_b": (8, width),
        "upb": (8, hidden), "diag": (16, both),
    }
    low.update({"W_" + name[2:]: dims for name, dims in stored_shapes(dims).items()})
    low.update({"G_" + name: (count // 2, 2) + part for name, part in sum_shapes(dims).items()})
    low.update({"T_x": (width, all_rows), "T_nl": (width, all_rows)})
    shapes = {name: pltpu.VMEM(dims, BF16) for name, dims in low.items()}
    shapes.update({name: pltpu.VMEM(dims, F32) for name, dims in high.items()})
    return shapes


WEIGHTS = ("wp", "wo", "wu", "wd")
FORWARD = WEIGHTS + (
    "x", "q_t", "k", "k_t", "v", "v_t", "mask", "toep", "e", "inv", "mix_t", "mix", "sum", "nl", "act", "gp", "xh",
    "rs", "out",
)
BACKWARD = WEIGHTS + (
    "g", "q_t", "k", "k_t", "v", "e", "inv", "gp", "xh", "rs", "grad", "dz", "dpre", "sum", "da", "dm_t", "dq_t",
    "dk_t", "dv_t", "dq", "dk", "dv", "sm_a", "sm_b", "upb", "diag", "gout",
)
KEPT = ("q_t", "k", "k_t", "v", "e", "inv", "gp", "xhat", "scale")
SMALL = ("sm_a", "sm_b", "upb", "diag")


def kept_shapes(dims):
    rows, width, hidden, heads, micro, count = dims
    both = 2 * rows
    low = {
        "q_t": (width, both), "k": (rows, width), "k_t": (width, rows), "v": (rows, width),
        "e": (2, heads, rows, rows), "gp": (both, hidden), "xhat": (2, both, width), "out": (both, width),
        "grad": (both, width),
    }
    high = {
        "inv": (2, 16, rows), "scale": (2, both, 128), "sm_a": (8, width), "sm_b": (8, width),
        "upb": (8, hidden), "diag": (16, both), "d_total": (both, width), "d_summed": (both, width),
        "sm_c": (8, width),
    }
    return low, high


def stored_shapes(dims):
    rows, width, hidden, heads, micro, count = dims
    wide = 2 * rows * micro
    return {
        "w_x": (wide, width), "w_mix_t": (width, wide), "w_nl": (wide, width), "w_act": (wide, hidden),
        "w_dz": (wide, width), "w_dpre": (wide, hidden), "w_da": (wide, width), "w_dq": (wide, width),
        "w_dk": (wide // 2, width), "w_dv": (wide // 2, width),
    }


def sum_shapes(dims):
    rows, width, hidden, heads, micro, count = dims
    own, wide = width // count, hidden // count
    return {"down": (wide, width), "up": (own, hidden), "first": (2 * own, width), "second": (2 * own, width)}


SMEM = pl.BlockSpec(memory_space=pltpu.SMEM)
VMEM = pl.BlockSpec(memory_space=pltpu.VMEM)
ANY = pl.BlockSpec(memory_space=pl.ANY)
SPECS = dict(
    active=SMEM, core=SMEM, token=SMEM, lengths=SMEM, order=VMEM, predicted=VMEM, rel_table=VMEM, up_bias=VMEM, biases=VMEM, gains=VMEM
)


def kernel(run, m, dims, parts, names_in, names_out, names_scratch, *refs):
    r = dict(zip(names_in, refs))
    refs = refs[len(names_in):]
    r.update(zip(names_out, refs))
    refs = refs[len(names_out):]
    s = dict(zip(names_scratch, refs))
    cp = Copies(refs[len(names_scratch)])

    if "token" in r:
        r["token"][0] = 0
    if "tail" in parts:
        run(Layer(m, dims, r, s, cp, parts))
        return

    @pl.when(r["active"][0] == 1)
    def _():
        run(Layer(m, dims, r, s, cp, parts))


def call(run, m, fixed, parts, state, reads, writes, names_scratch, flops, copies):
    dims = fixed["dims"]
    low, high = kept_shapes(dims)
    shapes = {name: jax.ShapeDtypeStruct(dims, BF16) for name, dims in {**low, **stored_shapes(dims)}.items()}
    shapes.update({name: jax.ShapeDtypeStruct(dims, F32) for name, dims in high.items()})
    shapes["token"] = jax.ShapeDtypeStruct((1,), jnp.int32)
    for name, part in sum_shapes(dims).items():
        piece = (part[0], part[1] // PIECES[name])
        for i in range(PIECES[name]):
            shapes[f"s_{name}{i}"] = jax.ShapeDtypeStruct((dims[5] // 2,) + piece, BF16)
        shapes["k_" + name] = jax.ShapeDtypeStruct((dims[5] // 2,) + part, BF16)
    passed = [name for name in writes if name in state]
    made = [name for name in writes if name not in state]
    names_in = [name for name in reads if name not in passed]
    made += ["token"] * ("token" in state)
    names_in += ["old_token"] * ("token" in state)
    operands = [state[name.removeprefix("old_")] for name in names_in]
    all_scratch = scratch_shapes(dims)
    outs = pl.pallas_call(
        partial(
            kernel, run, m, dims, parts, names_in + ["old_" + name for name in passed], passed + made, names_scratch
        ),
        in_specs=[SPECS.get(name, ANY) for name in names_in] + [ANY] * len(passed),
        out_specs=[SPECS.get(name, ANY) for name in passed + made],
        out_shape=[shapes[name] for name in passed + made],
        scratch_shapes=[all_scratch[name] for name in names_scratch] + [pltpu.SemaphoreType.DMA((copies,))],
        input_output_aliases={len(operands) + i: i for i in range(len(passed))},
        compiler_params=pltpu.CompilerParams(vmem_limit_bytes=VMEM_LIMIT),
        cost_estimate=pl.CostEstimate(flops=flops, bytes_accessed=1_000, transcendentals=0),
    )(*operands, *[state[name] for name in passed])
    return {**state, **dict(zip(passed + made, outs))}


INPUTS = ("active", "lengths", "order", "predicted", "rel_table", "up_bias", "biases", "gains")
MATRICES = ("proj_weight", "out_weight", "up_weight", "down_weight")
FORWARD_STORE = ("w_x", "w_mix_t", "w_nl", "w_act")
BACKWARD_STORE = ("w_dz", "w_dpre", "w_da", "w_dq", "w_dk", "w_dv")


def forward(m, fixed, state):
    return call(
        run_forward, m, fixed, ("fwd",), state, INPUTS + MATRICES + ("xc", "xq"), KEPT + ("out",) + FORWARD_STORE,
        FORWARD, 8_000_000_000, 64,
    )


def backward(m, fixed, state):
    return call(
        run_backward, m, fixed, ("back",), state, ("active", "gains") + MATRICES + ("gc", "gq") + KEPT,
        ("grad",) + SMALL + BACKWARD_STORE, BACKWARD, 8_000_000_000, 64,
    )


def forward_backward(m, fixed, state):
    scratch = FORWARD + tuple(name for name in BACKWARD if name not in FORWARD)
    return call(
        run_both, m, fixed, ("fwd", "back"), state, INPUTS + MATRICES + ("xc", "xq", "gc", "gq"),
        ("out", "grad") + SMALL + FORWARD_STORE + BACKWARD_STORE, scratch, 16_000_000_000, 80,
    )


def tails(m, fixed):
    flags = ("active", "core")
    return (
        lambda state: call(
            tail_down, m, fixed, ("tail", "back"), state, flags + ("gains", "gc", "gq", "xhat", "scale", "w_act"),
            ("w_dz", "sm_a", "d_total") + sent("down"),
            ("g", "xh", "rs", "grad", "sm_a", "W_act", "W_dz", "G_down"), 1_000, 24,
        ),
        lambda state: call(
            tail_up, m, fixed, ("tail", "back"), state, flags + ("down_weight", "gp", "w_nl", "w_dz"),
            ("w_dpre", "upb") + sent("up"), ("dz", "wd", "gp", "upb", "W_nl", "T_nl", "W_dpre", "G_up"),
            1_000, 24,
        ),
        lambda state: call(
            tail_norm, m, fixed, ("back",), state,
            ("active", "gains", "up_weight", "d_total", "xhat", "scale", "w_dpre"), ("w_da", "sm_c", "d_summed"),
            ("dpre", "wu", "grad", "sum", "xh", "rs", "da", "sm_b"), 1_000, 24,
        ),
        lambda state: call(
            tail_attention, m, fixed, ("tail", "back"), state,
            flags + ("out_weight", "w_x", "w_mix_t", "w_da", "inv", "e", "q_t", "k", "k_t", "v"),
            ("w_dq", "w_dk", "w_dv", "sm_b", "diag") + sent("first", "second"),
            (
                "wo", "inv", "e", "q_t", "k", "k_t", "v", "dm_t", "dq_t", "dk_t", "dv_t", "sm_b", "diag", "W_x",
                "T_x", "W_mix_t", "W_da", "W_dq", "W_dk", "W_dv", "G_first", "G_second",
            ),
            1_000, 48,
        ),
        lambda state: call(
            tail_input, m, fixed, ("back",), state,
            ("active", "proj_weight", "d_summed", "w_dq", "w_dk", "w_dv"), ("grad",),
            ("wp", "grad", "dq", "dk", "dv", "gout"), 1_000, 16,
        ),
    )


def step_kernel(ends, pieces, refs):
    own, token, keep, *refs = refs
    come, refs = refs[:pieces], refs[pieces:]
    outs, (keep_s, come_s, sum_s, sems) = refs[:-4], refs[-4:]
    outs[-1][0] = 0
    count, _, columns = keep.shape
    columns //= pieces
    if ends:
        places = [0]
    else:
        half = count // 2
        places = [(1 - own[0]) * half + i for i in range(half)] + [own[0] * half + i for i in range(half)]
    copies, each = [], pieces + 1
    for i, p in enumerate(places):
        copies.append(pltpu.make_async_copy(keep.at[p], keep_s.at[i], sems.at[each * i]))
        for j in range(pieces):
            part = come_s.at[i, :, pl.ds(j * columns, columns)]
            copies.append(pltpu.make_async_copy(come[j].at[p], part, sems.at[each * i + j + 1]))
    for copy in copies:
        copy.start()
    back = []
    for i in range(count):
        for copy in copies[each * i:each * (i + 1)]:
            copy.wait()
        sum_s[i] = (keep_s[i].astype(F32) + come_s[i].astype(F32)).astype(sum_s.dtype)
        half = max(count // 2, 1)
        back.append(pltpu.make_async_copy(sum_s.at[i], outs[i // half].at[i % half], sems.at[each * count + i]))
        back[-1].start()
    for copy in back:
        copy.wait()


def step(state, keep, come, own):
    ends = own is None
    count, rows, columns = keep.shape
    own = jnp.zeros((1,), jnp.int32) if ends else own.reshape(1)
    half = jax.ShapeDtypeStruct((max(count // 2, 1), rows, columns), F32 if ends else keep.dtype)
    outs = pl.pallas_call(
        lambda *refs: step_kernel(ends, len(come), refs),
        in_specs=[SMEM, SMEM, ANY] + [ANY] * len(come),
        out_specs=[ANY] * (2 - ends) + [SMEM],
        out_shape=[half] * (2 - ends) + [jax.ShapeDtypeStruct((1,), jnp.int32)],
        scratch_shapes=[
            pltpu.VMEM(keep.shape, keep.dtype),
            pltpu.VMEM(keep.shape, keep.dtype),
            pltpu.VMEM(keep.shape, half.dtype),
            pltpu.SemaphoreType.DMA(((2 + len(come)) * count,)),
        ],
        compiler_params=pltpu.CompilerParams(vmem_limit_bytes=VMEM_LIMIT),
        cost_estimate=pl.CostEstimate(flops=1_000, bytes_accessed=1_000, transcendentals=0),
    )(own, state["token"], keep, *come)
    state["token"] = outs[-1]
    return outs[:-1]


class Sum:
    def __init__(self, axis, send, keep, order):
        self.axis, self.order = axis, list(order)
        self.place = lax.axis_index(axis)
        self.send(send, keep, 0)

    def send(self, send, keep, bit):
        route = [(device, device ^ (1 << bit)) for device in range(lax.axis_size(self.axis))]
        self.keep, self.come = keep, [lax.ppermute(part, self.axis, route) for part in send]

    def step(self, state=None):
        if not self.order and state is not None:
            return step(state, self.keep, self.come, None)[0][0]
        if not self.order:
            return self.keep[0].astype(F32) + self.come[0][0].astype(F32)
        bit = self.order.pop(0)
        own = (self.place >> bit) & 1
        if state is not None:
            send, keep = step(state, self.keep, self.come, own)
        else:
            come = jnp.concatenate(self.come, axis=2) if len(self.come) > 1 else self.come[0]
            half = come.shape[0] // 2
            total = lambda at: (
                lax.dynamic_slice_in_dim(self.keep, at * half, half).astype(F32)
                + lax.dynamic_slice_in_dim(come, at * half, half).astype(F32)
            ).astype(BF16)
            send, keep = total(1 - own), total(own)
        self.send([send], keep, bit)


def body(
    content_in,
    query_in,
    content_cot,
    query_cot,
    lengths,
    order,
    predicted,
    proj_weight,
    out_weight,
    up_weight,
    down_weight,
    up_bias,
    biases,
    gains,
    rel_table,
):
    micro, rows, width = content_in.shape
    hidden = up_bias.shape[1]
    heads = rel_table.shape[1] // BUCKETS
    first = (lax.axis_index("section") == 0).astype(jnp.int32).reshape(1)
    second = 1 - first
    state = dict(
        lengths=lengths,
        order=order,
        predicted=predicted,
        proj_weight=proj_weight,
        out_weight=out_weight,
        up_weight=up_weight,
        down_weight=down_weight,
        up_bias=up_bias,
        biases=biases,
        gains=gains,
        rel_table=rel_table,
    )
    fixed = dict(dims=(rows, width, hidden, heads, micro, lax.axis_size("dp")))
    flat = lambda a: a.reshape(micro * rows, width)
    halves = lambda a: (a[:rows], a[rows:])
    stored = BACKWARD_STORE + FORWARD_STORE
    own = KEPT + ("out", "grad") + SMALL
    kept = [{} for m in range(micro)]
    store = {}

    def run(function, m, active, **more):
        after = function(m, fixed, {**state, **kept[m], **store, "active": active, **more})
        kept[m] = {name: after[name] for name in own if name in after}
        store.update({name: after[name] for name in stored if name in after})

    across = lambda block, route: lax.ppermute(block, "section", route)
    arrived, returned = [None] * micro, [None] * micro
    for m in range(micro):
        run(forward, m, first, xc=flat(content_in), xq=flat(query_in))
        arrived[m] = [across(block, [(0, 1)]) for block in halves(kept[m]["out"])]
    for m in range(micro):
        run(
            forward_backward, m, second, xc=arrived[m][0], xq=arrived[m][1], gc=flat(content_cot), gq=flat(query_cot)
        )
        returned[m] = [across(block, [(1, 0)]) for block in halves(kept[m]["grad"])]
    count = fixed["dims"][5]
    place = lax.axis_index("dp")
    own_rows = width // count
    last = micro - 1
    for m in range(last):
        run(backward, m, first, gc=returned[m][0], gq=returned[m][1])
    state = {**state, **kept[last], **store, "active": first, "gc": returned[last][0], "gq": returned[last][1]}
    state["core"] = (place & 1).reshape(1)
    state["token"] = jnp.zeros((1,), jnp.int32)

    def open_sum(name):
        sends = [state[f"s_{name}{i}"] for i in range(PIECES[name])]
        return Sum("dp", sends, state["k_" + name], step_order(name, count))

    call_down, call_up, call_norm, call_attention, call_input = tails(last, fixed)
    state = call_down(state)
    down_sum = open_sum("down")
    down_sum.step(state)
    state = call_up(state)
    up_sum = open_sum("up")
    down_sum.step(state)
    up_sum.step(state)
    state = call_norm(state)
    down_sum.step(state)
    state = call_attention(state)
    first_sum, second_sum = open_sum("first"), open_sum("second")
    up_sum.step(state)
    first_sum.step(state)
    second_sum.step(state)
    token = state["token"].astype(F32)
    state = call_input(state)
    up_sum.step(state)
    second_sum.step(state)
    for _ in range(len(up_sum.order)):
        up_sum.step(state)
    up_grad = up_sum.step(state)
    first_sum.step(state)
    kept[last] = {**kept[last], **{name: state[name] for name in SMALL + ("grad",)}}
    kept[last]["sm_b"] = state["sm_b"] + jnp.where(first == 1, state["sm_c"], 0.0)
    sm_a, sm_b, upb, diag = [sum(part[name] for part in kept) + token for name in SMALL]
    small = jnp.stack([sm_b[0], sm_b[1], sm_b[2], sm_a[0], sm_b[3], sm_a[1], sm_b[4], sm_a[2]])
    bucket = bucket_index(rows - jnp.arange(2 * rows))
    tables = jnp.dot(
        (bucket[None, :] == jnp.arange(BUCKETS)[:, None]).astype(F32), diag[:heads].T, precision=lax.Precision.HIGHEST
    )
    extras = jnp.concatenate(
        [
            small.reshape(8, count, own_rows).transpose(1, 0, 2).reshape(count, 8 * own_rows),
            upb[0].reshape(count, hidden // count),
            tables.reshape(count, heads * BUCKETS // count),
        ],
        axis=1,
    )
    extras = jnp.sum(lax.all_to_all(extras, "dp", 0, 0, tiled=True), axis=0)
    results = {}
    sums = dict(down=down_sum, second=second_sum, first=first_sum)
    while sums:
        for name in list(sums):
            result = sums[name].step()
            if result is not None:
                results[name] = result
                del sums[name]
    down_grad = results["down"]
    split = lambda name: results[name].reshape(2, own_rows, width)
    proj_grad = jnp.concatenate([split("first"), split("second")[:1]])[None]
    out_grad = split("second")[1][None]
    small = extras[: 8 * own_rows].reshape(1, 8, own_rows)
    up_small = extras[8 * own_rows : 8 * own_rows + hidden // count][None]
    tab_small = extras[8 * own_rows + hidden // count :][None]
    stack = lambda name, i: jnp.stack([halves(part[name])[i] for part in kept])[None]
    return (
        stack("out", 0),
        stack("out", 1),
        stack("grad", 0),
        stack("grad", 1),
        proj_grad,
        out_grad,
        up_grad[None],
        down_grad[None],
        up_small,
        small[:, 0:6],
        small[:, 6:8],
        tab_small,
    )


def solution(mesh):
    return jax.shard_map(
        body,
        mesh=mesh,
        in_specs=(
            P(None, "dp", None),
            P(None, "dp", None),
            P(None, "dp", None),
            P(None, "dp", None),
            P(None, "dp", None),
            P(None, "dp"),
            P(None, "dp"),
            P("section", None, None, None),
            P("section", None, None),
            P("section", None, None),
            P("section", None, None),
            P("section", None),
            P("section", None, None),
            P("section", None, None),
            P("section", None),
        ),
        out_specs=(
            P("section", None, "dp", None),
            P("section", None, "dp", None),
            P("section", None, "dp", None),
            P("section", None, "dp", None),
            P("section", None, "dp", None),
            P("section", "dp", None),
            P("section", "dp", None),
            P("section", "dp", None),
            P("section", "dp"),
            P("section", None, "dp"),
            P("section", None, "dp"),
            P("section", "dp"),
        ),
        check_vma=False,
    )
```

```python
from functools import partial

import jax
import jax.numpy as jnp
from jax import lax
from jax.experimental import pallas as pl
from jax.experimental.pallas import tpu as pltpu
from jax.sharding import PartitionSpec as P

LN_EPS = 1e-05
NEG_FILL = -1e30
BUCKET_EDGES = (12, 16, 23, 32, 46, 64, 91)
BUCKETS = 32
F32, BF16 = jnp.float32, jnp.bfloat16
VMEM_LIMIT = 60 * 1024 * 1024
STEP_LIMIT = 16 * 1024 * 1024
TAIL = (0.127414796, -0.142248368, 0.7107068705, -0.7265760135, 0.5307027145)
TAIL_SLOPE = 0.3275911 / 2**0.5
DENSITY = 0.3989422804014327


def nn(left, right):
    return jnp.dot(left, right, preferred_element_type=F32)


def nt(left, right):
    return lax.dot_general(left, right, (((1,), (1,)), ((), ())), preferred_element_type=F32)


def iota(shape, dim):
    return lax.broadcasted_iota(jnp.int32, shape, dim)


def bucket_index(relative):
    magnitude = jnp.abs(relative)
    far_part = jnp.full_like(magnitude, 8)
    for edge_at in BUCKET_EDGES:
        far_part = far_part + jnp.where(magnitude >= edge_at, 1, 0)
    near_far = jnp.where(magnitude < 8, magnitude, far_part)
    return near_far + jnp.where(relative > 0, 16, 0)


def gelu_and_slope(v):
    z = jnp.abs(v)
    t = 1.0 / (1.0 + TAIL_SLOPE * z)
    poly = TAIL[4]
    for coefficient in TAIL[3::-1]:
        poly = coefficient + t * poly
    bell = jnp.exp(-0.5 * (v * v))
    tail = t * poly * bell
    below = jnp.where(v >= 0, 1.0 - tail, tail)
    return v * below, below + DENSITY * (v * bell)


class Copies:
    def __init__(self, sems):
        self.sems, self.used, self.open = sems, 0, []

    def copy(self, src, dst, at):
        return pltpu.make_async_copy(src, dst, self.sems.at[at])

    def start(self, src, dst):
        copy = self.copy(src, dst, self.used)
        self.used += 1
        copy.start()
        return copy

    def out(self, src, dst):
        self.open.append((src, dst, self.used))
        self.start(src, dst)

    def finish(self):
        for src, dst, at in self.open:
            self.copy(src, dst, at).wait()


def head_map(entries, heads, span):
    entry = iota((16, entries), 1)
    own_head = (entry - heads * ((entry * 5462) >> 16)) == iota((16, entries), 0)
    bucket = bucket_index(span // 2 - iota((entries, span), 1))
    row = iota((entries, span), 0)
    own_bucket = (row >= heads * bucket) & (row < heads * bucket + heads)
    return own_head, own_bucket


def make_masks(lengths, order_ref, predicted_ref, m, rows):
    def place(shape, dim):
        token = iota(shape, dim)
        segment, start, end = jnp.zeros(shape, jnp.int32), jnp.zeros(shape, jnp.int32), 0
        for slot in range(lengths.shape[2]):
            size = lengths[m, 0, slot]
            end = end + size
            passed = token >= end
            segment = segment + jnp.where(passed, 1, 0)
            start = start + jnp.where(passed, size, 0)
        inside = token < end
        return jnp.where(inside, segment, -1 - token), inside & (token - start > 0)

    segment, later = place((1, rows), 1)
    order = order_ref[pl.ds(m, 1), :]
    flag = (predicted_ref[pl.ds(m, 1), :] > 0) & later
    gate = jnp.where(flag, order, -1).astype(F32)
    gate_column = jnp.transpose(jnp.broadcast_to(gate, (128, rows)))
    segment_column = jnp.transpose(jnp.broadcast_to(segment.astype(F32), (128, rows)))
    gate_column = jnp.concatenate([gate_column] * (rows // 128), axis=1)
    segment_column = jnp.concatenate([segment_column] * (rows // 128), axis=1)
    same = segment_column == segment.astype(F32)
    order = order.astype(F32)
    return [
        jnp.where(same & (gate_column <= order), 0.0, NEG_FILL),
        jnp.where(same & (gate_column < order), 0.0, NEG_FILL),
    ]


def tn(left, right):
    return lax.dot_general(left, right, (((0,), (0,)), ((), ())), preferred_element_type=F32)


UNROLL_HEADS = 12
UNROLL_CHUNKS = 6
UNROLL_BLOCKS = 8
STEP = 256
CHUNK = 512
BLOCK = 64


MATRIX = dict(wp="proj_weight", wo="out_weight", wu="up_weight", wd="down_weight")


def loop(count, unroll, body):
    def turn(i, carry):
        for j in range(unroll):
            body(i * unroll + j)
        return carry

    if unroll == count:
        for i in range(count):
            body(i)
    else:
        lax.fori_loop(0, count // unroll, turn, 0)


def loop_heads(heads, body):
    def turn(i, carry):
        for j in range(UNROLL_HEADS):
            body(i * UNROLL_HEADS + j, j % 2)
        return carry

    if UNROLL_HEADS == heads:
        turn(0, 0)
    else:
        lax.fori_loop(0, heads // UNROLL_HEADS, turn, 0)


def span_of(i, size):
    return pl.ds(i * size if isinstance(i, int) else pl.multiple_of(i * size, size), size)


class Layer:
    def __init__(self, m, dims, r, s, cp, parts):
        self.m, self.r, self.s, self.cp, self.parts = m, r, s, cp, parts
        self.rows, self.width, self.hidden, self.heads, self.micro, self.count = dims
        self.depth = self.width // self.heads
        self.span = 2 * self.rows
        self.mine = pl.ds(m * 2 * self.rows, 2 * self.rows)
        self.mine_half = pl.ds(m * self.rows, self.rows)
        self.waits, self.later = {}, False

    def load(self, name, src, dst):
        self.waits[name] = (src, dst, self.cp.used)
        self.cp.used += 1
        if not self.later:
            self.begin(name)

    def begin(self, *names):
        for name in names or self.waits:
            self.cp.copy(*self.waits[name]).start()

    def need(self, *names):
        for name in names:
            if name in self.waits:
                self.cp.copy(*self.waits.pop(name)).wait()

    def load_weights(self, *names):
        r, s = self.r, self.s
        for name in names:
            self.load(name, r[MATRIX[name]].at[0], s[name])

    def load_streams(self, name, content, query):
        rows, dst = self.rows, self.s[name]
        if content.shape[0] != rows:
            content, query = content.at[self.mine_half], query.at[self.mine_half]
        self.load(name + "0", content, dst.at[pl.ds(0, rows)])
        self.load(name + "1", query, dst.at[pl.ds(rows, rows)])

    def out_streams(self, name):
        for i, stream in enumerate("cq"):
            self.cp.out(self.s[name + "_s"].at[pl.ds(i * self.rows, self.rows)], self.r[f"{name}_{stream}"])

    def forward(self):
        r, s, cp = self.r, self.s, self.cp
        rows, width, heads, depth, span = self.rows, self.width, self.heads, self.depth, self.span
        keep = "back" not in self.parts
        biases, gains = r["biases"], r["gains"]
        s["mask"][0], s["mask"][1] = make_masks(r["lengths"], r["order"], r["predicted"], self.m, rows)
        own_head, own_bucket = head_map(heads * BUCKETS, heads, span)
        picked = jnp.where(own_head, r["rel_table"][...], 0.0)
        s["toep"][...] = jnp.dot(
            picked, jnp.where(own_bucket, 1.0, 0.0), precision=lax.Precision.HIGHEST, preferred_element_type=F32
        )
        self.need("x0", "x1", "wp")
        cp.out(s["x"], r["w_x"].at[self.mine])
        for n in range(0, width, STEP):
            at = slice(n, n + STEP)
            q = nn(s["x"][...], s["wp"][0, :, at]) + biases[0, 0:1, at]
            s["q_t"][at, :] = jnp.transpose(q.astype(BF16) * 0.125)
        for n in range(0, width, STEP):
            at = slice(n, n + STEP)
            k = nn(s["x"][0:rows, :], s["wp"][1, :, at]).astype(BF16)
            s["k"][:, at] = k
            s["k_t"][at, :] = jnp.transpose(k)
            v = (nn(s["x"][0:rows, :], s["wp"][2, :, at]) + biases[0, 1:2, at]).astype(BF16)
            s["v"][:, at] = v
            s["v_t"][at, :] = jnp.transpose(v)
        blank = jnp.zeros((depth, 2 * rows), BF16)
        def head_step(head, odd):
            pair = span_of((head - odd) // 2, 2 * depth)
            at = span_of(head, depth)
            q_head = s["q_t"][at, :]
            stacked = jnp.concatenate([blank, q_head] if odd else [q_head, blank], axis=0)
            scores = nn(s["k"][:, pair], stacked)
            line = jnp.broadcast_to(s["toep"][pl.ds(head, 1), :], (rows, span))
            rel = pltpu.roll(line, rows, 1, stride=1, stride_axis=0)[:, :rows]
            for i in range(2):
                lanes = slice(i * rows, (i + 1) * rows)
                logits = scores[:, lanes] + rel + s["mask"][i]
                e = jnp.exp(logits - jnp.max(logits, axis=0, keepdims=True))
                inv = 1.0 / jnp.sum(e, axis=0, keepdims=True)
                e = e.astype(BF16)
                s["e"][i, head] = e
                s["inv"][i, pl.ds(head, 1), :] = inv
                s["mix_t"][at, lanes] = (nn(s["v_t"][at, :], e) * inv).astype(BF16)
        loop_heads(heads, head_step)
        if keep:
            for name in ("q_t", "k", "k_t", "v", "e", "inv"):
                cp.out(s[name], r[name])
        cp.out(s["mix_t"], r["w_mix_t"].at[:, self.mine])
        for n in range(0, width, STEP):
            s["mix"][:, n:n + STEP] = jnp.transpose(s["mix_t"][n:n + STEP, :])
        self.need("wo", "wu", "wd")
        for n in range(0, width, STEP):
            s["sum"][:, n:n + STEP] = nn(s["mix"][...], s["wo"][:, n:n + STEP])
        def block_step(n):
            at = span_of(n, BLOCK)
            summed = s["x"][at, :].astype(F32) + s["sum"][at, :] + biases[0, 2:3, :]
            center = summed - jnp.mean(summed, axis=1, keepdims=True)
            scale = lax.rsqrt(jnp.mean(center * center, axis=1, keepdims=True) + LN_EPS)
            xhat = center * scale
            normed = xhat * gains[0, 0:1, :] + biases[0, 4:5, :]
            s["xh"][0, at, :] = xhat.astype(BF16)
            s["rs"][0, at, :] = jnp.broadcast_to(scale, (BLOCK, 128))
            s["nl"][at, :] = normed.astype(BF16)
            s["sum"][at, :] = normed + biases[0, 3:4, :]
        loop(2 * self.rows // BLOCK, UNROLL_BLOCKS, block_step)
        if keep:
            cp.out(s["xh"].at[0], r["xhat"].at[0])
            cp.out(s["rs"].at[0], r["scale"].at[0])
        cp.out(s["nl"], r["w_nl"].at[self.mine])
        def chunk_step(j):
            at = span_of(j, CHUNK)
            act, slope = gelu_and_slope(nn(s["nl"][...], s["wu"][:, at]) + r["up_bias"][0:1, at])
            s["act"][:, at] = act.astype(BF16)
            s["gp"][:, at] = slope.astype(BF16)
        loop(self.hidden // CHUNK, UNROLL_CHUNKS, chunk_step)
        cp.out(s["act"], r["w_act"].at[self.mine])
        if keep:
            cp.out(s["gp"], r["gp"])
        for n in range(0, width, STEP):
            s["sum"][:, n:n + STEP] += nn(s["act"][...], s["wd"][:, n:n + STEP])
        def block_step(n):
            at = span_of(n, BLOCK)
            total = s["sum"][at, :]
            center = total - jnp.mean(total, axis=1, keepdims=True)
            scale = lax.rsqrt(jnp.mean(center * center, axis=1, keepdims=True) + LN_EPS)
            xhat = center * scale
            s["xh"][1, at, :] = xhat.astype(BF16)
            s["rs"][1, at, :] = jnp.broadcast_to(scale, (BLOCK, 128))
            s["out_s"][at, :] = (xhat * gains[0, 1:2, :] + biases[0, 5:6, :]).astype(BF16)
        loop(2 * self.rows // BLOCK, UNROLL_BLOCKS, block_step)
        self.out_streams("out")
        if keep:
            cp.out(s["xh"].at[1], r["xhat"].at[1])
            cp.out(s["rs"].at[1], r["scale"].at[1])

    def norm_back(self, which, grad, at, gain_sum, shift_sum):
        s = self.s
        xhat = s["xh"][which, at, :].astype(F32)
        ref, row = gain_sum
        s[ref][row:row + 1, :] += jnp.sum(grad * xhat, axis=0, keepdims=True)
        ref, row = shift_sum
        s[ref][row:row + 1, :] += jnp.sum(grad, axis=0, keepdims=True)
        scaled = grad * self.r["gains"][0, which:which + 1, :]
        mean_a = jnp.mean(scaled, axis=1, keepdims=True)
        mean_b = jnp.mean(scaled * xhat, axis=1, keepdims=True)
        return (scaled - mean_a - xhat * mean_b) * s["rs"][which, at, 0:1]

    def back_norm_two(self, dz):
        s = self.s
        s["sm_a"][...] = jnp.zeros(s["sm_a"].shape, F32)
        self.need("g0", "g1", "xh1", "rs1")
        def block_step(n):
            at = span_of(n, BLOCK)
            back = self.norm_back(1, s["g"][at, :].astype(F32), at, ("sm_a", 2), ("sm_a", 1))
            s["grad"][at, :] = back
            low = back.astype(BF16)
            dz[at, :] = low
            s["sm_a"][0:1, :] += jnp.sum(low.astype(F32), axis=0, keepdims=True)
        loop(2 * self.rows // BLOCK, UNROLL_BLOCKS, block_step)
        self.cp.out(dz, self.r["w_dz"].at[self.mine])
        self.cp.out(s["sm_a"], self.r["sm_a"])

    def back_up(self, dz, dpre):
        s = self.s
        self.need("wd")
        self.need("gp")
        def chunk_step(j):
            at = span_of(j, CHUNK)
            d_act = nt(dz[...], s["wd"][at, :])
            d_pre = (d_act * s["gp"][:, at].astype(F32)).astype(BF16)
            dpre[:, at] = d_pre
            s["upb"][0:1, at] = jnp.sum(d_pre.astype(F32), axis=0, keepdims=True)
        loop(self.hidden // CHUNK, UNROLL_CHUNKS, chunk_step)
        self.cp.out(dpre, self.r["w_dpre"].at[self.mine])
        self.cp.out(s["upb"], self.r["upb"])

    def back_norm_one(self, dpre, da):
        s = self.s
        s["sm_b"][...] = jnp.zeros(s["sm_b"].shape, F32)
        self.need("wu")
        for n in range(0, self.width, STEP):
            s["sum"][:, n:n + STEP] = nt(dpre[...], s["wu"][n:n + STEP, :])
        self.need("xh0", "rs0", "grad")
        def block_step(n):
            at = span_of(n, BLOCK)
            back = self.norm_back(0, s["grad"][at, :] + s["sum"][at, :], at, ("sm_b", 4), ("sm_b", 3))
            s["grad"][at, :] = back
            low = back.astype(BF16)
            da[at, :] = low
            s["sm_b"][2:3, :] += jnp.sum(low.astype(F32), axis=0, keepdims=True)
        loop(2 * self.rows // BLOCK, UNROLL_BLOCKS, block_step)
        self.cp.out(da, self.r["w_da"].at[self.mine])

    def back_attention(self, da, dq, dk, dv):
        s, cp, r = self.s, self.cp, self.r
        rows, width, heads, depth, span = self.rows, self.width, self.heads, self.depth, self.span
        self.need("wo", "inv")
        for n in range(0, width, STEP):
            d_mix = nt(s["wo"][n:n + STEP, :], da[...])
            for h in range(n // depth, (n + STEP) // depth):
                inv = jnp.concatenate([s["inv"][i, h:h + 1, :] for i in range(2)], axis=1)
                s["dm_t"][h * depth:(h + 1) * depth, :] = (d_mix[h * depth - n:(h + 1) * depth - n, :] * inv).astype(BF16)
        self.need("e", "q_t", "k", "k_t", "v")
        blank = jnp.zeros((depth, 2 * rows), BF16)
        s["diag"][...] = jnp.zeros(s["diag"].shape, F32)
        def head_step(head, odd):
            pair = span_of((head - odd) // 2, 2 * depth)
            at = span_of(head, depth)
            dm_head = s["dm_t"][at, :]
            stacked = jnp.concatenate([blank, dm_head] if odd else [dm_head, blank], axis=0)
            d_prob = nn(s["v"][:, pair], stacked)
            parts, whole = [], 0.0
            for i in range(2):
                e = s["e"][i, head].astype(F32)
                part = d_prob[:, i * rows:(i + 1) * rows]
                mean = jnp.sum(e * part, axis=0, keepdims=True) * s["inv"][i, pl.ds(head, 1), :]
                d_score = (e * (part - mean)).astype(BF16)
                parts.append(d_score)
                whole = whole + d_score.astype(F32)
            both = jnp.concatenate(parts, axis=1)
            e_both = jnp.concatenate([s["e"][0, head], s["e"][1, head]], axis=1)
            s["dq_t"][at, :] = (nn(s["k_t"][at, :], both) * 0.125).astype(BF16)
            s["dv_t"][at, :] = nt(dm_head, e_both).astype(BF16)
            s["dk_t"][at, :] = nt(s["q_t"][at, :], both).astype(BF16)
            wide = jnp.concatenate([jnp.zeros_like(whole), whole], axis=1)
            count = rows
            while count > 8:
                count //= 2
                wide = wide[:count, :] + pltpu.roll(wide[count:, :], span - count, 1)
            line = wide[0:1, :]
            for k in range(1, 8):
                line = line + pltpu.roll(wide, span - k, 1)[k:k + 1, :]
            s["diag"][pl.ds(head, 1), :] = line
        loop_heads(heads, head_step)
        for n in range(0, width, STEP):
            at = slice(n, n + STEP)
            part = jnp.transpose(s["dq_t"][at, :])
            dq[:, at] = part
            s["sm_b"][0:1, at] = jnp.sum(part.astype(F32), axis=0, keepdims=True)
            dk[:, at] = jnp.transpose(s["dk_t"][at, :])
            part = jnp.transpose(s["dv_t"][at, :])
            dv[:, at] = part
            s["sm_b"][1:2, at] = jnp.sum(part.astype(F32), axis=0, keepdims=True)
        cp.out(dq, r["w_dq"].at[self.mine])
        cp.out(dk, r["w_dk"].at[self.mine_half])
        cp.out(dv, r["w_dv"].at[self.mine_half])
        cp.out(s["sm_b"], r["sm_b"])
        cp.out(s["diag"], r["diag"])

    def back_input(self, dq, dk, dv):
        s, rows = self.s, self.rows
        self.need("wp")
        for n in range(0, self.width, STEP):
            at = slice(n, n + STEP)
            back = s["grad"][:, at] + nt(dq[...], s["wp"][0, at, :])
            more = nt(dk[...], s["wp"][1, at, :]) + nt(dv[...], s["wp"][2, at, :])
            s["grad_s"][0:rows, at] = (back[0:rows, :] + more).astype(BF16)
            s["grad_s"][rows:, at] = back[rows:, :].astype(BF16)
        self.out_streams("grad")


def run_forward(layer):
    layer.load_streams("x", layer.r["xc"], layer.r["xq"])
    layer.load_weights("wp", "wo", "wu", "wd")
    layer.forward()
    layer.cp.finish()


def run_backward(layer):
    r, s = layer.r, layer.s
    layer.load_streams("g", r["gc"], r["gq"])
    for i in (1, 0):
        layer.load(f"xh{i}", r["xhat"].at[i], s["xh"].at[i])
        layer.load(f"rs{i}", r["scale"].at[i], s["rs"].at[i])
    layer.load_weights("wd")
    layer.load("gp", r["gp"], s["gp"])
    layer.load_weights("wu", "wo")
    for name in ("inv", "e", "q_t", "k", "k_t", "v"):
        layer.load(name, r[name], s[name])
    layer.load_weights("wp")
    all_back(layer)
    layer.cp.finish()


def all_back(layer):
    s = layer.s
    layer.back_norm_two(s["dz"])
    layer.back_up(s["dz"], s["dpre"])
    layer.back_norm_one(s["dpre"], s["da"])
    layer.back_attention(s["da"], s["dq"], s["dk"], s["dv"])
    layer.back_input(s["dq"], s["dk"], s["dv"])


def run_both(layer):
    layer.load_streams("x", layer.r["xc"], layer.r["xq"])
    layer.load_weights("wp", "wo", "wu", "wd")
    layer.load_streams("g", layer.r["gc"], layer.r["gq"])
    layer.forward()
    all_back(layer)
    layer.cp.finish()


def step_order(name, count):
    straight = list(range(1, count.bit_length() - 1))
    return straight[1:] + straight[:1] if name in TURNED else straight


def part_at(name, device, count):
    at = 0
    for bit in step_order(name, count):
        at = 2 * at + (device >> bit & 1)
    return at


def emit(layer, name, first, columns, value):
    parts = layer.s["G_" + name]
    size = value.shape[0] // layer.count
    for device in range(layer.count):
        rows = value[device * size:(device + 1) * size, :].astype(BF16)
        parts[part_at(name, device, layer.count), device % 2, first:first + size, columns] = rows


TURNED = ("up",)
PIECES = dict(down=1, up=4, first=3, second=1)


def sent(*names):
    return tuple(f"s_{name}{i}" for name in names for i in range(PIECES[name])) + tuple("k_" + name for name in names)


def send_parts(layer, *names):
    core = layer.r["core"][0]
    for name in names:
        for i in range(PIECES[name]):
            columns = layer.r[f"s_{name}{i}"].shape[2]
            layer.cp.out(
                layer.s["G_" + name].at[:, 1 - core, :, pl.ds(i * columns, columns)], layer.r[f"s_{name}{i}"]
            )
    for name in names:
        layer.cp.out(layer.s["G_" + name].at[:, core], layer.r["k_" + name])


def tail_down(layer):
    r, s, cp = layer.r, layer.s, layer.cp
    active = r["active"][0] == 1
    other = pl.ds((1 - layer.m) * 2 * layer.rows, 2 * layer.rows)
    mine = s["W_dz"].at[layer.mine]

    layer.later = True
    layer.load_streams("g", r["gc"], r["gq"])
    layer.load("xh1", r["xhat"].at[1], s["xh"].at[1])
    layer.load("rs1", r["scale"].at[1], s["rs"].at[1])
    layer.later = False

    @pl.when(active)
    def _():
        layer.begin()

    layer.load("act", r["w_act"], s["W_act"])
    layer.load("other", r["w_dz"].at[other], s["W_dz"].at[other])

    @pl.when(active)
    def _():
        layer.back_norm_two(mine)
        cp.out(s["grad"], r["d_total"])

    opened, cp.open = cp.open, []

    @pl.when(jnp.logical_not(active))
    def _():
        cp.start(r["w_dz"].at[layer.mine], mine).wait()

    layer.need("act", "other")
    size = layer.hidden // layer.count
    for n in range(0, layer.hidden, 2 * size):
        both = tn(s["W_act"][:, n:n + 2 * size], s["W_dz"][...]).astype(BF16)
        at = part_at("down", n // size, layer.count)
        s["G_down"][at, 0] = both[:size]
        s["G_down"][at, 1] = both[size:]
    send_parts(layer, "down")

    @pl.when(active)
    def _():
        for src, dst, at in opened:
            cp.copy(src, dst, at).wait()

    cp.finish()


def tail_up(layer):
    r, s, cp = layer.r, layer.s, layer.cp
    active = r["active"][0] == 1
    other = pl.ds((1 - layer.m) * 2 * layer.rows, 2 * layer.rows)
    mine = s["W_dpre"].at[layer.mine]

    layer.later = True
    layer.load("dz", r["w_dz"].at[layer.mine], s["dz"])
    layer.load_weights("wd")
    layer.load("gp", r["gp"], s["gp"])
    layer.load_weights("wu")
    layer.load("grad", r["d_total"], s["grad"])
    layer.load("xh0", r["xhat"].at[0], s["xh"].at[0])
    layer.load("rs0", r["scale"].at[0], s["rs"].at[0])
    layer.later = False

    @pl.when(active)
    def _():
        layer.begin("dz", "wd", "gp", "wu", "grad", "xh0", "rs0")

    layer.load("nl", r["w_nl"], s["W_nl"])
    layer.load("other", r["w_dpre"].at[other], s["W_dpre"].at[other])

    @pl.when(active)
    def _():
        layer.need("dz")
        layer.back_up(s["dz"], mine)

    opened, cp.open = cp.open, []

    @pl.when(jnp.logical_not(active))
    def _():
        cp.start(r["w_dpre"].at[layer.mine], mine).wait()

    layer.need("nl", "other")
    for n in range(0, layer.width, STEP):
        at = slice(n, n + STEP)
        s["T_nl"][at, :] = jnp.transpose(s["W_nl"][:, at])
    for n in range(0, layer.hidden, CHUNK):
        emit(layer, "up", 0, slice(n, n + CHUNK), nn(s["T_nl"][...], s["W_dpre"][:, n:n + CHUNK]))
    send_parts(layer, "up")
    sends, cp.open = cp.open, opened

    @pl.when(active)
    def _():
        layer.back_norm_one(mine, s["da"])
        cp.out(s["grad"], r["d_summed"])
        cp.out(s["sm_b"], r["sm_c"])
        cp.finish()

    cp.open = sends
    cp.finish()


def tail_attention(layer):
    r, s, cp = layer.r, layer.s, layer.cp
    rows = layer.rows
    active = r["active"][0] == 1
    other = pl.ds((1 - layer.m) * 2 * rows, 2 * rows)
    other_half = pl.ds((1 - layer.m) * rows, rows)
    places = (
        ("dq", layer.mine, other), ("dk", layer.mine_half, other_half), ("dv", layer.mine_half, other_half),
    )
    mine = {name: s["W_" + name].at[own] for name, own, _ in places}

    layer.load("da", r["w_da"], s["W_da"])
    layer.later = True
    layer.load_weights("wo")
    for name in ("inv", "e", "q_t", "k", "k_t", "v"):
        layer.load(name, r[name], s[name])
    layer.later = False

    @pl.when(active)
    def _():
        layer.begin("wo", "inv", "e", "q_t", "k", "k_t", "v")

    layer.load("x", r["w_x"], s["W_x"])
    layer.load("mix", r["w_mix_t"], s["W_mix_t"])
    for name, _, far in places:
        layer.load("other" + name, r["w_" + name].at[far], s["W_" + name].at[far])
    layer.need("da")

    @pl.when(active)
    def _():
        s["sm_b"][...] = jnp.zeros(s["sm_b"].shape, F32)
        layer.back_attention(s["W_da"].at[layer.mine], mine["dq"], mine["dk"], mine["dv"])

    opened, cp.open = cp.open, []

    @pl.when(jnp.logical_not(active))
    def _():
        copies = [cp.start(r["w_" + name].at[own], mine[name]) for name, own, _ in places]
        for copy in copies:
            copy.wait()

    layer.need("x", "mix", *["other" + name for name, _, _ in places])
    for n in range(0, layer.width, STEP):
        at = slice(n, n + STEP)
        s["T_x"][at, :] = jnp.transpose(s["W_x"][:, at])
    content = jnp.concatenate([s["T_x"][:, m * 2 * rows:(m * 2 + 1) * rows] for m in range(layer.micro)], axis=1)
    size = layer.width // layer.count
    for n in range(0, layer.width, STEP):
        at = slice(n, n + STEP)
        emit(layer, "first", 0, at, nn(s["T_x"][...], s["W_dq"][:, at]))
        emit(layer, "first", size, at, nn(content, s["W_dk"][:, at]))
        emit(layer, "first", 2 * size, at, nn(content, s["W_dv"][:, at]))
        emit(layer, "second", 0, at, nn(s["W_mix_t"][...], s["W_da"][:, at]))
    send_parts(layer, "first", "second")

    @pl.when(active)
    def _():
        for src, dst, at in opened:
            cp.copy(src, dst, at).wait()

    cp.finish()


def tail_input(layer):
    r, s = layer.r, layer.s
    layer.load_weights("wp")
    layer.load("grad", r["d_summed"], s["grad"])
    layer.load("dq", r["w_dq"].at[layer.mine], s["dq"])
    layer.load("dk", r["w_dk"].at[layer.mine_half], s["dk"])
    layer.load("dv", r["w_dv"].at[layer.mine_half], s["dv"])
    layer.need("grad", "dq", "dk", "dv")
    layer.back_input(s["dq"], s["dk"], s["dv"])
    layer.cp.finish()


def scratch_shapes(dims):
    rows, width, hidden, heads, micro, count = dims
    both, all_rows = 2 * rows, 2 * rows * micro
    low = {
        "x": (both, width), "wp": (3, width, width), "wo": (width, width), "wu": (width, hidden),
        "wd": (hidden, width), "q_t": (width, both), "k": (rows, width), "k_t": (width, rows),
        "v": (rows, width), "v_t": (width, rows), "e": (2, heads, rows, rows), "mix_t": (width, both),
        "mix": (both, width), "nl": (both, width), "act": (both, hidden), "gp": (both, hidden),
        "xh": (2, both, width), "out_s": (both, width), "g": (both, width), "dz": (both, width),
        "dpre": (both, hidden), "da": (both, width), "dm_t": (width, both), "dq_t": (width, both),
        "dk_t": (width, rows), "dv_t": (width, rows), "dq": (both, width), "dk": (rows, width),
        "dv": (rows, width), "grad_s": (both, width),
    }
    high = {
        "mask": (2, rows, rows), "toep": (16, both), "inv": (2, 16, rows), "sum": (both, width),
        "rs": (2, both, 128), "grad": (both, width), "sm_a": (8, width), "sm_b": (8, width),
        "upb": (8, hidden), "diag": (16, both),
    }
    low.update({"W_" + name[2:]: dims for name, dims in stored_shapes(dims).items()})
    low.update({"G_" + name: (count // 2, 2) + part for name, part in sum_shapes(dims).items()})
    low.update({"T_x": (width, all_rows), "T_nl": (width, all_rows)})
    shapes = {name: pltpu.VMEM(dims, BF16) for name, dims in low.items()}
    shapes.update({name: pltpu.VMEM(dims, F32) for name, dims in high.items()})
    return shapes


WEIGHTS = ("wp", "wo", "wu", "wd")
FORWARD = WEIGHTS + (
    "x", "q_t", "k", "k_t", "v", "v_t", "mask", "toep", "e", "inv", "mix_t", "mix", "sum", "nl", "act", "gp", "xh",
    "rs", "out_s",
)
BACKWARD = WEIGHTS + (
    "g", "q_t", "k", "k_t", "v", "e", "inv", "gp", "xh", "rs", "grad", "dz", "dpre", "sum", "da", "dm_t", "dq_t",
    "dk_t", "dv_t", "dq", "dk", "dv", "sm_a", "sm_b", "upb", "diag", "grad_s",
)
KEPT = ("q_t", "k", "k_t", "v", "e", "inv", "gp", "xhat", "scale")
OUT, GRAD = ("out_c", "out_q"), ("grad_c", "grad_q")
SMALL = ("sm_a", "sm_b", "upb", "diag")


def kept_shapes(dims):
    rows, width, hidden, heads, micro, count = dims
    both = 2 * rows
    low = {
        "q_t": (width, both), "k": (rows, width), "k_t": (width, rows), "v": (rows, width),
        "e": (2, heads, rows, rows), "gp": (both, hidden), "xhat": (2, both, width), "out_c": (rows, width),
        "out_q": (rows, width), "grad_c": (rows, width), "grad_q": (rows, width),
    }
    high = {
        "inv": (2, 16, rows), "scale": (2, both, 128), "sm_a": (8, width), "sm_b": (8, width),
        "upb": (8, hidden), "diag": (16, both), "d_total": (both, width), "d_summed": (both, width),
        "sm_c": (8, width),
    }
    return low, high


def stored_shapes(dims):
    rows, width, hidden, heads, micro, count = dims
    wide = 2 * rows * micro
    return {
        "w_x": (wide, width), "w_mix_t": (width, wide), "w_nl": (wide, width), "w_act": (wide, hidden),
        "w_dz": (wide, width), "w_dpre": (wide, hidden), "w_da": (wide, width), "w_dq": (wide, width),
        "w_dk": (wide // 2, width), "w_dv": (wide // 2, width),
    }


def sum_shapes(dims):
    rows, width, hidden, heads, micro, count = dims
    own, wide = width // count, hidden // count
    return {"down": (wide, width), "up": (own, hidden), "first": (3 * own, width), "second": (own, width)}


SMEM = pl.BlockSpec(memory_space=pltpu.SMEM)
VMEM = pl.BlockSpec(memory_space=pltpu.VMEM)
ANY = pl.BlockSpec(memory_space=pl.ANY)
SPECS = dict(
    active=SMEM, core=SMEM, token=SMEM, lengths=SMEM, order=VMEM, predicted=VMEM, rel_table=VMEM, up_bias=VMEM, biases=VMEM, gains=VMEM
)


def kernel(run, m, dims, parts, names_in, names_out, names_scratch, *refs):
    r = dict(zip(names_in, refs))
    refs = refs[len(names_in):]
    r.update(zip(names_out, refs))
    refs = refs[len(names_out):]
    s = dict(zip(names_scratch, refs))
    cp = Copies(refs[len(names_scratch)])

    if "token" in r:
        r["token"][0] = 0
    if "tail" in parts:
        run(Layer(m, dims, r, s, cp, parts))
        return

    @pl.when(r["active"][0] == 1)
    def _():
        run(Layer(m, dims, r, s, cp, parts))


def call(run, m, fixed, parts, state, reads, writes, names_scratch, flops, copies):
    dims = fixed["dims"]
    low, high = kept_shapes(dims)
    shapes = {name: jax.ShapeDtypeStruct(dims, BF16) for name, dims in {**low, **stored_shapes(dims)}.items()}
    shapes.update({name: jax.ShapeDtypeStruct(dims, F32) for name, dims in high.items()})
    shapes["token"] = jax.ShapeDtypeStruct((1,), jnp.int32)
    for name, part in sum_shapes(dims).items():
        piece = (part[0], part[1] // PIECES[name])
        for i in range(PIECES[name]):
            shapes[f"s_{name}{i}"] = jax.ShapeDtypeStruct((dims[5] // 2,) + piece, BF16)
        shapes["k_" + name] = jax.ShapeDtypeStruct((dims[5] // 2,) + part, BF16)
    passed = [name for name in writes if name in state]
    made = [name for name in writes if name not in state]
    names_in = [name for name in reads if name not in passed]
    made += ["token"] * ("token" in state)
    names_in += ["old_token"] * ("token" in state)
    operands = [state[name.removeprefix("old_")] for name in names_in]
    all_scratch = scratch_shapes(dims)
    outs = pl.pallas_call(
        partial(
            kernel, run, m, dims, parts, names_in + ["old_" + name for name in passed], passed + made, names_scratch
        ),
        in_specs=[SPECS.get(name, ANY) for name in names_in] + [ANY] * len(passed),
        out_specs=[SPECS.get(name, ANY) for name in passed + made],
        out_shape=[shapes[name] for name in passed + made],
        scratch_shapes=[all_scratch[name] for name in names_scratch] + [pltpu.SemaphoreType.DMA((copies,))],
        input_output_aliases={len(operands) + i: i for i in range(len(passed))},
        compiler_params=pltpu.CompilerParams(vmem_limit_bytes=VMEM_LIMIT),
        cost_estimate=pl.CostEstimate(flops=flops, bytes_accessed=1_000, transcendentals=0),
    )(*operands, *[state[name] for name in passed])
    return {**state, **dict(zip(passed + made, outs))}


INPUTS = ("active", "lengths", "order", "predicted", "rel_table", "up_bias", "biases", "gains")
MATRICES = ("proj_weight", "out_weight", "up_weight", "down_weight")
FORWARD_STORE = ("w_x", "w_mix_t", "w_nl", "w_act")
BACKWARD_STORE = ("w_dz", "w_dpre", "w_da", "w_dq", "w_dk", "w_dv")


def forward(m, fixed, state):
    return call(
        run_forward, m, fixed, ("fwd",), state, INPUTS + MATRICES + ("xc", "xq"), KEPT + OUT + FORWARD_STORE,
        FORWARD, 8_000_000_000, 64,
    )


def backward(m, fixed, state):
    return call(
        run_backward, m, fixed, ("back",), state, ("active", "gains") + MATRICES + ("gc", "gq") + KEPT,
        GRAD + SMALL + BACKWARD_STORE, BACKWARD, 8_000_000_000, 64,
    )


def forward_backward(m, fixed, state):
    scratch = FORWARD + tuple(name for name in BACKWARD if name not in FORWARD)
    return call(
        run_both, m, fixed, ("fwd", "back"), state, INPUTS + MATRICES + ("xc", "xq", "gc", "gq"),
        OUT + GRAD + SMALL + FORWARD_STORE + BACKWARD_STORE, scratch, 16_000_000_000, 80,
    )


def tails(m, fixed):
    flags = ("active", "core")
    return (
        lambda state: call(
            tail_down, m, fixed, ("tail", "back"), state, flags + ("gains", "gc", "gq", "xhat", "scale", "w_act"),
            ("w_dz", "sm_a", "d_total") + sent("down"),
            ("g", "xh", "rs", "grad", "sm_a", "W_act", "W_dz", "G_down"), 1_000, 24,
        ),
        lambda state: call(
            tail_up, m, fixed, ("tail", "back"), state,
            flags + ("gains", "down_weight", "up_weight", "gp", "w_nl", "w_dz", "d_total", "xhat", "scale"),
            ("w_dpre", "upb", "w_da", "sm_c", "d_summed") + sent("up"),
            (
                "dz", "wd", "gp", "upb", "wu", "grad", "sum", "xh", "rs", "da", "sm_b", "W_nl", "T_nl", "W_dpre",
                "G_up",
            ),
            1_000, 24,
        ),
        lambda state: call(
            tail_attention, m, fixed, ("tail", "back"), state,
            flags + ("out_weight", "w_x", "w_mix_t", "w_da", "inv", "e", "q_t", "k", "k_t", "v"),
            ("w_dq", "w_dk", "w_dv", "sm_b", "diag") + sent("first", "second"),
            (
                "wo", "inv", "e", "q_t", "k", "k_t", "v", "dm_t", "dq_t", "dk_t", "dv_t", "sm_b", "diag", "W_x",
                "T_x", "W_mix_t", "W_da", "W_dq", "W_dk", "W_dv", "G_first", "G_second",
            ),
            1_000, 48,
        ),
        lambda state: call(
            tail_input, m, fixed, ("back",), state,
            ("active", "proj_weight", "d_summed", "w_dq", "w_dk", "w_dv"), GRAD,
            ("wp", "grad", "dq", "dk", "dv", "grad_s"), 1_000, 16,
        ),
    )


def step_kernel(ends, pieces, refs):
    own, token, keep, *refs = refs
    come, refs = refs[:pieces], refs[pieces:]
    outs, (keep_s, come_s, sum_s, sems) = refs[:-4], refs[-4:]
    outs[-1][0] = 0
    count, _, columns = keep.shape
    columns //= pieces
    if ends:
        places = [0]
    else:
        half = count // 2
        places = [(1 - own[0]) * half + i for i in range(half)] + [own[0] * half + i for i in range(half)]
    copies, each = [], pieces + 1
    for i, p in enumerate(places):
        copies.append(pltpu.make_async_copy(keep.at[p], keep_s.at[i], sems.at[each * i]))
        for j in range(pieces):
            part = come_s.at[i, :, pl.ds(j * columns, columns)]
            copies.append(pltpu.make_async_copy(come[j].at[p], part, sems.at[each * i + j + 1]))
    for copy in copies:
        copy.start()
    back = []
    for i in range(count):
        for copy in copies[each * i:each * (i + 1)]:
            copy.wait()
        sum_s[i] = (keep_s[i].astype(F32) + come_s[i].astype(F32)).astype(sum_s.dtype)
        half = max(count // 2, 1)
        back.append(pltpu.make_async_copy(sum_s.at[i], outs[i // half].at[i % half], sems.at[each * count + i]))
        back[-1].start()
    for copy in back:
        copy.wait()


def step(state, keep, come, own):
    ends = own is None
    count, rows, columns = keep.shape
    own = jnp.zeros((1,), jnp.int32) if ends else own.reshape(1)
    half = jax.ShapeDtypeStruct((max(count // 2, 1), rows, columns), F32 if ends else keep.dtype)
    small = keep.size * keep.dtype.itemsize < 1_500_000
    outs = pl.pallas_call(
        lambda *refs: step_kernel(ends, len(come), refs),
        in_specs=[SMEM, SMEM, ANY] + [ANY] * len(come),
        out_specs=[ANY] * (2 - ends) + [SMEM],
        out_shape=[half] * (2 - ends) + [jax.ShapeDtypeStruct((1,), jnp.int32)],
        scratch_shapes=[
            pltpu.VMEM(keep.shape, keep.dtype),
            pltpu.VMEM(keep.shape, keep.dtype),
            pltpu.VMEM(keep.shape, half.dtype),
            pltpu.SemaphoreType.DMA(((2 + len(come)) * count,)),
        ],
        compiler_params=pltpu.CompilerParams(vmem_limit_bytes=STEP_LIMIT if small else VMEM_LIMIT),
        cost_estimate=pl.CostEstimate(flops=1_000, bytes_accessed=1_000, transcendentals=0),
    )(own, state["token"], keep, *come)
    state["token"] = outs[-1]
    return outs[:-1]


class Sum:
    def __init__(self, axis, send, keep, order):
        self.axis, self.order = axis, list(order)
        self.place = lax.axis_index(axis)
        self.send(send, keep, 0)

    def send(self, send, keep, bit):
        route = [(device, device ^ (1 << bit)) for device in range(lax.axis_size(self.axis))]
        self.keep, self.come = keep, [lax.ppermute(part, self.axis, route) for part in send]

    def step(self, state=None):
        if not self.order and state is not None:
            return step(state, self.keep, self.come, None)[0][0]
        if not self.order:
            return self.keep[0].astype(F32) + self.come[0][0].astype(F32)
        bit = self.order.pop(0)
        own = (self.place >> bit) & 1
        if state is not None:
            send, keep = step(state, self.keep, self.come, own)
        else:
            come = jnp.concatenate(self.come, axis=2) if len(self.come) > 1 else self.come[0]
            half = come.shape[0] // 2
            total = lambda at: (
                lax.dynamic_slice_in_dim(self.keep, at * half, half).astype(F32)
                + lax.dynamic_slice_in_dim(come, at * half, half).astype(F32)
            ).astype(BF16)
            send, keep = total(1 - own), total(own)
        self.send([send], keep, bit)


def body(
    content_in,
    query_in,
    content_cot,
    query_cot,
    lengths,
    order,
    predicted,
    proj_weight,
    out_weight,
    up_weight,
    down_weight,
    up_bias,
    biases,
    gains,
    rel_table,
):
    micro, rows, width = content_in.shape
    hidden = up_bias.shape[1]
    heads = rel_table.shape[1] // BUCKETS
    first = (lax.axis_index("section") == 0).astype(jnp.int32).reshape(1)
    second = 1 - first
    state = dict(
        lengths=lengths,
        order=order,
        predicted=predicted,
        proj_weight=proj_weight,
        out_weight=out_weight,
        up_weight=up_weight,
        down_weight=down_weight,
        up_bias=up_bias,
        biases=biases,
        gains=gains,
        rel_table=rel_table,
    )
    fixed = dict(dims=(rows, width, hidden, heads, micro, lax.axis_size("dp")))
    flat = lambda a: a.reshape(micro * rows, width)
    stored = BACKWARD_STORE + FORWARD_STORE
    own = KEPT + OUT + GRAD + SMALL
    kept = [{} for m in range(micro)]
    store = {}

    def run(function, m, active, **more):
        after = function(m, fixed, {**state, **kept[m], **store, "active": active, **more})
        kept[m] = {name: after[name] for name in own if name in after}
        store.update({name: after[name] for name in stored if name in after})

    across = lambda block, route: lax.ppermute(block, "section", route)
    arrived, returned = [None] * micro, [None] * micro
    for m in range(micro):
        run(forward, m, first, xc=flat(content_in), xq=flat(query_in))
        arrived[m] = [across(kept[m][name], [(0, 1)]) for name in OUT]
    for m in range(micro):
        run(
            forward_backward, m, second, xc=arrived[m][0], xq=arrived[m][1], gc=flat(content_cot), gq=flat(query_cot)
        )
        returned[m] = [across(kept[m][name], [(1, 0)]) for name in GRAD]
    count = fixed["dims"][5]
    place = lax.axis_index("dp")
    own_rows = width // count
    last = micro - 1
    for m in range(last):
        run(backward, m, first, gc=returned[m][0], gq=returned[m][1])
    state = {**state, **kept[last], **store, "active": first, "gc": returned[last][0], "gq": returned[last][1]}
    state["core"] = (place & 1).reshape(1)
    state["token"] = jnp.zeros((1,), jnp.int32)

    def open_sum(name):
        sends = [state[f"s_{name}{i}"] for i in range(PIECES[name])]
        return Sum("dp", sends, state["k_" + name], step_order(name, count))

    call_down, call_up, call_attention, call_input = tails(last, fixed)
    state = call_down(state)
    down_sum = open_sum("down")
    state = call_up(state)
    up_sum = open_sum("up")
    down_sum.step(state)
    up_sum.step(state)
    state = call_attention(state)
    first_sum, second_sum = open_sum("first"), open_sum("second")
    down_sum.step(state)
    up_sum.step(state)
    first_sum.step(state)
    second_sum.step(state)
    state = call_input(state)
    first_sum.step(state)
    second_sum.step(state)
    token = state["token"].astype(F32)
    down_sum.step(state)
    up_sum.step(state)
    sums = dict(first=first_sum, second=second_sum, down=down_sum, up=up_sum)
    results = {}
    while sums:
        for name in list(sums):
            result = sums[name].step(state)
            if result is not None:
                results[name] = result
                del sums[name]
    down_grad, up_grad = results["down"], results["up"]
    kept[last] = {**kept[last], **{name: state[name] for name in SMALL + GRAD}}
    kept[last]["sm_b"] = state["sm_b"] + jnp.where(first == 1, state["sm_c"], 0.0)
    sm_a, sm_b, upb, diag = [sum(part[name] for part in kept) + token for name in SMALL]
    small = jnp.stack([sm_b[0], sm_b[1], sm_b[2], sm_a[0], sm_b[3], sm_a[1], sm_b[4], sm_a[2]])
    bucket = bucket_index(rows - jnp.arange(2 * rows))
    tables = jnp.dot(
        (bucket[None, :] == jnp.arange(BUCKETS)[:, None]).astype(F32), diag[:heads].T, precision=lax.Precision.HIGHEST
    )
    extras = jnp.concatenate(
        [
            small.reshape(8, count, own_rows).transpose(1, 0, 2).reshape(count, 8 * own_rows),
            upb[0].reshape(count, hidden // count),
            tables.reshape(count, heads * BUCKETS // count),
        ],
        axis=1,
    )
    extras = jnp.sum(jnp.where(state["token"] == 0, lax.all_to_all(extras, "dp", 0, 0, tiled=True), 0.0), axis=0)
    proj_grad = results["first"].reshape(1, 3, own_rows, width)
    out_grad = results["second"][None]
    small = extras[: 8 * own_rows].reshape(1, 8, own_rows)
    up_small = extras[8 * own_rows : 8 * own_rows + hidden // count][None]
    tab_small = extras[8 * own_rows + hidden // count :][None]
    stack = lambda name: jnp.stack([part[name] for part in kept])[None]
    return (
        *[stack(name) for name in OUT + GRAD],
        proj_grad,
        out_grad,
        up_grad[None],
        down_grad[None],
        up_small,
        small[:, 0:6],
        small[:, 6:8],
        tab_small,
    )


def solution(mesh):
    return jax.shard_map(
        body,
        mesh=mesh,
        in_specs=(
            P(None, "dp", None),
            P(None, "dp", None),
            P(None, "dp", None),
            P(None, "dp", None),
            P(None, "dp", None),
            P(None, "dp"),
            P(None, "dp"),
            P("section", None, None, None),
            P("section", None, None),
            P("section", None, None),
            P("section", None, None),
            P("section", None),
            P("section", None, None),
            P("section", None, None),
            P("section", None),
        ),
        out_specs=(
            P("section", None, "dp", None),
            P("section", None, "dp", None),
            P("section", None, "dp", None),
            P("section", None, "dp", None),
            P("section", None, "dp", None),
            P("section", "dp", None),
            P("section", "dp", None),
            P("section", "dp", None),
            P("section", "dp"),
            P("section", None, "dp"),
            P("section", None, "dp"),
            P("section", "dp"),
        ),
        check_vma=False,
    )
```

```python
from functools import partial

import jax
import jax.numpy as jnp
from jax import lax
from jax.experimental import pallas as pl
from jax.experimental.pallas import tpu as pltpu
from jax.sharding import PartitionSpec as P

LN_EPS = 1e-05
NEG_FILL = -1e30
BUCKET_EDGES = (12, 16, 23, 32, 46, 64, 91)
BUCKETS = 32
F32, BF16 = jnp.float32, jnp.bfloat16
VMEM_LIMIT = 60 * 1024 * 1024
STEP_LIMIT = 16 * 1024 * 1024
TAIL = (0.127414796, -0.142248368, 0.7107068705, -0.7265760135, 0.5307027145)
TAIL_SLOPE = 0.3275911 / 2**0.5
DENSITY = 0.3989422804014327


def nn(left, right):
    return jnp.dot(left, right, preferred_element_type=F32)


def nt(left, right):
    return lax.dot_general(left, right, (((1,), (1,)), ((), ())), preferred_element_type=F32)


def iota(shape, dim):
    return lax.broadcasted_iota(jnp.int32, shape, dim)


def bucket_index(relative):
    magnitude = jnp.abs(relative)
    far_part = jnp.full_like(magnitude, 8)
    for edge_at in BUCKET_EDGES:
        far_part = far_part + jnp.where(magnitude >= edge_at, 1, 0)
    near_far = jnp.where(magnitude < 8, magnitude, far_part)
    return near_far + jnp.where(relative > 0, 16, 0)


def gelu_and_slope(v):
    z = jnp.abs(v)
    t = 1.0 / (1.0 + TAIL_SLOPE * z)
    poly = TAIL[4]
    for coefficient in TAIL[3::-1]:
        poly = coefficient + t * poly
    bell = jnp.exp(-0.5 * (v * v))
    tail = t * poly * bell
    below = jnp.where(v >= 0, 1.0 - tail, tail)
    return v * below, below + DENSITY * (v * bell)


class Copies:
    def __init__(self, sems):
        self.sems, self.used, self.open = sems, 0, []

    def copy(self, src, dst, at):
        return pltpu.make_async_copy(src, dst, self.sems.at[at])

    def start(self, src, dst):
        copy = self.copy(src, dst, self.used)
        self.used += 1
        copy.start()
        return copy

    def out(self, src, dst):
        self.open.append((src, dst, self.used))
        self.start(src, dst)

    def finish(self):
        for src, dst, at in self.open:
            self.copy(src, dst, at).wait()


def head_map(entries, heads, span):
    entry = iota((16, entries), 1)
    own_head = (entry - heads * ((entry * 5462) >> 16)) == iota((16, entries), 0)
    bucket = bucket_index(span // 2 - iota((entries, span), 1))
    row = iota((entries, span), 0)
    own_bucket = (row >= heads * bucket) & (row < heads * bucket + heads)
    return own_head, own_bucket


def make_masks(lengths, order_ref, predicted_ref, m, rows):
    def place(shape, dim):
        token = iota(shape, dim)
        segment, start, end = jnp.zeros(shape, jnp.int32), jnp.zeros(shape, jnp.int32), 0
        for slot in range(lengths.shape[2]):
            size = lengths[m, 0, slot]
            end = end + size
            passed = token >= end
            segment = segment + jnp.where(passed, 1, 0)
            start = start + jnp.where(passed, size, 0)
        inside = token < end
        return jnp.where(inside, segment, -1 - token), inside & (token - start > 0)

    segment, later = place((1, rows), 1)
    order = order_ref[pl.ds(m, 1), :]
    flag = (predicted_ref[pl.ds(m, 1), :] > 0) & later
    gate = jnp.where(flag, order, -1).astype(F32)
    gate_column = jnp.transpose(jnp.broadcast_to(gate, (128, rows)))
    segment_column = jnp.transpose(jnp.broadcast_to(segment.astype(F32), (128, rows)))
    gate_column = jnp.concatenate([gate_column] * (rows // 128), axis=1)
    segment_column = jnp.concatenate([segment_column] * (rows // 128), axis=1)
    same = segment_column == segment.astype(F32)
    order = order.astype(F32)
    return [
        jnp.where(same & (gate_column <= order), 0.0, NEG_FILL),
        jnp.where(same & (gate_column < order), 0.0, NEG_FILL),
    ]


def tn(left, right):
    return lax.dot_general(left, right, (((0,), (0,)), ((), ())), preferred_element_type=F32)


UNROLL_HEADS = 12
UNROLL_CHUNKS = 6
UNROLL_BLOCKS = 8
STEP = 256
CHUNK = 512
BLOCK = 64


MATRIX = dict(wp="proj_weight", wo="out_weight", wu="up_weight", wd="down_weight")


def loop(count, unroll, body):
    def turn(i, carry):
        for j in range(unroll):
            body(i * unroll + j)
        return carry

    if unroll == count:
        for i in range(count):
            body(i)
    else:
        lax.fori_loop(0, count // unroll, turn, 0)


def loop_heads(heads, body):
    def turn(i, carry):
        for j in range(UNROLL_HEADS):
            body(i * UNROLL_HEADS + j, j % 2)
        return carry

    if UNROLL_HEADS == heads:
        turn(0, 0)
    else:
        lax.fori_loop(0, heads // UNROLL_HEADS, turn, 0)


def span_of(i, size):
    return pl.ds(i * size if isinstance(i, int) else pl.multiple_of(i * size, size), size)


class Layer:
    def __init__(self, m, dims, r, s, cp, parts):
        self.m, self.r, self.s, self.cp, self.parts = m, r, s, cp, parts
        self.rows, self.width, self.hidden, self.heads, self.micro, self.count = dims
        self.depth = self.width // self.heads
        self.span = 2 * self.rows
        self.mine = pl.ds(m * 2 * self.rows, 2 * self.rows)
        self.mine_half = pl.ds(m * self.rows, self.rows)
        self.waits, self.later = {}, False

    def load(self, name, src, dst):
        self.waits[name] = (src, dst, self.cp.used)
        self.cp.used += 1
        if not self.later:
            self.begin(name)

    def begin(self, *names):
        for name in names or self.waits:
            self.cp.copy(*self.waits[name]).start()

    def need(self, *names):
        for name in names:
            if name in self.waits:
                self.cp.copy(*self.waits.pop(name)).wait()

    def load_weights(self, *names):
        r, s = self.r, self.s
        for name in names:
            self.load(name, r[MATRIX[name]].at[0], s[name])

    def load_streams(self, name, content, query):
        rows, dst = self.rows, self.s[name]
        if content.shape[0] != rows:
            content, query = content.at[self.mine_half], query.at[self.mine_half]
        self.load(name + "0", content, dst.at[pl.ds(0, rows)])
        self.load(name + "1", query, dst.at[pl.ds(rows, rows)])

    def out_streams(self, name):
        for i, stream in enumerate("cq"):
            self.cp.out(self.s[name + "_s"].at[pl.ds(i * self.rows, self.rows)], self.r[f"{name}_{stream}"])

    def forward(self):
        r, s, cp = self.r, self.s, self.cp
        rows, width, heads, depth, span = self.rows, self.width, self.heads, self.depth, self.span
        keep = "back" not in self.parts
        biases, gains = r["biases"], r["gains"]
        s["mask"][0], s["mask"][1] = make_masks(r["lengths"], r["order"], r["predicted"], self.m, rows)
        own_head, own_bucket = head_map(heads * BUCKETS, heads, span)
        picked = jnp.where(own_head, r["rel_table"][...], 0.0)
        s["toep"][...] = jnp.dot(
            picked, jnp.where(own_bucket, 1.0, 0.0), precision=lax.Precision.HIGHEST, preferred_element_type=F32
        )
        self.need("x0", "x1", "wp")
        cp.out(s["x"], r["w_x"].at[self.mine])
        for n in range(0, width, STEP):
            at = slice(n, n + STEP)
            q = nn(s["x"][...], s["wp"][0, :, at]) + biases[0, 0:1, at]
            s["q_t"][at, :] = jnp.transpose(q.astype(BF16) * 0.125)
        for n in range(0, width, STEP):
            at = slice(n, n + STEP)
            k = nn(s["x"][0:rows, :], s["wp"][1, :, at]).astype(BF16)
            s["k"][:, at] = k
            s["k_t"][at, :] = jnp.transpose(k)
            v = (nn(s["x"][0:rows, :], s["wp"][2, :, at]) + biases[0, 1:2, at]).astype(BF16)
            s["v"][:, at] = v
            s["v_t"][at, :] = jnp.transpose(v)
        blank = jnp.zeros((depth, 2 * rows), BF16)
        def head_step(head, odd):
            pair = span_of((head - odd) // 2, 2 * depth)
            at = span_of(head, depth)
            q_head = s["q_t"][at, :]
            stacked = jnp.concatenate([blank, q_head] if odd else [q_head, blank], axis=0)
            scores = nn(s["k"][:, pair], stacked)
            line = jnp.broadcast_to(s["toep"][pl.ds(head, 1), :], (rows, span))
            rel = pltpu.roll(line, rows, 1, stride=1, stride_axis=0)[:, :rows]
            for i in range(2):
                lanes = slice(i * rows, (i + 1) * rows)
                logits = scores[:, lanes] + rel + s["mask"][i]
                e = jnp.exp(logits - jnp.max(logits, axis=0, keepdims=True))
                inv = 1.0 / jnp.sum(e, axis=0, keepdims=True)
                e = e.astype(BF16)
                s["e"][i, head] = e
                s["inv"][i, pl.ds(head, 1), :] = inv
                s["mix_t"][at, lanes] = (nn(s["v_t"][at, :], e) * inv).astype(BF16)
        loop_heads(heads, head_step)
        if keep:
            for name in ("q_t", "k", "k_t", "v", "e", "inv"):
                cp.out(s[name], r[name])
        cp.out(s["mix_t"], r["w_mix_t"].at[:, self.mine])
        for n in range(0, width, STEP):
            s["mix"][:, n:n + STEP] = jnp.transpose(s["mix_t"][n:n + STEP, :])
        self.need("wo", "wu", "wd")
        for n in range(0, width, STEP):
            s["sum"][:, n:n + STEP] = nn(s["mix"][...], s["wo"][:, n:n + STEP])
        def block_step(n):
            at = span_of(n, BLOCK)
            summed = s["x"][at, :].astype(F32) + s["sum"][at, :] + biases[0, 2:3, :]
            center = summed - jnp.mean(summed, axis=1, keepdims=True)
            scale = lax.rsqrt(jnp.mean(center * center, axis=1, keepdims=True) + LN_EPS)
            xhat = center * scale
            normed = xhat * gains[0, 0:1, :] + biases[0, 4:5, :]
            s["xh"][0, at, :] = xhat.astype(BF16)
            s["rs"][0, at, :] = jnp.broadcast_to(scale, (BLOCK, 128))
            s["nl"][at, :] = normed.astype(BF16)
            s["sum"][at, :] = normed + biases[0, 3:4, :]
        loop(2 * self.rows // BLOCK, UNROLL_BLOCKS, block_step)
        if keep:
            cp.out(s["xh"].at[0], r["xhat"].at[0])
            cp.out(s["rs"].at[0], r["scale"].at[0])
        cp.out(s["nl"], r["w_nl"].at[self.mine])
        def chunk_step(j):
            at = span_of(j, CHUNK)
            act, slope = gelu_and_slope(nn(s["nl"][...], s["wu"][:, at]) + r["up_bias"][0:1, at])
            s["act"][:, at] = act.astype(BF16)
            s["gp"][:, at] = slope.astype(BF16)
        loop(self.hidden // CHUNK, UNROLL_CHUNKS, chunk_step)
        cp.out(s["act"], r["w_act"].at[self.mine])
        if keep:
            cp.out(s["gp"], r["gp"])
        for n in range(0, width, STEP):
            s["sum"][:, n:n + STEP] += nn(s["act"][...], s["wd"][:, n:n + STEP])
        def block_step(n):
            at = span_of(n, BLOCK)
            total = s["sum"][at, :]
            center = total - jnp.mean(total, axis=1, keepdims=True)
            scale = lax.rsqrt(jnp.mean(center * center, axis=1, keepdims=True) + LN_EPS)
            xhat = center * scale
            s["xh"][1, at, :] = xhat.astype(BF16)
            s["rs"][1, at, :] = jnp.broadcast_to(scale, (BLOCK, 128))
            s["out_s"][at, :] = (xhat * gains[0, 1:2, :] + biases[0, 5:6, :]).astype(BF16)
        loop(2 * self.rows // BLOCK, UNROLL_BLOCKS, block_step)
        self.out_streams("out")
        if keep:
            cp.out(s["xh"].at[1], r["xhat"].at[1])
            cp.out(s["rs"].at[1], r["scale"].at[1])

    def norm_back(self, which, grad, at, gain_sum, shift_sum):
        s = self.s
        xhat = s["xh"][which, at, :].astype(F32)
        ref, row = gain_sum
        s[ref][row:row + 1, :] += jnp.sum(grad * xhat, axis=0, keepdims=True)
        ref, row = shift_sum
        s[ref][row:row + 1, :] += jnp.sum(grad, axis=0, keepdims=True)
        scaled = grad * self.r["gains"][0, which:which + 1, :]
        mean_a = jnp.mean(scaled, axis=1, keepdims=True)
        mean_b = jnp.mean(scaled * xhat, axis=1, keepdims=True)
        return (scaled - mean_a - xhat * mean_b) * s["rs"][which, at, 0:1]

    def back_norm_two(self, dz):
        s = self.s
        s["sm_a"][...] = jnp.zeros(s["sm_a"].shape, F32)
        self.need("g0", "g1", "xh1", "rs1")
        def block_step(n):
            at = span_of(n, BLOCK)
            back = self.norm_back(1, s["g"][at, :].astype(F32), at, ("sm_a", 2), ("sm_a", 1))
            s["grad"][at, :] = back
            low = back.astype(BF16)
            dz[at, :] = low
            s["sm_a"][0:1, :] += jnp.sum(low.astype(F32), axis=0, keepdims=True)
        loop(2 * self.rows // BLOCK, UNROLL_BLOCKS, block_step)
        self.cp.out(dz, self.r["w_dz"].at[self.mine])
        self.cp.out(s["sm_a"], self.r["sm_a"])

    def back_up(self, dz, dpre):
        s = self.s
        self.need("wd")
        self.need("gp")
        def chunk_step(j):
            at = span_of(j, CHUNK)
            d_act = nt(dz[...], s["wd"][at, :])
            d_pre = (d_act * s["gp"][:, at].astype(F32)).astype(BF16)
            dpre[:, at] = d_pre
            s["upb"][0:1, at] = jnp.sum(d_pre.astype(F32), axis=0, keepdims=True)
        loop(self.hidden // CHUNK, UNROLL_CHUNKS, chunk_step)
        self.cp.out(dpre, self.r["w_dpre"].at[self.mine])
        self.cp.out(s["upb"], self.r["upb"])

    def back_norm_one(self, dpre, da):
        s = self.s
        s["sm_b"][...] = jnp.zeros(s["sm_b"].shape, F32)
        self.need("wu")
        for n in range(0, self.width, STEP):
            s["sum"][:, n:n + STEP] = nt(dpre[...], s["wu"][n:n + STEP, :])
        self.need("xh0", "rs0", "grad")
        def block_step(n):
            at = span_of(n, BLOCK)
            back = self.norm_back(0, s["grad"][at, :] + s["sum"][at, :], at, ("sm_b", 4), ("sm_b", 3))
            s["grad"][at, :] = back
            low = back.astype(BF16)
            da[at, :] = low
            s["sm_b"][2:3, :] += jnp.sum(low.astype(F32), axis=0, keepdims=True)
        loop(2 * self.rows // BLOCK, UNROLL_BLOCKS, block_step)
        self.cp.out(da, self.r["w_da"].at[self.mine])

    def back_attention(self, da, dq, dk, dv):
        s, cp, r = self.s, self.cp, self.r
        rows, width, heads, depth, span = self.rows, self.width, self.heads, self.depth, self.span
        self.need("wo", "inv")
        for n in range(0, width, STEP):
            d_mix = nt(s["wo"][n:n + STEP, :], da[...])
            for h in range(n // depth, (n + STEP) // depth):
                inv = jnp.concatenate([s["inv"][i, h:h + 1, :] for i in range(2)], axis=1)
                s["dm_t"][h * depth:(h + 1) * depth, :] = (d_mix[h * depth - n:(h + 1) * depth - n, :] * inv).astype(BF16)
        self.need("e", "q_t", "k", "k_t", "v")
        blank = jnp.zeros((depth, 2 * rows), BF16)
        s["diag"][...] = jnp.zeros(s["diag"].shape, F32)
        def head_step(head, odd):
            pair = span_of((head - odd) // 2, 2 * depth)
            at = span_of(head, depth)
            dm_head = s["dm_t"][at, :]
            stacked = jnp.concatenate([blank, dm_head] if odd else [dm_head, blank], axis=0)
            d_prob = nn(s["v"][:, pair], stacked)
            parts, whole = [], 0.0
            for i in range(2):
                e = s["e"][i, head].astype(F32)
                part = d_prob[:, i * rows:(i + 1) * rows]
                mean = jnp.sum(e * part, axis=0, keepdims=True) * s["inv"][i, pl.ds(head, 1), :]
                d_score = (e * (part - mean)).astype(BF16)
                parts.append(d_score)
                whole = whole + d_score.astype(F32)
            both = jnp.concatenate(parts, axis=1)
            e_both = jnp.concatenate([s["e"][0, head], s["e"][1, head]], axis=1)
            s["dq_t"][at, :] = (nn(s["k_t"][at, :], both) * 0.125).astype(BF16)
            s["dv_t"][at, :] = nt(dm_head, e_both).astype(BF16)
            s["dk_t"][at, :] = nt(s["q_t"][at, :], both).astype(BF16)
            wide = jnp.concatenate([jnp.zeros_like(whole), whole], axis=1)
            count = rows
            while count > 8:
                count //= 2
                wide = wide[:count, :] + pltpu.roll(wide[count:, :], span - count, 1)
            line = wide[0:1, :]
            for k in range(1, 8):
                line = line + pltpu.roll(wide, span - k, 1)[k:k + 1, :]
            s["diag"][pl.ds(head, 1), :] = line
        loop_heads(heads, head_step)
        for n in range(0, width, STEP):
            at = slice(n, n + STEP)
            part = jnp.transpose(s["dq_t"][at, :])
            dq[:, at] = part
            s["sm_b"][0:1, at] = jnp.sum(part.astype(F32), axis=0, keepdims=True)
            dk[:, at] = jnp.transpose(s["dk_t"][at, :])
            part = jnp.transpose(s["dv_t"][at, :])
            dv[:, at] = part
            s["sm_b"][1:2, at] = jnp.sum(part.astype(F32), axis=0, keepdims=True)
        cp.out(dq, r["w_dq"].at[self.mine])
        cp.out(dk, r["w_dk"].at[self.mine_half])
        cp.out(dv, r["w_dv"].at[self.mine_half])
        cp.out(s["sm_b"], r["sm_b"])
        cp.out(s["diag"], r["diag"])

    def back_input(self, dq, dk, dv):
        s, rows = self.s, self.rows
        self.need("wp")
        for n in range(0, self.width, STEP):
            at = slice(n, n + STEP)
            back = s["grad"][:, at] + nt(dq[...], s["wp"][0, at, :])
            more = nt(dk[...], s["wp"][1, at, :]) + nt(dv[...], s["wp"][2, at, :])
            s["grad_s"][0:rows, at] = (back[0:rows, :] + more).astype(BF16)
            s["grad_s"][rows:, at] = back[rows:, :].astype(BF16)
        self.out_streams("grad")


def run_forward(layer):
    layer.load_streams("x", layer.r["xc"], layer.r["xq"])
    layer.load_weights("wp", "wo", "wu", "wd")
    layer.forward()
    layer.cp.finish()


def run_backward(layer):
    r, s = layer.r, layer.s
    layer.load_streams("g", r["gc"], r["gq"])
    for i in (1, 0):
        layer.load(f"xh{i}", r["xhat"].at[i], s["xh"].at[i])
        layer.load(f"rs{i}", r["scale"].at[i], s["rs"].at[i])
    layer.load_weights("wd")
    layer.load("gp", r["gp"], s["gp"])
    layer.load_weights("wu", "wo")
    for name in ("inv", "e", "q_t", "k", "k_t", "v"):
        layer.load(name, r[name], s[name])
    layer.load_weights("wp")
    all_back(layer)
    layer.cp.finish()


def all_back(layer):
    s = layer.s
    layer.back_norm_two(s["dz"])
    layer.back_up(s["dz"], s["dpre"])
    layer.back_norm_one(s["dpre"], s["da"])
    layer.back_attention(s["da"], s["dq"], s["dk"], s["dv"])
    layer.back_input(s["dq"], s["dk"], s["dv"])


def run_both(layer):
    layer.load_streams("x", layer.r["xc"], layer.r["xq"])
    layer.load_weights("wp", "wo", "wu", "wd")
    layer.load_streams("g", layer.r["gc"], layer.r["gq"])
    layer.forward()
    all_back(layer)
    layer.cp.finish()


def step_order(name, count):
    straight = list(range(1, count.bit_length() - 1))
    return straight[1:] + straight[:1] if name in TURNED else straight


def part_at(name, device, count):
    at = 0
    for bit in step_order(name, count):
        at = 2 * at + (device >> bit & 1)
    return at


def emit(layer, name, first, columns, value):
    parts = layer.s["G_" + name]
    size = value.shape[0] // layer.count
    for device in range(layer.count):
        rows = value[device * size:(device + 1) * size, :].astype(BF16)
        parts[part_at(name, device, layer.count), device % 2, first:first + size, columns] = rows


TURNED = ("up",)
PIECES = dict(down=1, up=4, first=3, second=1)


def sent(*names):
    return tuple(f"s_{name}{i}" for name in names for i in range(PIECES[name])) + tuple("k_" + name for name in names)


def send_piece(layer, name, i):
    core = layer.r["core"][0]
    columns = layer.r[f"s_{name}{i}"].shape[2]
    at = pl.ds(i * columns, columns)
    layer.cp.out(layer.s["G_" + name].at[:, 1 - core, :, at], layer.r[f"s_{name}{i}"])
    layer.cp.out(layer.s["G_" + name].at[:, core, :, at], layer.r["k_" + name].at[:, :, at])


def tail_down(layer):
    r, s, cp = layer.r, layer.s, layer.cp
    active = r["active"][0] == 1
    other = pl.ds((1 - layer.m) * 2 * layer.rows, 2 * layer.rows)
    mine = s["W_dz"].at[layer.mine]

    layer.later = True
    layer.load_streams("g", r["gc"], r["gq"])
    layer.load("xh1", r["xhat"].at[1], s["xh"].at[1])
    layer.load("rs1", r["scale"].at[1], s["rs"].at[1])
    layer.later = False

    @pl.when(active)
    def _():
        layer.begin()

    layer.load("act", r["w_act"], s["W_act"])
    layer.load("other", r["w_dz"].at[other], s["W_dz"].at[other])

    @pl.when(active)
    def _():
        layer.back_norm_two(mine)
        cp.out(s["grad"], r["d_total"])

    opened, cp.open = cp.open, []

    @pl.when(jnp.logical_not(active))
    def _():
        cp.start(r["w_dz"].at[layer.mine], mine).wait()

    layer.need("act", "other")
    size = layer.hidden // layer.count
    for n in range(0, layer.hidden, 2 * size):
        both = tn(s["W_act"][:, n:n + 2 * size], s["W_dz"][...]).astype(BF16)
        at = part_at("down", n // size, layer.count)
        s["G_down"][at, 0] = both[:size]
        s["G_down"][at, 1] = both[size:]
    send_piece(layer, "down", 0)

    @pl.when(active)
    def _():
        for src, dst, at in opened:
            cp.copy(src, dst, at).wait()

    cp.finish()


def tail_up(layer):
    r, s, cp = layer.r, layer.s, layer.cp
    active = r["active"][0] == 1
    other = pl.ds((1 - layer.m) * 2 * layer.rows, 2 * layer.rows)
    mine = s["W_dpre"].at[layer.mine]

    layer.later = True
    layer.load("dz", r["w_dz"].at[layer.mine], s["dz"])
    layer.load_weights("wd")
    layer.load("gp", r["gp"], s["gp"])
    layer.load_weights("wu")
    layer.load("grad", r["d_total"], s["grad"])
    layer.load("xh0", r["xhat"].at[0], s["xh"].at[0])
    layer.load("rs0", r["scale"].at[0], s["rs"].at[0])
    layer.later = False

    @pl.when(active)
    def _():
        layer.begin("dz", "wd", "gp", "wu", "grad", "xh0", "rs0")

    layer.load("nl", r["w_nl"], s["W_nl"])
    layer.load("other", r["w_dpre"].at[other], s["W_dpre"].at[other])

    @pl.when(active)
    def _():
        layer.need("dz")
        layer.back_up(s["dz"], mine)

    opened, cp.open = cp.open, []

    @pl.when(jnp.logical_not(active))
    def _():
        cp.start(r["w_dpre"].at[layer.mine], mine).wait()

    layer.need("nl", "other")
    for n in range(0, layer.width, STEP):
        at = slice(n, n + STEP)
        s["T_nl"][at, :] = jnp.transpose(s["W_nl"][:, at])
    for n in range(0, layer.hidden, CHUNK):
        emit(layer, "up", 0, slice(n, n + CHUNK), nn(s["T_nl"][...], s["W_dpre"][:, n:n + CHUNK]))
    for i in range(PIECES["up"]):
        send_piece(layer, "up", i)
    sends, cp.open = cp.open, opened

    @pl.when(active)
    def _():
        layer.back_norm_one(mine, s["da"])
        cp.out(s["grad"], r["d_summed"])
        cp.out(s["sm_b"], r["sm_c"])
        cp.finish()

    cp.open = sends
    cp.finish()


def tail_attention(layer):
    r, s, cp = layer.r, layer.s, layer.cp
    rows = layer.rows
    active = r["active"][0] == 1
    other = pl.ds((1 - layer.m) * 2 * rows, 2 * rows)
    other_half = pl.ds((1 - layer.m) * rows, rows)
    places = (
        ("dq", layer.mine, other), ("dk", layer.mine_half, other_half), ("dv", layer.mine_half, other_half),
    )
    mine = {name: s["W_" + name].at[own] for name, own, _ in places}

    layer.load("da", r["w_da"], s["W_da"])
    layer.later = True
    layer.load_weights("wo")
    for name in ("inv", "e", "q_t", "k", "k_t", "v"):
        layer.load(name, r[name], s[name])
    layer.later = False

    @pl.when(active)
    def _():
        layer.begin("wo", "inv", "e", "q_t", "k", "k_t", "v")

    layer.load("x", r["w_x"], s["W_x"])
    layer.load("mix", r["w_mix_t"], s["W_mix_t"])
    for name, _, far in places:
        layer.load("other" + name, r["w_" + name].at[far], s["W_" + name].at[far])
    layer.need("da")

    @pl.when(active)
    def _():
        s["sm_b"][...] = jnp.zeros(s["sm_b"].shape, F32)
        layer.back_attention(s["W_da"].at[layer.mine], mine["dq"], mine["dk"], mine["dv"])

    opened, cp.open = cp.open, []

    @pl.when(jnp.logical_not(active))
    def _():
        copies = [cp.start(r["w_" + name].at[own], mine[name]) for name, own, _ in places]
        for copy in copies:
            copy.wait()

    layer.need("x", "mix", *["other" + name for name, _, _ in places])
    for n in range(0, layer.width, STEP):
        at = slice(n, n + STEP)
        s["T_x"][at, :] = jnp.transpose(s["W_x"][:, at])
    content = jnp.concatenate([s["T_x"][:, m * 2 * rows:(m * 2 + 1) * rows] for m in range(layer.micro)], axis=1)
    size = layer.width // layer.count
    for n in range(0, layer.width, STEP):
        at = slice(n, n + STEP)
        emit(layer, "first", 0, at, nn(s["T_x"][...], s["W_dq"][:, at]))
        emit(layer, "first", size, at, nn(content, s["W_dk"][:, at]))
        emit(layer, "first", 2 * size, at, nn(content, s["W_dv"][:, at]))
        emit(layer, "second", 0, at, nn(s["W_mix_t"][...], s["W_da"][:, at]))
        send_piece(layer, "first", n // STEP)
    send_piece(layer, "second", 0)

    @pl.when(active)
    def _():
        for src, dst, at in opened:
            cp.copy(src, dst, at).wait()

    cp.finish()


def tail_input(layer):
    r, s = layer.r, layer.s
    layer.load_weights("wp")
    layer.load("grad", r["d_summed"], s["grad"])
    layer.load("dq", r["w_dq"].at[layer.mine], s["dq"])
    layer.load("dk", r["w_dk"].at[layer.mine_half], s["dk"])
    layer.load("dv", r["w_dv"].at[layer.mine_half], s["dv"])
    layer.need("grad", "dq", "dk", "dv")
    layer.back_input(s["dq"], s["dk"], s["dv"])
    layer.cp.finish()


def scratch_shapes(dims):
    rows, width, hidden, heads, micro, count = dims
    both, all_rows = 2 * rows, 2 * rows * micro
    low = {
        "x": (both, width), "wp": (3, width, width), "wo": (width, width), "wu": (width, hidden),
        "wd": (hidden, width), "q_t": (width, both), "k": (rows, width), "k_t": (width, rows),
        "v": (rows, width), "v_t": (width, rows), "e": (2, heads, rows, rows), "mix_t": (width, both),
        "mix": (both, width), "nl": (both, width), "act": (both, hidden), "gp": (both, hidden),
        "xh": (2, both, width), "out_s": (both, width), "g": (both, width), "dz": (both, width),
        "dpre": (both, hidden), "da": (both, width), "dm_t": (width, both), "dq_t": (width, both),
        "dk_t": (width, rows), "dv_t": (width, rows), "dq": (both, width), "dk": (rows, width),
        "dv": (rows, width), "grad_s": (both, width),
    }
    high = {
        "mask": (2, rows, rows), "toep": (16, both), "inv": (2, 16, rows), "sum": (both, width),
        "rs": (2, both, 128), "grad": (both, width), "sm_a": (8, width), "sm_b": (8, width),
        "upb": (8, hidden), "diag": (16, both),
    }
    low.update({"W_" + name[2:]: dims for name, dims in stored_shapes(dims).items()})
    low.update({"G_" + name: (count // 2, 2) + part for name, part in sum_shapes(dims).items()})
    low.update({"T_x": (width, all_rows), "T_nl": (width, all_rows)})
    shapes = {name: pltpu.VMEM(dims, BF16) for name, dims in low.items()}
    shapes.update({name: pltpu.VMEM(dims, F32) for name, dims in high.items()})
    return shapes


WEIGHTS = ("wp", "wo", "wu", "wd")
FORWARD = WEIGHTS + (
    "x", "q_t", "k", "k_t", "v", "v_t", "mask", "toep", "e", "inv", "mix_t", "mix", "sum", "nl", "act", "gp", "xh",
    "rs", "out_s",
)
BACKWARD = WEIGHTS + (
    "g", "q_t", "k", "k_t", "v", "e", "inv", "gp", "xh", "rs", "grad", "dz", "dpre", "sum", "da", "dm_t", "dq_t",
    "dk_t", "dv_t", "dq", "dk", "dv", "sm_a", "sm_b", "upb", "diag", "grad_s",
)
KEPT = ("q_t", "k", "k_t", "v", "e", "inv", "gp", "xhat", "scale")
OUT, GRAD = ("out_c", "out_q"), ("grad_c", "grad_q")
SMALL = ("sm_a", "sm_b", "upb", "diag")


def kept_shapes(dims):
    rows, width, hidden, heads, micro, count = dims
    both = 2 * rows
    low = {
        "q_t": (width, both), "k": (rows, width), "k_t": (width, rows), "v": (rows, width),
        "e": (2, heads, rows, rows), "gp": (both, hidden), "xhat": (2, both, width), "out_c": (rows, width),
        "out_q": (rows, width), "grad_c": (rows, width), "grad_q": (rows, width),
    }
    high = {
        "inv": (2, 16, rows), "scale": (2, both, 128), "sm_a": (8, width), "sm_b": (8, width),
        "upb": (8, hidden), "diag": (16, both), "d_total": (both, width), "d_summed": (both, width),
        "sm_c": (8, width),
    }
    return low, high


def stored_shapes(dims):
    rows, width, hidden, heads, micro, count = dims
    wide = 2 * rows * micro
    return {
        "w_x": (wide, width), "w_mix_t": (width, wide), "w_nl": (wide, width), "w_act": (wide, hidden),
        "w_dz": (wide, width), "w_dpre": (wide, hidden), "w_da": (wide, width), "w_dq": (wide, width),
        "w_dk": (wide // 2, width), "w_dv": (wide // 2, width),
    }


def sum_shapes(dims):
    rows, width, hidden, heads, micro, count = dims
    own, wide = width // count, hidden // count
    return {"down": (wide, width), "up": (own, hidden), "first": (3 * own, width), "second": (own, width)}


SMEM = pl.BlockSpec(memory_space=pltpu.SMEM)
VMEM = pl.BlockSpec(memory_space=pltpu.VMEM)
ANY = pl.BlockSpec(memory_space=pl.ANY)
SPECS = dict(
    active=SMEM, core=SMEM, token=SMEM, lengths=SMEM, order=VMEM, predicted=VMEM, rel_table=VMEM, up_bias=VMEM, biases=VMEM, gains=VMEM
)


def kernel(run, m, dims, parts, names_in, names_out, names_scratch, *refs):
    r = dict(zip(names_in, refs))
    refs = refs[len(names_in):]
    r.update(zip(names_out, refs))
    refs = refs[len(names_out):]
    s = dict(zip(names_scratch, refs))
    cp = Copies(refs[len(names_scratch)])

    if "token" in r:
        r["token"][0] = 0
    if "tail" in parts:
        run(Layer(m, dims, r, s, cp, parts))
        return

    @pl.when(r["active"][0] == 1)
    def _():
        run(Layer(m, dims, r, s, cp, parts))


def call(run, m, fixed, parts, state, reads, writes, names_scratch, flops, copies):
    dims = fixed["dims"]
    low, high = kept_shapes(dims)
    shapes = {name: jax.ShapeDtypeStruct(dims, BF16) for name, dims in {**low, **stored_shapes(dims)}.items()}
    shapes.update({name: jax.ShapeDtypeStruct(dims, F32) for name, dims in high.items()})
    shapes["token"] = jax.ShapeDtypeStruct((1,), jnp.int32)
    for name, part in sum_shapes(dims).items():
        piece = (part[0], part[1] // PIECES[name])
        for i in range(PIECES[name]):
            shapes[f"s_{name}{i}"] = jax.ShapeDtypeStruct((dims[5] // 2,) + piece, BF16)
        shapes["k_" + name] = jax.ShapeDtypeStruct((dims[5] // 2,) + part, BF16)
    passed = [name for name in writes if name in state]
    made = [name for name in writes if name not in state]
    names_in = [name for name in reads if name not in passed]
    made += ["token"] * ("token" in state)
    names_in += ["old_token"] * ("token" in state)
    operands = [state[name.removeprefix("old_")] for name in names_in]
    all_scratch = scratch_shapes(dims)
    outs = pl.pallas_call(
        partial(
            kernel, run, m, dims, parts, names_in + ["old_" + name for name in passed], passed + made, names_scratch
        ),
        in_specs=[SPECS.get(name, ANY) for name in names_in] + [ANY] * len(passed),
        out_specs=[SPECS.get(name, ANY) for name in passed + made],
        out_shape=[shapes[name] for name in passed + made],
        scratch_shapes=[all_scratch[name] for name in names_scratch] + [pltpu.SemaphoreType.DMA((copies,))],
        input_output_aliases={len(operands) + i: i for i in range(len(passed))},
        compiler_params=pltpu.CompilerParams(vmem_limit_bytes=VMEM_LIMIT),
        cost_estimate=pl.CostEstimate(flops=flops, bytes_accessed=1_000, transcendentals=0),
    )(*operands, *[state[name] for name in passed])
    return {**state, **dict(zip(passed + made, outs))}


INPUTS = ("active", "lengths", "order", "predicted", "rel_table", "up_bias", "biases", "gains")
MATRICES = ("proj_weight", "out_weight", "up_weight", "down_weight")
FORWARD_STORE = ("w_x", "w_mix_t", "w_nl", "w_act")
BACKWARD_STORE = ("w_dz", "w_dpre", "w_da", "w_dq", "w_dk", "w_dv")


def forward(m, fixed, state):
    return call(
        run_forward, m, fixed, ("fwd",), state, INPUTS + MATRICES + ("xc", "xq"), KEPT + OUT + FORWARD_STORE,
        FORWARD, 8_000_000_000, 64,
    )


def backward(m, fixed, state):
    return call(
        run_backward, m, fixed, ("back",), state, ("active", "gains") + MATRICES + ("gc", "gq") + KEPT,
        GRAD + SMALL + BACKWARD_STORE, BACKWARD, 8_000_000_000, 64,
    )


def forward_backward(m, fixed, state):
    scratch = FORWARD + tuple(name for name in BACKWARD if name not in FORWARD)
    return call(
        run_both, m, fixed, ("fwd", "back"), state, INPUTS + MATRICES + ("xc", "xq", "gc", "gq"),
        OUT + GRAD + SMALL + FORWARD_STORE + BACKWARD_STORE, scratch, 16_000_000_000, 80,
    )


def tails(m, fixed):
    flags = ("active", "core")
    return (
        lambda state: call(
            tail_down, m, fixed, ("tail", "back"), state, flags + ("gains", "gc", "gq", "xhat", "scale", "w_act"),
            ("w_dz", "sm_a", "d_total") + sent("down"),
            ("g", "xh", "rs", "grad", "sm_a", "W_act", "W_dz", "G_down"), 1_000, 24,
        ),
        lambda state: call(
            tail_up, m, fixed, ("tail", "back"), state,
            flags + ("gains", "down_weight", "up_weight", "gp", "w_nl", "w_dz", "d_total", "xhat", "scale"),
            ("w_dpre", "upb", "w_da", "sm_c", "d_summed") + sent("up"),
            (
                "dz", "wd", "gp", "upb", "wu", "grad", "sum", "xh", "rs", "da", "sm_b", "W_nl", "T_nl", "W_dpre",
                "G_up",
            ),
            1_000, 24,
        ),
        lambda state: call(
            tail_attention, m, fixed, ("tail", "back"), state,
            flags + ("out_weight", "w_x", "w_mix_t", "w_da", "inv", "e", "q_t", "k", "k_t", "v"),
            ("w_dq", "w_dk", "w_dv", "sm_b", "diag") + sent("first", "second"),
            (
                "wo", "inv", "e", "q_t", "k", "k_t", "v", "dm_t", "dq_t", "dk_t", "dv_t", "sm_b", "diag", "W_x",
                "T_x", "W_mix_t", "W_da", "W_dq", "W_dk", "W_dv", "G_first", "G_second",
            ),
            1_000, 48,
        ),
        lambda state: call(
            tail_input, m, fixed, ("back",), state,
            ("active", "proj_weight", "d_summed", "w_dq", "w_dk", "w_dv"), GRAD,
            ("wp", "grad", "dq", "dk", "dv", "grad_s"), 1_000, 16,
        ),
    )


def step_kernel(ends, pieces, refs):
    own, token, keep, *refs = refs
    come, refs = refs[:pieces], refs[pieces:]
    outs, (keep_s, come_s, sum_s, sems) = refs[:-4], refs[-4:]
    outs[-1][0] = 0
    count, _, columns = keep.shape
    columns //= pieces
    if ends:
        places = [0]
    else:
        half = count // 2
        places = [(1 - own[0]) * half + i for i in range(half)] + [own[0] * half + i for i in range(half)]
    copies, each = [], pieces + 1
    for i, p in enumerate(places):
        copies.append(pltpu.make_async_copy(keep.at[p], keep_s.at[i], sems.at[each * i]))
        for j in range(pieces):
            part = come_s.at[i, :, pl.ds(j * columns, columns)]
            copies.append(pltpu.make_async_copy(come[j].at[p], part, sems.at[each * i + j + 1]))
    for copy in copies:
        copy.start()
    back = []
    for i in range(count):
        for copy in copies[each * i:each * (i + 1)]:
            copy.wait()
        sum_s[i] = (keep_s[i].astype(F32) + come_s[i].astype(F32)).astype(sum_s.dtype)
        half = max(count // 2, 1)
        back.append(pltpu.make_async_copy(sum_s.at[i], outs[i // half].at[i % half], sems.at[each * count + i]))
        back[-1].start()
    for copy in back:
        copy.wait()


def step(state, keep, come, own):
    ends = own is None
    count, rows, columns = keep.shape
    own = jnp.zeros((1,), jnp.int32) if ends else own.reshape(1)
    half = jax.ShapeDtypeStruct((max(count // 2, 1), rows, columns), F32 if ends else keep.dtype)
    small = keep.size * keep.dtype.itemsize < 1_500_000
    outs = pl.pallas_call(
        lambda *refs: step_kernel(ends, len(come), refs),
        in_specs=[SMEM, SMEM, ANY] + [ANY] * len(come),
        out_specs=[ANY] * (2 - ends) + [SMEM],
        out_shape=[half] * (2 - ends) + [jax.ShapeDtypeStruct((1,), jnp.int32)],
        scratch_shapes=[
            pltpu.VMEM(keep.shape, keep.dtype),
            pltpu.VMEM(keep.shape, keep.dtype),
            pltpu.VMEM(keep.shape, half.dtype),
            pltpu.SemaphoreType.DMA(((2 + len(come)) * count,)),
        ],
        compiler_params=pltpu.CompilerParams(vmem_limit_bytes=STEP_LIMIT if small else VMEM_LIMIT),
        cost_estimate=pl.CostEstimate(flops=1_000, bytes_accessed=1_000, transcendentals=0),
    )(own, state["token"], keep, *come)
    state["token"] = outs[-1]
    return outs[:-1]


class Sum:
    def __init__(self, axis, send, keep, order):
        self.axis, self.order = axis, list(order)
        self.place = lax.axis_index(axis)
        self.send(send, keep, 0)

    def send(self, send, keep, bit):
        route = [(device, device ^ (1 << bit)) for device in range(lax.axis_size(self.axis))]
        self.keep, self.come = keep, [lax.ppermute(part, self.axis, route) for part in send]

    def step(self, state=None):
        if not self.order and state is not None:
            return step(state, self.keep, self.come, None)[0][0]
        if not self.order:
            return self.keep[0].astype(F32) + self.come[0][0].astype(F32)
        bit = self.order.pop(0)
        own = (self.place >> bit) & 1
        if state is not None:
            send, keep = step(state, self.keep, self.come, own)
        else:
            come = jnp.concatenate(self.come, axis=2) if len(self.come) > 1 else self.come[0]
            half = come.shape[0] // 2
            total = lambda at: (
                lax.dynamic_slice_in_dim(self.keep, at * half, half).astype(F32)
                + lax.dynamic_slice_in_dim(come, at * half, half).astype(F32)
            ).astype(BF16)
            send, keep = total(1 - own), total(own)
        self.send([send], keep, bit)


def body(
    content_in,
    query_in,
    content_cot,
    query_cot,
    lengths,
    order,
    predicted,
    proj_weight,
    out_weight,
    up_weight,
    down_weight,
    up_bias,
    biases,
    gains,
    rel_table,
):
    micro, rows, width = content_in.shape
    hidden = up_bias.shape[1]
    heads = rel_table.shape[1] // BUCKETS
    first = (lax.axis_index("section") == 0).astype(jnp.int32).reshape(1)
    second = 1 - first
    state = dict(
        lengths=lengths,
        order=order,
        predicted=predicted,
        proj_weight=proj_weight,
        out_weight=out_weight,
        up_weight=up_weight,
        down_weight=down_weight,
        up_bias=up_bias,
        biases=biases,
        gains=gains,
        rel_table=rel_table,
    )
    fixed = dict(dims=(rows, width, hidden, heads, micro, lax.axis_size("dp")))
    flat = lambda a: a.reshape(micro * rows, width)
    stored = BACKWARD_STORE + FORWARD_STORE
    own = KEPT + OUT + GRAD + SMALL
    kept = [{} for m in range(micro)]
    store = {}

    def run(function, m, active, **more):
        after = function(m, fixed, {**state, **kept[m], **store, "active": active, **more})
        kept[m] = {name: after[name] for name in own if name in after}
        store.update({name: after[name] for name in stored if name in after})

    across = lambda block, route: lax.ppermute(block, "section", route)
    arrived, returned = [None] * micro, [None] * micro
    for m in range(micro):
        run(forward, m, first, xc=flat(content_in), xq=flat(query_in))
        arrived[m] = [across(kept[m][name], [(0, 1)]) for name in OUT]
    for m in range(micro):
        run(
            forward_backward, m, second, xc=arrived[m][0], xq=arrived[m][1], gc=flat(content_cot), gq=flat(query_cot)
        )
        returned[m] = [across(kept[m][name], [(1, 0)]) for name in GRAD]
    count = fixed["dims"][5]
    place = lax.axis_index("dp")
    own_rows = width // count
    last = micro - 1
    for m in range(last):
        run(backward, m, first, gc=returned[m][0], gq=returned[m][1])
    state = {**state, **kept[last], **store, "active": first, "gc": returned[last][0], "gq": returned[last][1]}
    state["core"] = (place & 1).reshape(1)
    state["token"] = jnp.zeros((1,), jnp.int32)

    def open_sum(name):
        sends = [state[f"s_{name}{i}"] for i in range(PIECES[name])]
        return Sum("dp", sends, state["k_" + name], step_order(name, count))

    call_down, call_up, call_attention, call_input = tails(last, fixed)
    state = call_down(state)
    down_sum = open_sum("down")
    state = call_up(state)
    up_sum = open_sum("up")
    down_sum.step(state)
    up_sum.step(state)
    state = call_attention(state)
    first_sum, second_sum = open_sum("first"), open_sum("second")
    down_sum.step(state)
    up_sum.step(state)
    first_sum.step(state)
    second_sum.step(state)
    token = state["token"].astype(F32)
    state = call_input(state)
    first_sum.step(state)
    second_sum.step(state)
    down_sum.step(state)
    up_sum.step(state)
    sums = dict(second=second_sum, down=down_sum, first=first_sum, up=up_sum)
    results = {}
    while sums:
        for name in list(sums):
            result = sums[name].step(state)
            if result is not None:
                results[name] = result
                del sums[name]
    down_grad, up_grad = results["down"], results["up"]
    kept[last] = {**kept[last], **{name: state[name] for name in SMALL + GRAD}}
    kept[last]["sm_b"] = state["sm_b"] + jnp.where(first == 1, state["sm_c"], 0.0)
    sm_a, sm_b, upb, diag = [sum(part[name] for part in kept) + token for name in SMALL]
    small = jnp.stack([sm_b[0], sm_b[1], sm_b[2], sm_a[0], sm_b[3], sm_a[1], sm_b[4], sm_a[2]])
    bucket = bucket_index(rows - jnp.arange(2 * rows))
    tables = jnp.dot(
        (bucket[None, :] == jnp.arange(BUCKETS)[:, None]).astype(F32), diag[:heads].T, precision=lax.Precision.HIGHEST
    )
    extras = jnp.concatenate(
        [
            small.reshape(8, count, own_rows).transpose(1, 0, 2).reshape(count, 8 * own_rows),
            upb[0].reshape(count, hidden // count),
            tables.reshape(count, heads * BUCKETS // count),
        ],
        axis=1,
    )
    extras = jnp.sum(jnp.where(state["token"] == 0, lax.all_to_all(extras, "dp", 0, 0, tiled=True), 0.0), axis=0)
    proj_grad = results["first"].reshape(1, 3, own_rows, width)
    out_grad = results["second"][None]
    small = extras[: 8 * own_rows].reshape(1, 8, own_rows)
    up_small = extras[8 * own_rows : 8 * own_rows + hidden // count][None]
    tab_small = extras[8 * own_rows + hidden // count :][None]
    stack = lambda name: jnp.stack([part[name] for part in kept])[None]
    return (
        *[stack(name) for name in OUT + GRAD],
        proj_grad,
        out_grad,
        up_grad[None],
        down_grad[None],
        up_small,
        small[:, 0:6],
        small[:, 6:8],
        tab_small,
    )


def solution(mesh):
    return jax.shard_map(
        body,
        mesh=mesh,
        in_specs=(
            P(None, "dp", None),
            P(None, "dp", None),
            P(None, "dp", None),
            P(None, "dp", None),
            P(None, "dp", None),
            P(None, "dp"),
            P(None, "dp"),
            P("section", None, None, None),
            P("section", None, None),
            P("section", None, None),
            P("section", None, None),
            P("section", None),
            P("section", None, None),
            P("section", None, None),
            P("section", None),
        ),
        out_specs=(
            P("section", None, "dp", None),
            P("section", None, "dp", None),
            P("section", None, "dp", None),
            P("section", None, "dp", None),
            P("section", None, "dp", None),
            P("section", "dp", None),
            P("section", "dp", None),
            P("section", "dp", None),
            P("section", "dp"),
            P("section", None, "dp"),
            P("section", None, "dp"),
            P("section", "dp"),
        ),
        check_vma=False,
    )
```
